32 devices in a mesh: tok: 4 (over y, x), col: 8 (over z, core).
Axes of the slice: x: 2, y: 2, z: 4, core: 2. Of those that a mesh axis runs over, the one named last changes fastest.
Arguments:
- tokens: bfloat16 [512, 8192], P('tok', 'col'), may hold values from -36 to 36, as said below
- norm_gain: float32 [8192], replicated, may hold values from 0.1 to 1.9
- gate_block_entries: bfloat16 [4, 1728, 128, 128], P('tok', 'col'), may hold values from -0.09375 to 0.09375
- gate_block_places: int32 [4, 1728], P('tok', 'col'), may hold values from -1 to 383, as said below
- up_block_entries: bfloat16 [4, 1728, 128, 128], P('tok', 'col'), may hold values from -0.09375 to 0.09375
- up_block_places: int32 [4, 1728], P('tok', 'col'), may hold values from -1 to 383, as said below
- down_values: bfloat16 [8, 864, 128, 128], P(None, 'col'), may hold values from -0.0546875 to 0.0546875
- down_slots: int32 [8, 864], P(None, 'col'), may hold values from -1 to 191, as said below
Outputs:
- mixed: bfloat16 [512, 8192], P('tok', 'col')
The draws below stay inside these ranges and needn't reach their ends.
Inputs may be any that keep to these rules, and one draw needn't show every extreme that they name: `tokens`: entries are bounded by construction. `gate_block_places`: A panel is one index of the first dimension and 216 consecutive entries of the second. Its entries that are not -1 are distinct block positions, -1 marks an unused entry; a panel lists at most 216 blocks, and some panel lists exactly 216 in every draw. `up_block_places`: as for gate_block_places, with its own draw. `down_slots`: A panel is one index of the first dimension and 108 consecutive entries of the second. Its entries that are not -1 are distinct block positions, -1 marks an unused entry; a panel lists at most 108 blocks, and some panel lists exactly 108 in every draw.
All inputs are finite; a program needn't handle non-finite values.
Results may differ from the reference program's by a relative error of at most 0.0065.
Values may be sent and summed in bfloat16 or wider, within the bound.
No kernel may reach another device: no remote copies, remote signals or barrier semaphores. Data moves between devices by JAX's collectives and lax.ppermute only.
A program may use at most 320 MiB of HBM per device.

```python
import math
import jax
import jax.numpy as jnp
from jax import lax

MODEL_WIDTH = 8192
HIDDEN_UNITS = 24576
MASK_BLOCK_EDGE = 128
TOKENS = 512
PANEL_ROWS = 16
PANEL_COLUMNS = 24
GATE_UP_LISTED = 216
FRB = 24
DCB = 8
CAP_DN = 108
N_TOK = 4
N_COL = 8


def panel_block_places(key, panel_total, slots_per, capacity):
    lowest = slots_per * 7 // 16
    key_count, key_perm, key_full = jax.random.split(key, 3)
    counts = jax.random.randint(key_count, (panel_total,), lowest, capacity + 1)
    chosen = jax.random.randint(key_full, (), 0, panel_total)
    counts = jnp.where(jnp.arange(panel_total) == chosen, capacity, counts)
    panel_keys = jax.random.split(key_perm, panel_total)
    orders = jax.vmap(lambda single: jax.random.permutation(single, slots_per)[:capacity])(panel_keys)
    keeping = jnp.arange(capacity)[None, :] < counts[:, None]
    return jnp.where(keeping, orders, -1).astype(jnp.int32)


def draw_tokens(key, part):
    key_base, key_rows, key_cols = jax.random.split(jax.random.fold_in(key, 7), 3)
    base = jnp.clip(jax.random.normal(key_base, (TOKENS, MODEL_WIDTH), jnp.float32), -4.0, 4.0)
    row_scale = 0.3 * jnp.exp(jax.random.uniform(key_rows, (TOKENS, 1), jnp.float32, 0.0, math.log(10.0)))
    col_scale = 0.3 * jnp.exp(jax.random.uniform(key_cols, (1, MODEL_WIDTH), jnp.float32, 0.0, math.log(10.0)))
    return (base * row_scale * col_scale).astype(jnp.bfloat16)


def draw_gate_block_places(key, part):
    block_listing = panel_block_places(jax.random.fold_in(key, 11), N_TOK * N_COL, PANEL_ROWS * PANEL_COLUMNS, GATE_UP_LISTED)
    return block_listing.reshape(N_TOK, N_COL * GATE_UP_LISTED)


def draw_up_block_places(key, part):
    block_listing = panel_block_places(jax.random.fold_in(key, 12), N_TOK * N_COL, PANEL_ROWS * PANEL_COLUMNS, GATE_UP_LISTED)
    return block_listing.reshape(N_TOK, N_COL * GATE_UP_LISTED)


def draw_down_slots(key, part):
    block_listing = panel_block_places(jax.random.fold_in(key, 13), N_COL * N_COL, FRB * DCB, CAP_DN)
    return block_listing.reshape(N_COL, N_COL * CAP_DN)


def steps_of(stream_key, dims, cuts, least, top_value):
    level = 1.0
    for dim, blocks in cuts:
        steps = jax.random.uniform(jax.random.fold_in(jax.random.fold_in(stream_key, 6), dim), (blocks,), jnp.float32, least / len(cuts), top_value / len(cuts))
        level = level * jnp.repeat(jnp.exp(steps), dims[dim] // blocks).reshape((-1,) + (1,) * (len(dims) - 1 - dim))
    return level


def centred(key, extent, width, most, pieces=(), kind=jnp.bfloat16):
    drawn = jax.random.normal(key, extent, jnp.float32) * width
    if len(pieces) > 0:
        drawn = steps_of(key, extent, pieces, -0.22, 0.18) * drawn
    return jnp.clip(drawn, min=-most, max=most).astype(kind)


def setup_inputs(seed: int = 0) -> dict:
    keys = jax.random.split(jax.random.key(seed), 9)
    tokens = draw_tokens(jax.random.fold_in(keys[8], 71), 0)
    norm_gain = jnp.clip(1.0 + 0.18 * jax.random.normal(keys[1], (MODEL_WIDTH,), jnp.float32), 0.1, 1.9)
    gate_block_entries = centred(keys[2], (N_TOK, N_COL * GATE_UP_LISTED, MASK_BLOCK_EDGE, MASK_BLOCK_EDGE), (MODEL_WIDTH // 2) ** -0.5, 0.09375, ((0, 4), (1, 8)))
    gate_block_places = draw_gate_block_places(jax.random.fold_in(keys[8], 71), 0)
    up_block_entries = centred(keys[4], (N_TOK, N_COL * GATE_UP_LISTED, MASK_BLOCK_EDGE, MASK_BLOCK_EDGE), (MODEL_WIDTH // 2) ** -0.5, 0.09375, ((0, 4), (1, 8)))
    up_block_places = draw_up_block_places(jax.random.fold_in(keys[8], 71), 0)
    down_values = centred(keys[6], (N_COL, N_COL * CAP_DN, MASK_BLOCK_EDGE, MASK_BLOCK_EDGE), (HIDDEN_UNITS // 2) ** -0.5, 0.0546875, ((1, 8),))
    down_slots = draw_down_slots(jax.random.fold_in(keys[8], 71), 0)
    return {"tokens": tokens, "norm_gain": norm_gain, "gate_block_entries": gate_block_entries, "gate_block_places": gate_block_places, "up_block_entries": up_block_entries, "up_block_places": up_block_places, "down_values": down_values, "down_slots": down_slots}


EPSILON = 1e-05

def dense_weight_matrix(values, slot_ids, capacity, rows_per, cols_per, row_blocks, col_blocks):
    panel_rows, entries = slot_ids.shape
    block_edge = values.shape[-1]
    listed = slot_ids >= 0
    clipped = jnp.where(listed, slot_ids, 0)
    panel_index = jnp.arange(panel_rows, dtype=jnp.int32)[:, None]
    column_panel = (jnp.arange(entries, dtype=jnp.int32) // capacity)[None, :]
    block_row = jnp.where(listed, panel_index * rows_per + clipped // cols_per, row_blocks)
    block_col = column_panel * cols_per + clipped % cols_per
    blocks = jnp.zeros((row_blocks, col_blocks, block_edge, block_edge), values.dtype)
    blocks = blocks.at[block_row, block_col].set(values, mode='drop')
    return blocks.transpose(0, 2, 1, 3).reshape(row_blocks * block_edge, col_blocks * block_edge)

def reference(tokens, norm_gain, gate_block_entries, gate_block_places, up_block_entries, up_block_places, down_values, down_slots):
    widened = tokens.astype(jnp.float32)
    mean_square = lax.optimization_barrier(jnp.mean(widened * widened, axis=1, keepdims=True))
    normed = (widened * lax.rsqrt(mean_square + EPSILON) * norm_gain).astype(jnp.bfloat16)
    gate_dense_matrix = dense_weight_matrix(gate_block_entries, gate_block_places, GATE_UP_LISTED, PANEL_ROWS, PANEL_COLUMNS, MODEL_WIDTH // MASK_BLOCK_EDGE, HIDDEN_UNITS // MASK_BLOCK_EDGE)
    gate_sum = jnp.dot(normed, gate_dense_matrix, preferred_element_type=jnp.float32)
    up_dense_matrix = dense_weight_matrix(up_block_entries, up_block_places, GATE_UP_LISTED, PANEL_ROWS, PANEL_COLUMNS, MODEL_WIDTH // MASK_BLOCK_EDGE, HIDDEN_UNITS // MASK_BLOCK_EDGE)
    up_sum = jnp.dot(normed, up_dense_matrix, preferred_element_type=jnp.float32)
    hidden = (jax.nn.silu(gate_sum) * up_sum).astype(jnp.bfloat16)
    down_full = dense_weight_matrix(down_values, down_slots, CAP_DN, FRB, DCB, HIDDEN_UNITS // MASK_BLOCK_EDGE, MODEL_WIDTH // MASK_BLOCK_EDGE)
    return jnp.dot(hidden, down_full, preferred_element_type=jnp.float32).astype(jnp.bfloat16)
```

```python
import functools

import jax
import jax.numpy as jnp
from jax import lax
from jax.experimental import pallas as pl
from jax.experimental.pallas import tpu as pltpu
from jax.sharding import PartitionSpec as P

MODEL_WIDTH = 8192
HIDDEN_UNITS = 24576

EPSILON = 1e-05
MIB = 1 << 20


def lookup(places, slots):
    hit = places[..., None, :] == slots[:, None]
    entry = jnp.arange(places.shape[-1], dtype=jnp.int32)
    return jnp.max(jnp.where(hit, entry, -1), axis=-1)


def put(out_ref, row, col, source_ref, entry):
    edge = source_ref.shape[-1]
    block = source_ref[0, jnp.maximum(entry, 0)]
    block = jnp.where(entry >= 0, block, jnp.zeros_like(block))
    out_ref[0, pl.ds(pl.multiple_of(row * edge, edge), edge), col * edge:(col + 1) * edge] = block


def spread_gate_up_kernel(gate_at, up_at, gate_ref, up_ref, out_ref, *, rows, cols):
    chunk = pl.program_id(0)

    @pl.loop(0, rows)
    def _(row):
        for col in range(cols):
            at = (chunk * rows + row) * cols + col
            put(out_ref, row, col, gate_ref, gate_at[at])
            put(out_ref, row, cols + col, up_ref, up_at[at])


def spread_gate_up(gate_at, up_at, gate, up, chunks, rows, cols):
    edge = gate.shape[-1]
    whole = pl.BlockSpec(gate.shape, lambda k, *_: (0, 0, 0, 0), pipeline_mode=pl.Buffered(1))
    out = jax.ShapeDtypeStruct((chunks, rows * edge, 2 * cols * edge), gate.dtype)
    return pl.pallas_call(
        functools.partial(spread_gate_up_kernel, rows=rows, cols=cols),
        out_shape=out,
        grid_spec=pltpu.PrefetchScalarGridSpec(
            num_scalar_prefetch=2,
            grid=(chunks,),
            in_specs=[whole, whole],
            out_specs=pl.BlockSpec((1,) + out.shape[1:], lambda k, *_: (k, 0, 0)),
        ),
        compiler_params=pltpu.CompilerParams(vmem_limit_bytes=48 * MIB),
        cost_estimate=pl.CostEstimate(
            flops=0, bytes_accessed=2 * (2 * gate.size + out.size), transcendentals=0
        ),
        name="spread_gate_up",
    )(gate_at, up_at, gate, up)


def spread_down_kernel(at_ref, values_ref, out_ref, *, rows, cols):
    panel, chunk = pl.program_id(0), pl.program_id(1)
    base = (panel * pl.num_programs(1) + chunk) * rows * cols

    @pl.loop(0, rows)
    def _(row):
        for col in range(cols):
            put(out_ref.at[0], row, col, values_ref, at_ref[base + row * cols + col])


def spread_down(at, values, chunks, rows, cols):
    panels, _, edge, _ = values.shape
    out = jax.ShapeDtypeStruct((chunks, panels, rows * edge, cols * edge), values.dtype)
    return pl.pallas_call(
        functools.partial(spread_down_kernel, rows=rows, cols=cols),
        out_shape=out,
        grid_spec=pltpu.PrefetchScalarGridSpec(
            num_scalar_prefetch=1,
            grid=(panels, chunks),
            in_specs=[pl.BlockSpec((1,) + values.shape[1:], lambda g, k, *_: (g, 0, 0, 0))],
            out_specs=pl.BlockSpec((1, 1) + out.shape[2:], lambda g, k, *_: (k, g, 0, 0)),
        ),
        compiler_params=pltpu.CompilerParams(vmem_limit_bytes=48 * MIB),
        cost_estimate=pl.CostEstimate(
            flops=0, bytes_accessed=2 * (values.size + out.size), transcendentals=0
        ),
        name="spread_down",
    )(at, values)


def gate_up_kernel(*refs, parts):
    own, other = refs[:parts], refs[parts:2 * parts]
    weight = refs[2 * parts]
    outs, held = refs[2 * parts + 1:3 * parts + 1], refs[-1]
    count, half = own[0].shape

    @pl.when(pl.program_id(0) == 0)
    def _():
        for part in range(parts):
            rows = slice(part * count, (part + 1) * count)
            held[rows, :half] = own[part][...]
            held[rows, half:] = other[part][...]

    product = jnp.dot(held[...], weight[0], preferred_element_type=jnp.float32)
    for part in range(parts):
        outs[part][...] = product[part * count:(part + 1) * count].astype(outs[part].dtype)


def gate_up(own, other, dense, chunk):
    parts = len(own)
    count, half = own[0].shape
    _, depth, width = dense.shape
    tile = 256
    out = jax.ShapeDtypeStruct((count, width), own[0].dtype)
    return pl.pallas_call(
        functools.partial(gate_up_kernel, parts=parts),
        out_shape=[out] * parts,
        grid=(width // tile,),
        in_specs=[pl.BlockSpec((count, half), lambda n: (0, 0))] * (2 * parts)
        + [pl.BlockSpec((1, depth, tile), lambda n: (chunk, 0, n))],
        out_specs=[pl.BlockSpec((count, tile), lambda n: (0, n))] * parts,
        scratch_shapes=[pltpu.VMEM((parts * count, 2 * half), own[0].dtype)],
        compiler_params=pltpu.CompilerParams(vmem_limit_bytes=32 * MIB),
        cost_estimate=pl.CostEstimate(
            flops=2 * parts * count * depth * width,
            bytes_accessed=2 * (depth * width + parts * count * (depth + width)),
            transcendentals=0,
        ),
        name=f"gate_up_{chunk}",
    )(*own, *other, dense)


def down_kernel(hidden_ref, weight_ref, before_ref, out_ref, total):
    panel = pl.program_id(0)

    @pl.when(panel == 0)
    def _():
        total[...] = before_ref[...]

    total[...] += jnp.dot(hidden_ref[0], weight_ref[0, 0], preferred_element_type=jnp.float32)

    @pl.when(panel == pl.num_programs(0) - 1)
    def _():
        out_ref[...] = total[...].astype(out_ref.dtype)


def down(hidden, dense, before, chunk, dtype):
    panels, count, depth = hidden.shape
    width = dense.shape[-1]
    return pl.pallas_call(
        down_kernel,
        out_shape=jax.ShapeDtypeStruct((count, width), dtype),
        grid=(panels,),
        in_specs=[
            pl.BlockSpec((1, count, depth), lambda g: (g, 0, 0)),
            pl.BlockSpec((1, 1, depth, width), lambda g: (chunk, g, 0, 0)),
            pl.BlockSpec((count, width), lambda g: (0, 0)),
        ],
        out_specs=pl.BlockSpec((count, width), lambda g: (0, 0)),
        scratch_shapes=[pltpu.VMEM((count, width), jnp.float32)],
        compiler_params=pltpu.CompilerParams(vmem_limit_bytes=32 * MIB),
        cost_estimate=pl.CostEstimate(
            flops=2 * panels * count * depth * width,
            bytes_accessed=2 * panels * depth * (width + count) + 6 * count * width,
            transcendentals=0,
        ),
        name=f"down_{chunk}",
    )(hidden, dense, before)


def shards(
    tokens,
    norm_gain,
    gate_block_entries,
    gate_block_places,
    up_block_entries,
    up_block_places,
    down_values,
    down_slots,
):
    edge = gate_block_entries.shape[-1]
    tok_size = lax.axis_size("tok")
    col_size = lax.axis_size("col")
    rows_per = MODEL_WIDTH // edge // tok_size
    cols_per = HIDDEN_UNITS // edge // col_size
    width_blocks = MODEL_WIDTH // edge // col_size
    chunks = 4 if cols_per % 4 == 0 else 1
    chunk_cols = cols_per // chunks
    count, features = tokens.shape
    half = MODEL_WIDTH // tok_size // 2
    tok, col = lax.axis_index("tok"), lax.axis_index("col")
    side = col % 2

    def swap_tok(array, step):
        return lax.ppermute(array, "tok", [(i, i ^ step) for i in range(tok_size)])

    def swap_core(array):
        return lax.ppermute(array, "col", [(i, i ^ 1) for i in range(col_size)])

    k, r, q = jnp.meshgrid(
        jnp.arange(chunks), jnp.arange(rows_per), jnp.arange(chunk_cols), indexing="ij"
    )
    row = (r + side * (rows_per // 2)) % rows_per
    slots = (row * cols_per + k * chunk_cols + q).reshape(-1).astype(jnp.int32)
    gate_at = lookup(gate_block_places[0], slots)
    up_at = lookup(up_block_places[0], slots)
    down_at = lookup(down_slots, jnp.arange(cols_per * width_blocks, dtype=jnp.int32)).reshape(-1)

    gathered = lax.all_gather(tokens, "col")
    dense = spread_gate_up(
        gate_at, up_at, gate_block_entries, up_block_entries, chunks, rows_per, chunk_cols
    )
    down_dense = spread_down(down_at, down_values, chunks, chunk_cols, width_blocks)

    widened = gathered.astype(jnp.float32)
    mean_square = jnp.mean(widened * widened, axis=(0, 2))[:, None]
    scale = lax.rsqrt(mean_square + EPSILON)
    subs = half // features

    def normed(panel):
        at = panel * 2 + side
        piece = lax.dynamic_slice_in_dim(gathered, at * subs, subs, 0)
        piece = piece.transpose(1, 0, 2).reshape(count, half).astype(jnp.float32)
        gain = lax.dynamic_slice_in_dim(norm_gain, at * half, half, 0)
        return (piece * scale * gain).astype(jnp.bfloat16)

    own = [normed(tok ^ part) for part in range(tok_size)]
    own = [own[0]] + [swap_tok(own[part], part) for part in range(1, tok_size)]
    other = [swap_core(part) for part in own]

    hiddens = []
    for chunk in range(chunks):
        sums = gate_up(own, other, dense, chunk)
        terms = [sums[0]] + [swap_tok(sums[part], part) for part in range(1, tok_size)]
        total = functools.reduce(jnp.add, [term.astype(jnp.float32) for term in terms])
        gate_sum, up_sum = jnp.split(total, 2, axis=1)
        hiddens.append((jax.nn.silu(gate_sum) * up_sum).astype(jnp.bfloat16))

    mixed = jnp.zeros((count, width_blocks * edge), jnp.float32)
    for chunk in range(chunks):
        hidden = lax.all_gather(hiddens[chunk], "col")
        last = chunk == chunks - 1
        mixed = down(hidden, down_dense, mixed, chunk, jnp.bfloat16 if last else jnp.float32)
    return mixed


def solution(mesh):
    return jax.shard_map(
        shards,
        mesh=mesh,
        in_specs=(
            P("tok", "col"),
            P(),
            P("tok", "col", None, None),
            P("tok", "col"),
            P("tok", "col", None, None),
            P("tok", "col"),
            P(None, "col", None, None),
            P(None, "col"),
        ),
        out_specs=P("tok", "col"),
        check_vma=False,
    )
```

```python
import functools

import jax
import jax.numpy as jnp
from jax import lax
from jax.experimental import pallas as pl
from jax.experimental.pallas import tpu as pltpu
from jax.sharding import PartitionSpec as P

MODEL_WIDTH = 8192
HIDDEN_UNITS = 24576

EPSILON = 1e-05
MIB = 1 << 20


def lookup(places, slots):
    hit = places[..., None, :] == slots[:, None]
    entry = jnp.arange(places.shape[-1], dtype=jnp.int32)
    return jnp.max(jnp.where(hit, entry, -1), axis=-1)


def put(out_ref, row, col, source_ref, entry):
    edge = source_ref.shape[-1]
    block = source_ref[0, jnp.maximum(entry, 0)]
    block = jnp.where(entry >= 0, block, jnp.zeros_like(block))
    out_ref[0, pl.ds(pl.multiple_of(row * edge, edge), edge), col * edge:(col + 1) * edge] = block


def spread_gate_up_kernel(gate_at, up_at, gate_ref, up_ref, out_ref, *, rows, cols):
    chunk = pl.program_id(0)

    @pl.loop(0, rows)
    def _(row):
        for col in range(cols):
            at = (chunk * rows + row) * cols + col
            put(out_ref, row, col, gate_ref, gate_at[at])
            put(out_ref, row, cols + col, up_ref, up_at[at])


def spread_gate_up(gate_at, up_at, gate, up, chunks, rows, cols):
    edge = gate.shape[-1]
    whole = pl.BlockSpec(gate.shape, lambda k, *_: (0, 0, 0, 0), pipeline_mode=pl.Buffered(1))
    out = jax.ShapeDtypeStruct((chunks, rows * edge, 2 * cols * edge), gate.dtype)
    return pl.pallas_call(
        functools.partial(spread_gate_up_kernel, rows=rows, cols=cols),
        out_shape=out,
        grid_spec=pltpu.PrefetchScalarGridSpec(
            num_scalar_prefetch=2,
            grid=(chunks,),
            in_specs=[whole, whole],
            out_specs=pl.BlockSpec((1,) + out.shape[1:], lambda k, *_: (k, 0, 0)),
        ),
        compiler_params=pltpu.CompilerParams(vmem_limit_bytes=48 * MIB),
        cost_estimate=pl.CostEstimate(
            flops=0, bytes_accessed=2 * (2 * gate.size + out.size), transcendentals=0
        ),
        name="spread_gate_up",
    )(gate_at, up_at, gate, up)


def spread_down_kernel(at_ref, values_ref, out_ref, *, rows, cols):
    panel, chunk = pl.program_id(0), pl.program_id(1)
    base = (panel * pl.num_programs(1) + chunk) * rows * cols

    @pl.loop(0, rows)
    def _(row):
        for col in range(cols):
            put(out_ref.at[0], row, col, values_ref, at_ref[base + row * cols + col])


def spread_down(at, values, chunks, rows, cols):
    panels, _, edge, _ = values.shape
    out = jax.ShapeDtypeStruct((chunks, panels, rows * edge, cols * edge), values.dtype)
    return pl.pallas_call(
        functools.partial(spread_down_kernel, rows=rows, cols=cols),
        out_shape=out,
        grid_spec=pltpu.PrefetchScalarGridSpec(
            num_scalar_prefetch=1,
            grid=(panels, chunks),
            in_specs=[pl.BlockSpec((1,) + values.shape[1:], lambda g, k, *_: (g, 0, 0, 0))],
            out_specs=pl.BlockSpec((1, 1) + out.shape[2:], lambda g, k, *_: (k, g, 0, 0)),
        ),
        compiler_params=pltpu.CompilerParams(vmem_limit_bytes=48 * MIB),
        cost_estimate=pl.CostEstimate(
            flops=0, bytes_accessed=2 * (values.size + out.size), transcendentals=0
        ),
        name="spread_down",
    )(at, values)


def gate_up_kernel(*refs, parts):
    own, other = refs[:parts], refs[parts:2 * parts]
    weight = refs[2 * parts]
    outs, held = refs[2 * parts + 1:3 * parts + 1], refs[-1]
    count, half = own[0].shape

    @pl.when(pl.program_id(0) == 0)
    def _():
        for part in range(parts):
            rows = slice(part * count, (part + 1) * count)
            held[rows, :half] = own[part][...]
            held[rows, half:] = other[part][...]

    product = jnp.dot(held[...], weight[0], preferred_element_type=jnp.float32)
    for part in range(parts):
        outs[part][...] = product[part * count:(part + 1) * count].astype(outs[part].dtype)


def gate_up(own, other, dense, chunk):
    parts = len(own)
    count, half = own[0].shape
    _, depth, width = dense.shape
    tile = 256
    out = jax.ShapeDtypeStruct((count, width), own[0].dtype)
    return pl.pallas_call(
        functools.partial(gate_up_kernel, parts=parts),
        out_shape=[out] * parts,
        grid=(width // tile,),
        in_specs=[pl.BlockSpec((count, half), lambda n: (0, 0))] * (2 * parts)
        + [pl.BlockSpec((1, depth, tile), lambda n: (chunk, 0, n))],
        out_specs=[pl.BlockSpec((count, tile), lambda n: (0, n))] * parts,
        scratch_shapes=[pltpu.VMEM((parts * count, 2 * half), own[0].dtype)],
        compiler_params=pltpu.CompilerParams(vmem_limit_bytes=32 * MIB),
        cost_estimate=pl.CostEstimate(
            flops=2 * parts * count * depth * width,
            bytes_accessed=2 * (depth * width + parts * count * (depth + width)),
            transcendentals=0,
        ),
        name=f"gate_up_{chunk}",
    )(*own, *other, dense)


def down_kernel(hidden_ref, weight_ref, before_ref, out_ref, total):
    panel = pl.program_id(0)

    @pl.when(panel == 0)
    def _():
        total[...] = before_ref[...]

    total[...] += jnp.dot(hidden_ref[0], weight_ref[0, 0], preferred_element_type=jnp.float32)

    @pl.when(panel == pl.num_programs(0) - 1)
    def _():
        out_ref[...] = total[...].astype(out_ref.dtype)


def down(hidden, dense, before, chunk, dtype):
    panels, count, depth = hidden.shape
    width = dense.shape[-1]
    return pl.pallas_call(
        down_kernel,
        out_shape=jax.ShapeDtypeStruct((count, width), dtype),
        grid=(panels,),
        in_specs=[
            pl.BlockSpec((1, count, depth), lambda g: (g, 0, 0)),
            pl.BlockSpec((1, 1, depth, width), lambda g: (chunk, g, 0, 0)),
            pl.BlockSpec((count, width), lambda g: (0, 0)),
        ],
        out_specs=pl.BlockSpec((count, width), lambda g: (0, 0)),
        scratch_shapes=[pltpu.VMEM((count, width), jnp.float32)],
        compiler_params=pltpu.CompilerParams(vmem_limit_bytes=32 * MIB),
        cost_estimate=pl.CostEstimate(
            flops=2 * panels * count * depth * width,
            bytes_accessed=2 * panels * depth * (width + count) + 6 * count * width,
            transcendentals=0,
        ),
        name=f"down_{chunk}",
    )(hidden, dense, before)


def by_tokens(
    tokens,
    norm_gain,
    gate_block_entries,
    gate_block_places,
    up_block_entries,
    up_block_places,
    down_values,
    down_slots,
):
    edge = gate_block_entries.shape[-1]
    tok_size = lax.axis_size("tok")
    col_size = lax.axis_size("col")
    rows_per = MODEL_WIDTH // edge // tok_size
    cols_per = HIDDEN_UNITS // edge // col_size
    width_blocks = MODEL_WIDTH // edge // col_size
    chunks = 4 if cols_per % 4 == 0 else 1
    chunk_cols = cols_per // chunks
    count, features = tokens.shape
    half = MODEL_WIDTH // tok_size // 2
    tok, col = lax.axis_index("tok"), lax.axis_index("col")
    side = col % 2

    def swap_tok(array, step):
        return lax.ppermute(array, "tok", [(i, i ^ step) for i in range(tok_size)])

    def swap_core(array):
        return lax.ppermute(array, "col", [(i, i ^ 1) for i in range(col_size)])

    k, r, q = jnp.meshgrid(
        jnp.arange(chunks), jnp.arange(rows_per), jnp.arange(chunk_cols), indexing="ij"
    )
    row = (r + side * (rows_per // 2)) % rows_per
    slots = (row * cols_per + k * chunk_cols + q).reshape(-1).astype(jnp.int32)
    gate_at = lookup(gate_block_places[0], slots)
    up_at = lookup(up_block_places[0], slots)
    down_at = lookup(down_slots, jnp.arange(cols_per * width_blocks, dtype=jnp.int32)).reshape(-1)

    gathered = lax.all_gather(tokens, "col")
    dense = spread_gate_up(
        gate_at, up_at, gate_block_entries, up_block_entries, chunks, rows_per, chunk_cols
    )
    down_dense = spread_down(down_at, down_values, chunks, chunk_cols, width_blocks)

    widened = gathered.astype(jnp.float32)
    mean_square = jnp.mean(widened * widened, axis=(0, 2))[:, None]
    scale = lax.rsqrt(mean_square + EPSILON)
    subs = half // features

    def normed(panel):
        at = panel * 2 + side
        piece = lax.dynamic_slice_in_dim(gathered, at * subs, subs, 0)
        piece = piece.transpose(1, 0, 2).reshape(count, half).astype(jnp.float32)
        gain = lax.dynamic_slice_in_dim(norm_gain, at * half, half, 0)
        return (piece * scale * gain).astype(jnp.bfloat16)

    own = [normed(tok ^ part) for part in range(tok_size)]
    own = [own[0]] + [swap_tok(own[part], part) for part in range(1, tok_size)]
    other = [swap_core(part) for part in own]

    hiddens = []
    for chunk in range(chunks):
        sums = gate_up(own, other, dense, chunk)
        terms = [sums[0]] + [swap_tok(sums[part], part) for part in range(1, tok_size)]
        total = functools.reduce(jnp.add, [term.astype(jnp.float32) for term in terms])
        gate_sum, up_sum = jnp.split(total, 2, axis=1)
        hiddens.append((jax.nn.silu(gate_sum) * up_sum).astype(jnp.bfloat16))

    mixed = jnp.zeros((count, width_blocks * edge), jnp.float32)
    for chunk in range(chunks):
        hidden = lax.all_gather(hiddens[chunk], "col")
        last = chunk == chunks - 1
        mixed = down(hidden, down_dense, mixed, chunk, jnp.bfloat16 if last else jnp.float32)
    return mixed

def spread_shares_kernel(gate_at, up_at, gate_ref, up_ref, out_ref, *, rows, shares, cols):
    chunk = pl.program_id(0)

    @pl.loop(0, rows)
    def _(row):
        for share in range(shares):
            for col in range(cols):
                at = ((chunk * rows + row) * shares + share) * cols + col
                put(out_ref, row, 2 * share * cols + col, gate_ref, gate_at[at])
                put(out_ref, row, (2 * share + 1) * cols + col, up_ref, up_at[at])


def spread_shares(gate_at, up_at, gate, up, chunks, rows, shares, cols):
    edge = gate.shape[-1]
    whole = pl.BlockSpec(gate.shape, lambda k, *_: (0, 0, 0, 0), pipeline_mode=pl.Buffered(1))
    out = jax.ShapeDtypeStruct((chunks, rows * edge, 2 * shares * cols * edge), gate.dtype)
    return pl.pallas_call(
        functools.partial(spread_shares_kernel, rows=rows, shares=shares, cols=cols),
        out_shape=out,
        grid_spec=pltpu.PrefetchScalarGridSpec(
            num_scalar_prefetch=2,
            grid=(chunks,),
            in_specs=[whole, whole],
            out_specs=pl.BlockSpec((1,) + out.shape[1:], lambda k, *_: (k, 0, 0)),
        ),
        compiler_params=pltpu.CompilerParams(vmem_limit_bytes=48 * MIB),
        cost_estimate=pl.CostEstimate(
            flops=0, bytes_accessed=2 * (2 * gate.size + out.size), transcendentals=0
        ),
        name="spread_gate_up",
    )(gate_at, up_at, gate, up)


def spread_panels_kernel(at_ref, panels_ref, values_ref, out_ref, *, chunks, rows, cols):
    panel = pl.program_id(0)
    for chunk in range(chunks):
        for row in range(rows):
            for col in range(cols):
                at = ((panel * chunks + chunk) * rows + row) * cols + col
                put(out_ref.at[pl.ds(chunk, 1)], row, col, values_ref, at_ref[at])


def spread_panels(at, panels, values, chunks, rows, cols):
    count, _, edge, _ = values.shape
    out = jax.ShapeDtypeStruct((chunks, count * rows * edge, cols * edge), values.dtype)
    return pl.pallas_call(
        functools.partial(spread_panels_kernel, chunks=chunks, rows=rows, cols=cols),
        out_shape=out,
        grid_spec=pltpu.PrefetchScalarGridSpec(
            num_scalar_prefetch=2,
            grid=(count,),
            in_specs=[
                pl.BlockSpec((1,) + values.shape[1:], lambda m, _, panels: (panels[m], 0, 0, 0))
            ],
            out_specs=pl.BlockSpec((chunks, rows * edge, cols * edge), lambda m, *_: (0, m, 0)),
        ),
        compiler_params=pltpu.CompilerParams(vmem_limit_bytes=48 * MIB),
        cost_estimate=pl.CostEstimate(
            flops=0, bytes_accessed=2 * (values.size + out.size), transcendentals=0
        ),
        name="spread_down",
    )(at, panels, values)

def pack_kernel(*refs, parts):
    count = refs[0].shape[0]
    for part in range(parts):
        refs[-1][part * count:(part + 1) * count] = refs[part][...]


def pack(pieces, after):
    parts = len(pieces)
    count, width = pieces[0].shape
    return pl.pallas_call(
        functools.partial(pack_kernel, parts=parts),
        out_shape=jax.ShapeDtypeStruct((parts * count, width), pieces[0].dtype),
        in_specs=[pl.BlockSpec(memory_space=pltpu.VMEM)] * parts
        + [pl.BlockSpec(memory_space=pl.ANY)] * len(after),
        out_specs=pl.BlockSpec(memory_space=pltpu.VMEM),
        cost_estimate=pl.CostEstimate(
            flops=0, bytes_accessed=4 * parts * count * width, transcendentals=0
        ),
        name="pack",
    )(*pieces, *after)


def pack_hidden_kernel(*refs, parts):
    out = refs[-1]
    count = out.shape[1] // parts
    for step in range(parts):
        for part in range(parts):
            there = part ^ step
            out[step, part * count:(part + 1) * count] = refs[step][there * count:(there + 1) * count]


def pack_hidden(pieces):
    parts = len(pieces)
    return pl.pallas_call(
        functools.partial(pack_hidden_kernel, parts=parts),
        out_shape=jax.ShapeDtypeStruct((parts,) + pieces[0].shape, pieces[0].dtype),
        in_specs=[pl.BlockSpec(memory_space=pltpu.VMEM)] * parts,
        out_specs=pl.BlockSpec(memory_space=pltpu.VMEM),
        cost_estimate=pl.CostEstimate(
            flops=0, bytes_accessed=4 * parts * pieces[0].size, transcendentals=0
        ),
        name="pack_hidden",
    )(*pieces)


def combine_kernel(*refs, parts):
    terms, scale, out = refs[:parts], refs[parts], refs[-1]
    total = functools.reduce(jnp.add, [term[...].astype(jnp.float32) for term in terms])
    total *= scale[...]
    width = out.shape[-1]
    gate_sum, up_sum = total[:, :width], total[:, width:]
    out[...] = (gate_sum / (1.0 + jnp.exp(-gate_sum)) * up_sum).astype(out.dtype)


def combine(terms, scale, after, chunk):
    parts = len(terms)
    count, width = terms[0].shape
    rows = count // 4
    return pl.pallas_call(
        functools.partial(combine_kernel, parts=parts),
        out_shape=jax.ShapeDtypeStruct((count, width // 2), terms[0].dtype),
        grid=(count // rows,),
        in_specs=[pl.BlockSpec((rows, width), lambda i: (i, 0))] * parts
        + [pl.BlockSpec((rows, 1), lambda i: (i, 0)), pl.BlockSpec(memory_space=pl.ANY)],
        out_specs=pl.BlockSpec((rows, width // 2), lambda i: (i, 0)),
        compiler_params=pltpu.CompilerParams(vmem_limit_bytes=32 * MIB),
        cost_estimate=pl.CostEstimate(
            flops=8 * count * width,
            bytes_accessed=2 * count * width * (parts + 1),
            transcendentals=count * width // 2,
        ),
        name=f"combine_{chunk}",
    )(*terms, scale, after)


def panel_product_kernel(own, other, weight, *outs):
    half = own.shape[1]
    product = jnp.dot(own[...], weight[0, :half], preferred_element_type=jnp.float32)
    product += jnp.dot(other[...], weight[0, half:], preferred_element_type=jnp.float32)
    for part, out in enumerate(outs):

        @pl.when(pl.program_id(0) == part)
        def _():
            out[...] = product.astype(out.dtype)


def panel_product(own, other, dense, parts, chunk):
    count, half = own.shape
    _, depth, width = dense.shape
    tile = width // parts
    out = jax.ShapeDtypeStruct((count, tile), own.dtype)
    return pl.pallas_call(
        panel_product_kernel,
        out_shape=[out] * parts,
        grid=(parts,),
        in_specs=[pl.BlockSpec((count, half), lambda n: (0, 0))] * 2
        + [pl.BlockSpec((1, depth, tile), lambda n: (chunk, 0, n))],
        out_specs=[pl.BlockSpec((count, tile), lambda n: (0, 0))] * parts,
        compiler_params=pltpu.CompilerParams(vmem_limit_bytes=40 * MIB),
        cost_estimate=pl.CostEstimate(
            flops=2 * count * depth * width,
            bytes_accessed=2 * (depth * width + count * (depth + width)),
            transcendentals=0,
        ),
        name=f"gate_up_{chunk}",
    )(own, other, dense)


def down_product_kernel(own, other, weight, *refs):
    before, out, held = refs[0] if len(refs) == 3 else None, refs[-2], refs[-1]
    panels, _, depth = own.shape

    @pl.when(pl.program_id(0) == 0)
    def _():
        for i in range(panels):
            held[:, i * depth:(i + 1) * depth] = own[i]
            held[:, (panels + i) * depth:(panels + i + 1) * depth] = other[i]

    product = jnp.dot(held[...], weight[0], preferred_element_type=jnp.float32)
    if before is not None:
        product += before[...]
    out[...] = product.astype(out.dtype)


def down_product(own, other, dense, before, chunk, dtype):
    panels, count, depth = own.shape
    _, total, width = dense.shape
    tile = width // 2
    tiles = pl.BlockSpec((count, tile), lambda n: (0, n))
    whole = pl.BlockSpec((panels, count, depth), lambda n: (0, 0, 0))
    added = [] if before is None else [before]
    return pl.pallas_call(
        down_product_kernel,
        out_shape=jax.ShapeDtypeStruct((count, width), dtype),
        grid=(width // tile,),
        in_specs=[whole, whole, pl.BlockSpec((1, total, tile), lambda n: (chunk, 0, n))]
        + [tiles] * len(added),
        out_specs=tiles,
        scratch_shapes=[pltpu.VMEM((count, total), own.dtype)],
        compiler_params=pltpu.CompilerParams(vmem_limit_bytes=40 * MIB),
        cost_estimate=pl.CostEstimate(
            flops=2 * count * total * width,
            bytes_accessed=2 * total * (width + count) + 8 * count * width,
            transcendentals=0,
        ),
        name=f"down_{chunk}",
    )(own, other, dense, *added)


def by_columns(
    tokens,
    norm_gain,
    gate_block_entries,
    gate_block_places,
    up_block_entries,
    up_block_places,
    down_values,
    down_slots,
):
    edge = gate_block_entries.shape[-1]
    tok_size = lax.axis_size("tok")
    col_size = lax.axis_size("col")
    rows_per = MODEL_WIDTH // edge // tok_size
    cols_per = HIDDEN_UNITS // edge // col_size
    width_blocks = MODEL_WIDTH // edge // col_size
    share = cols_per // tok_size
    chunks = 3 if share % 3 == 0 else 1
    cols = share // chunks
    count, half = tokens.shape
    tok, col = lax.axis_index("tok"), lax.axis_index("col")
    chip, side = col // 2, col % 2
    parts = range(tok_size)

    def swap_tok(array, step):
        return lax.ppermute(array, "tok", [(i, i ^ step) for i in parts])

    def swap_chip(array, step):
        return lax.ppermute(array, "col", [(i, i ^ (2 * step)) for i in range(col_size)])

    def swap_core(array):
        return lax.ppermute(array, "col", [(i, i ^ 1) for i in range(col_size)])

    def to_users(array, part):
        pairs = []
        for i in parts:
            for j in range(col_size):
                user = (j // 2) * col_size + 2 * (i ^ part) + j % 2
                pairs.append((i * col_size + j, user))
        return lax.ppermute(array, ("tok", "col"), pairs)

    widened = tokens.astype(jnp.float32)
    gain = lax.dynamic_slice_in_dim(norm_gain, col * half, half, 0)
    gained = (widened * gain).astype(jnp.bfloat16)
    pieces = [to_users(gained, part) for part in parts]
    squares = jnp.sum(widened * widened, axis=1)
    squares = jnp.where(jnp.arange(tok_size)[:, None] == tok, squares[None], 0.0)
    squares = lax.psum(squares, ("tok", "col"))

    k, r, p, q = jnp.meshgrid(
        jnp.arange(chunks), jnp.arange(rows_per), jnp.arange(tok_size), jnp.arange(cols),
        indexing="ij",
    )
    row = (r + side * (rows_per // 2)) % rows_per
    slots = (row * cols_per + (p ^ tok) * share + k * cols + q).reshape(-1).astype(jnp.int32)
    gate_at = lookup(gate_block_places[0], slots)
    up_at = lookup(up_block_places[0], slots)
    m = jnp.arange(col_size, dtype=jnp.int32)
    panels = 2 * ((m % tok_size) ^ chip) + (side ^ (m // tok_size))
    slots = tok * share * width_blocks + jnp.arange(share * width_blocks, dtype=jnp.int32)
    down_at = jnp.take(lookup(down_slots, slots), panels, axis=0).reshape(-1)

    dense = spread_shares(
        gate_at, up_at, gate_block_entries, up_block_entries, chunks, rows_per, tok_size, cols
    )
    down_dense = spread_panels(down_at, panels, down_values, chunks, cols, width_blocks)

    own = pack(pieces, [dense, down_dense])
    other = swap_core(own)

    sums = [panel_product(own, other, dense, tok_size, chunk) for chunk in range(chunks)]
    scale = lax.rsqrt(squares / MODEL_WIDTH + EPSILON)
    scale = jnp.take(scale, jnp.arange(tok_size) ^ chip, axis=0).reshape(-1, 1)
    mixed = None
    for chunk in range(chunks):
        terms = [sums[chunk][0]] + [swap_tok(sums[chunk][p], p) for p in parts[1:]]
        hidden = combine(terms, scale, sums[-1][0], chunk)
        held = pack_hidden([hidden] + [swap_chip(hidden, step) for step in parts[1:]])
        last = chunk == chunks - 1
        mixed = down_product(
            held, swap_core(held), down_dense, mixed, chunk, jnp.bfloat16 if last else jnp.float32
        )

    mixed = mixed.reshape(tok_size, count, -1)
    total = 0.0
    for step in parts:
        part = lax.dynamic_index_in_dim(mixed, chip ^ tok ^ step, 0, keepdims=False)
        total += (swap_tok(part, step) if step else part).astype(jnp.float32)
    return total.astype(jnp.bfloat16)


def shards(*arrays):
    tok_size = lax.axis_size("tok")
    col_size = lax.axis_size("col")
    blocks = HIDDEN_UNITS // arrays[2].shape[-1]
    even = blocks % (col_size * tok_size) == 0 and col_size == 2 * tok_size == 8
    return (by_columns if even else by_tokens)(*arrays)


def solution(mesh):
    return jax.shard_map(
        shards,
        mesh=mesh,
        in_specs=(
            P("tok", "col"),
            P(),
            P("tok", "col", None, None),
            P("tok", "col"),
            P("tok", "col", None, None),
            P("tok", "col"),
            P(None, "col", None, None),
            P(None, "col"),
        ),
        out_specs=P("tok", "col"),
        check_vma=False,
    )
```

```python
import functools

import jax
import jax.numpy as jnp
from jax import lax
from jax.experimental import pallas as pl
from jax.experimental.pallas import tpu as pltpu
from jax.sharding import PartitionSpec as P

MODEL_WIDTH = 8192
HIDDEN_UNITS = 24576

EPSILON = 1e-05
MIB = 1 << 20


def lookup(places, slots):
    hit = places[..., None, :] == slots[:, None]
    entry = jnp.arange(places.shape[-1], dtype=jnp.int32)
    return jnp.max(jnp.where(hit, entry, -1), axis=-1)


def put(out_ref, row, col, source_ref, entry):
    edge = source_ref.shape[-1]
    block = source_ref[0, jnp.maximum(entry, 0)]
    block = jnp.where(entry >= 0, block, jnp.zeros_like(block))
    out_ref[0, pl.ds(pl.multiple_of(row * edge, edge), edge), col * edge:(col + 1) * edge] = block


def spread_gate_up_kernel(gate_at, up_at, gate_ref, up_ref, out_ref, *, rows, cols):
    chunk = pl.program_id(0)

    @pl.loop(0, rows)
    def _(row):
        for col in range(cols):
            at = (chunk * rows + row) * cols + col
            put(out_ref, row, col, gate_ref, gate_at[at])
            put(out_ref, row, cols + col, up_ref, up_at[at])


def spread_gate_up(gate_at, up_at, gate, up, chunks, rows, cols):
    edge = gate.shape[-1]
    whole = pl.BlockSpec(gate.shape, lambda k, *_: (0, 0, 0, 0), pipeline_mode=pl.Buffered(1))
    out = jax.ShapeDtypeStruct((chunks, rows * edge, 2 * cols * edge), gate.dtype)
    return pl.pallas_call(
        functools.partial(spread_gate_up_kernel, rows=rows, cols=cols),
        out_shape=out,
        grid_spec=pltpu.PrefetchScalarGridSpec(
            num_scalar_prefetch=2,
            grid=(chunks,),
            in_specs=[whole, whole],
            out_specs=pl.BlockSpec((1,) + out.shape[1:], lambda k, *_: (k, 0, 0)),
        ),
        compiler_params=pltpu.CompilerParams(vmem_limit_bytes=48 * MIB),
        cost_estimate=pl.CostEstimate(
            flops=0, bytes_accessed=2 * (2 * gate.size + out.size), transcendentals=0
        ),
        name="spread_gate_up",
    )(gate_at, up_at, gate, up)


def spread_down_kernel(at_ref, values_ref, out_ref, *, rows, cols):
    panel, chunk = pl.program_id(0), pl.program_id(1)
    base = (panel * pl.num_programs(1) + chunk) * rows * cols

    @pl.loop(0, rows)
    def _(row):
        for col in range(cols):
            put(out_ref.at[0], row, col, values_ref, at_ref[base + row * cols + col])


def spread_down(at, values, chunks, rows, cols):
    panels, _, edge, _ = values.shape
    out = jax.ShapeDtypeStruct((chunks, panels, rows * edge, cols * edge), values.dtype)
    return pl.pallas_call(
        functools.partial(spread_down_kernel, rows=rows, cols=cols),
        out_shape=out,
        grid_spec=pltpu.PrefetchScalarGridSpec(
            num_scalar_prefetch=1,
            grid=(panels, chunks),
            in_specs=[pl.BlockSpec((1,) + values.shape[1:], lambda g, k, *_: (g, 0, 0, 0))],
            out_specs=pl.BlockSpec((1, 1) + out.shape[2:], lambda g, k, *_: (k, g, 0, 0)),
        ),
        compiler_params=pltpu.CompilerParams(vmem_limit_bytes=48 * MIB),
        cost_estimate=pl.CostEstimate(
            flops=0, bytes_accessed=2 * (values.size + out.size), transcendentals=0
        ),
        name="spread_down",
    )(at, values)


def gate_up_kernel(*refs, parts):
    own, other = refs[:parts], refs[parts:2 * parts]
    weight = refs[2 * parts]
    outs, held = refs[2 * parts + 1:3 * parts + 1], refs[-1]
    count, half = own[0].shape

    @pl.when(pl.program_id(0) == 0)
    def _():
        for part in range(parts):
            rows = slice(part * count, (part + 1) * count)
            held[rows, :half] = own[part][...]
            held[rows, half:] = other[part][...]

    product = jnp.dot(held[...], weight[0], preferred_element_type=jnp.float32)
    for part in range(parts):
        outs[part][...] = product[part * count:(part + 1) * count].astype(outs[part].dtype)


def gate_up(own, other, dense, chunk):
    parts = len(own)
    count, half = own[0].shape
    _, depth, width = dense.shape
    tile = 256
    out = jax.ShapeDtypeStruct((count, width), own[0].dtype)
    return pl.pallas_call(
        functools.partial(gate_up_kernel, parts=parts),
        out_shape=[out] * parts,
        grid=(width // tile,),
        in_specs=[pl.BlockSpec((count, half), lambda n: (0, 0))] * (2 * parts)
        + [pl.BlockSpec((1, depth, tile), lambda n: (chunk, 0, n))],
        out_specs=[pl.BlockSpec((count, tile), lambda n: (0, n))] * parts,
        scratch_shapes=[pltpu.VMEM((parts * count, 2 * half), own[0].dtype)],
        compiler_params=pltpu.CompilerParams(vmem_limit_bytes=32 * MIB),
        cost_estimate=pl.CostEstimate(
            flops=2 * parts * count * depth * width,
            bytes_accessed=2 * (depth * width + parts * count * (depth + width)),
            transcendentals=0,
        ),
        name=f"gate_up_{chunk}",
    )(*own, *other, dense)


def down_kernel(hidden_ref, weight_ref, before_ref, out_ref, total):
    panel = pl.program_id(0)

    @pl.when(panel == 0)
    def _():
        total[...] = before_ref[...]

    total[...] += jnp.dot(hidden_ref[0], weight_ref[0, 0], preferred_element_type=jnp.float32)

    @pl.when(panel == pl.num_programs(0) - 1)
    def _():
        out_ref[...] = total[...].astype(out_ref.dtype)


def down(hidden, dense, before, chunk, dtype):
    panels, count, depth = hidden.shape
    width = dense.shape[-1]
    return pl.pallas_call(
        down_kernel,
        out_shape=jax.ShapeDtypeStruct((count, width), dtype),
        grid=(panels,),
        in_specs=[
            pl.BlockSpec((1, count, depth), lambda g: (g, 0, 0)),
            pl.BlockSpec((1, 1, depth, width), lambda g: (chunk, g, 0, 0)),
            pl.BlockSpec((count, width), lambda g: (0, 0)),
        ],
        out_specs=pl.BlockSpec((count, width), lambda g: (0, 0)),
        scratch_shapes=[pltpu.VMEM((count, width), jnp.float32)],
        compiler_params=pltpu.CompilerParams(vmem_limit_bytes=32 * MIB),
        cost_estimate=pl.CostEstimate(
            flops=2 * panels * count * depth * width,
            bytes_accessed=2 * panels * depth * (width + count) + 6 * count * width,
            transcendentals=0,
        ),
        name=f"down_{chunk}",
    )(hidden, dense, before)


def by_tokens(
    tokens,
    norm_gain,
    gate_block_entries,
    gate_block_places,
    up_block_entries,
    up_block_places,
    down_values,
    down_slots,
):
    edge = gate_block_entries.shape[-1]
    tok_size = lax.axis_size("tok")
    col_size = lax.axis_size("col")
    rows_per = MODEL_WIDTH // edge // tok_size
    cols_per = HIDDEN_UNITS // edge // col_size
    width_blocks = MODEL_WIDTH // edge // col_size
    chunks = 4 if cols_per % 4 == 0 else 1
    chunk_cols = cols_per // chunks
    count, features = tokens.shape
    half = MODEL_WIDTH // tok_size // 2
    tok, col = lax.axis_index("tok"), lax.axis_index("col")
    side = col % 2

    def swap_tok(array, step):
        return lax.ppermute(array, "tok", [(i, i ^ step) for i in range(tok_size)])

    def swap_core(array):
        return lax.ppermute(array, "col", [(i, i ^ 1) for i in range(col_size)])

    k, r, q = jnp.meshgrid(
        jnp.arange(chunks), jnp.arange(rows_per), jnp.arange(chunk_cols), indexing="ij"
    )
    row = (r + side * (rows_per // 2)) % rows_per
    slots = (row * cols_per + k * chunk_cols + q).reshape(-1).astype(jnp.int32)
    gate_at = lookup(gate_block_places[0], slots)
    up_at = lookup(up_block_places[0], slots)
    down_at = lookup(down_slots, jnp.arange(cols_per * width_blocks, dtype=jnp.int32)).reshape(-1)

    gathered = lax.all_gather(tokens, "col")
    dense = spread_gate_up(
        gate_at, up_at, gate_block_entries, up_block_entries, chunks, rows_per, chunk_cols
    )
    down_dense = spread_down(down_at, down_values, chunks, chunk_cols, width_blocks)

    widened = gathered.astype(jnp.float32)
    mean_square = jnp.mean(widened * widened, axis=(0, 2))[:, None]
    scale = lax.rsqrt(mean_square + EPSILON)
    subs = half // features

    def normed(panel):
        at = panel * 2 + side
        piece = lax.dynamic_slice_in_dim(gathered, at * subs, subs, 0)
        piece = piece.transpose(1, 0, 2).reshape(count, half).astype(jnp.float32)
        gain = lax.dynamic_slice_in_dim(norm_gain, at * half, half, 0)
        return (piece * scale * gain).astype(jnp.bfloat16)

    own = [normed(tok ^ part) for part in range(tok_size)]
    own = [own[0]] + [swap_tok(own[part], part) for part in range(1, tok_size)]
    other = [swap_core(part) for part in own]

    hiddens, halves = [], []
    for chunk in range(chunks):
        sums = gate_up(own, other, dense, chunk)
        terms = [sums[0]] + [swap_tok(sums[part], part) for part in range(1, tok_size)]
        total = functools.reduce(jnp.add, [term.astype(jnp.float32) for term in terms])
        gate_sum, up_sum = jnp.split(total, 2, axis=1)
        hiddens.append((jax.nn.silu(gate_sum) * up_sum).astype(jnp.bfloat16))

    mixed = jnp.zeros((count, width_blocks * edge), jnp.float32)
    for chunk in range(chunks):
        hidden = lax.all_gather(hiddens[chunk], "col")
        last = chunk == chunks - 1
        mixed = down(hidden, down_dense, mixed, chunk, jnp.bfloat16 if last else jnp.float32)
    return mixed

def spread_shares_kernel(gate_at, up_at, gate_ref, up_ref, out_ref, *, rows, shares, cols):
    chunk = pl.program_id(0)

    @pl.loop(0, rows)
    def _(row):
        for share in range(shares):
            for col in range(cols):
                at = ((chunk * rows + row) * shares + share) * cols + col
                put(out_ref, row, 2 * share * cols + col, gate_ref, gate_at[at])
                put(out_ref, row, (2 * share + 1) * cols + col, up_ref, up_at[at])


def spread_shares(gate_at, up_at, gate, up, chunks, rows, shares, cols):
    edge = gate.shape[-1]
    whole = pl.BlockSpec(gate.shape, lambda k, *_: (0, 0, 0, 0), pipeline_mode=pl.Buffered(1))
    out = jax.ShapeDtypeStruct((chunks, rows * edge, 2 * shares * cols * edge), gate.dtype)
    return pl.pallas_call(
        functools.partial(spread_shares_kernel, rows=rows, shares=shares, cols=cols),
        out_shape=out,
        grid_spec=pltpu.PrefetchScalarGridSpec(
            num_scalar_prefetch=2,
            grid=(chunks,),
            in_specs=[whole, whole],
            out_specs=pl.BlockSpec((1,) + out.shape[1:], lambda k, *_: (k, 0, 0)),
        ),
        compiler_params=pltpu.CompilerParams(vmem_limit_bytes=54 * MIB),
        cost_estimate=pl.CostEstimate(
            flops=0, bytes_accessed=2 * (2 * gate.size + out.size), transcendentals=0
        ),
        name="spread_gate_up",
    )(gate_at, up_at, gate, up)


def spread_panels_kernel(at_ref, panels_ref, values_ref, out_ref, *, chunks, rows, cols):
    panel = pl.program_id(0)
    for chunk in range(chunks):
        for row in range(rows):
            for col in range(cols):
                at = ((panel * chunks + chunk) * rows + row) * cols + col
                put(out_ref.at[pl.ds(chunk, 1)], row, col, values_ref, at_ref[at])


def spread_panels(at, panels, values, chunks, rows, cols):
    count, _, edge, _ = values.shape
    out = jax.ShapeDtypeStruct((chunks, count * rows * edge, cols * edge), values.dtype)
    return pl.pallas_call(
        functools.partial(spread_panels_kernel, chunks=chunks, rows=rows, cols=cols),
        out_shape=out,
        grid_spec=pltpu.PrefetchScalarGridSpec(
            num_scalar_prefetch=2,
            grid=(count,),
            in_specs=[
                pl.BlockSpec((1,) + values.shape[1:], lambda m, _, panels: (panels[m], 0, 0, 0))
            ],
            out_specs=pl.BlockSpec((chunks, rows * edge, cols * edge), lambda m, *_: (0, m, 0)),
        ),
        compiler_params=pltpu.CompilerParams(vmem_limit_bytes=16 * MIB),
        cost_estimate=pl.CostEstimate(
            flops=0, bytes_accessed=2 * (values.size + out.size), transcendentals=0
        ),
        name="spread_down",
    )(at, panels, values)

def sum_squares_kernel(tokens, _, out):
    widened = tokens[...].astype(jnp.float32)
    out[...] = jnp.sum(widened * widened, axis=1)[None]


def sum_squares(tokens, after):
    return pl.pallas_call(
        sum_squares_kernel,
        out_shape=jax.ShapeDtypeStruct((1, tokens.shape[0]), jnp.float32),
        in_specs=[pl.BlockSpec(memory_space=pltpu.VMEM), pl.BlockSpec(memory_space=pl.ANY)],
        out_specs=pl.BlockSpec(memory_space=pltpu.VMEM),
        compiler_params=pltpu.CompilerParams(vmem_limit_bytes=4 * MIB),
        name="sum_squares",
    )(tokens, after)


def pack_kernel(*refs, parts):
    pieces, scale, gain, out = refs[:parts], refs[parts], refs[parts + 1], refs[-1]
    count = pieces[0].shape[0]
    for part in range(parts):
        rows = slice(part * count, (part + 1) * count)
        piece = pieces[part][...].astype(jnp.float32)
        out[rows] = (piece * scale[rows] * gain[...]).astype(out.dtype)


def pack(pieces, scale, gain, after):
    parts = len(pieces)
    count, width = pieces[0].shape
    return pl.pallas_call(
        functools.partial(pack_kernel, parts=parts),
        out_shape=jax.ShapeDtypeStruct((parts * count, width), pieces[0].dtype),
        in_specs=[pl.BlockSpec(memory_space=pltpu.VMEM)] * (parts + 2)
        + [pl.BlockSpec(memory_space=pl.ANY)] * len(after),
        out_specs=pl.BlockSpec(memory_space=pltpu.VMEM),
        compiler_params=pltpu.CompilerParams(vmem_limit_bytes=16 * MIB),
        cost_estimate=pl.CostEstimate(
            flops=0, bytes_accessed=4 * parts * count * width, transcendentals=0
        ),
        name="pack",
    )(*pieces, scale, gain, *after)


def pack_hidden_kernel(*refs, parts):
    out = refs[-1]
    count = out.shape[1] // parts
    for step in range(parts):
        for part in range(parts):
            there = part ^ step
            out[step, part * count:(part + 1) * count] = refs[step][there * count:(there + 1) * count]


def pack_hidden(pieces, after):
    parts = len(pieces)
    return pl.pallas_call(
        functools.partial(pack_hidden_kernel, parts=parts),
        out_shape=jax.ShapeDtypeStruct((parts,) + pieces[0].shape, pieces[0].dtype),
        in_specs=[pl.BlockSpec(memory_space=pltpu.VMEM)] * parts
        + [pl.BlockSpec(memory_space=pl.ANY)] * len(after),
        out_specs=pl.BlockSpec(memory_space=pltpu.VMEM),
        compiler_params=pltpu.CompilerParams(vmem_limit_bytes=16 * MIB),
        cost_estimate=pl.CostEstimate(
            flops=0, bytes_accessed=4 * parts * pieces[0].size, transcendentals=0
        ),
        name="pack_hidden",
    )(*pieces, *after)


def halfway_kernel(kept_a, came_a, kept_b, came_b, _, out_a, out_b):
    for kept, came, out in ((kept_a, came_a, out_a), (kept_b, came_b, out_b)):
        out[...] = (kept[0].astype(jnp.float32) + came[0].astype(jnp.float32)).astype(out.dtype)


def halfway(kept_a, came_a, kept_b, came_b, after, chunk):
    _, count, width = kept_a.shape
    second = pl.BlockSpec((1, count, width), lambda i: (1, 0, 0))
    whole = pl.BlockSpec((count, width), lambda i: (0, 0))
    out = jax.ShapeDtypeStruct((count, width), kept_a.dtype)
    return pl.pallas_call(
        halfway_kernel,
        out_shape=[out, out],
        grid=(1,),
        in_specs=[second] * 4 + [pl.BlockSpec(memory_space=pl.ANY)],
        out_specs=[whole, whole],
        compiler_params=pltpu.CompilerParams(vmem_limit_bytes=8 * MIB),
        cost_estimate=pl.CostEstimate(
            flops=2 * count * width, bytes_accessed=12 * count * width, transcendentals=0
        ),
        name=f"halfway_{chunk}",
    )(kept_a, came_a, kept_b, came_b, after)


def combine_kernel(*refs):
    terms, out = refs[:6], refs[-1]
    count = out.shape[0] // 2
    width = out.shape[1]
    for i in range(2):
        kept, came, last = terms[3 * i:3 * i + 3]
        total = kept[0].astype(jnp.float32) + came[0].astype(jnp.float32)
        total += last[...].astype(jnp.float32)
        gate_sum, up_sum = total[:, :width], total[:, width:]
        hidden = gate_sum / (1.0 + jnp.exp(-gate_sum)) * up_sum
        out[i * count:(i + 1) * count] = hidden.astype(out.dtype)


def combine(kept_a, came_a, last_a, kept_b, came_b, last_b, after, chunk):
    count, width = last_a.shape
    first = pl.BlockSpec((1, count, width), lambda i: (0, 0, 0))
    whole = pl.BlockSpec((count, width), lambda i: (0, 0))
    return pl.pallas_call(
        combine_kernel,
        out_shape=jax.ShapeDtypeStruct((2 * count, width // 2), last_a.dtype),
        grid=(1,),
        in_specs=[first, first, whole] * 2 + [pl.BlockSpec(memory_space=pl.ANY)],
        out_specs=pl.BlockSpec((2 * count, width // 2), lambda i: (0, 0)),
        compiler_params=pltpu.CompilerParams(vmem_limit_bytes=10 * MIB),
        cost_estimate=pl.CostEstimate(
            flops=8 * count * width,
            bytes_accessed=14 * count * width,
            transcendentals=count * width // 2,
        ),
        name=f"combine_{chunk}",
    )(kept_a, came_a, last_a, kept_b, came_b, last_b, after)


def panel_product_kernel(own, other, weight, kept_a, sent_a, kept_b, sent_b):
    half = own.shape[1]
    product = jnp.dot(own[...], weight[0, :half], preferred_element_type=jnp.float32)
    product += jnp.dot(other[...], weight[0, half:], preferred_element_type=jnp.float32)
    product = product.astype(kept_a.dtype)
    count = product.shape[0] // 2
    part = pl.program_id(0)
    for flip in range(2):

        @pl.when(part % 2 == flip)
        def _():
            (sent_a if flip else kept_a)[part // 2] = product[:count]

        @pl.when(part // 2 == flip)
        def _():
            (sent_b if flip else kept_b)[part % 2] = product[count:]


def panel_product(own, other, dense, chunk):
    count, half = own.shape
    _, depth, width = dense.shape
    tile = width // 4
    out = jax.ShapeDtypeStruct((2, count // 2, tile), own.dtype)
    return pl.pallas_call(
        panel_product_kernel,
        out_shape=[out] * 4,
        grid=(4,),
        in_specs=[pl.BlockSpec((count, half), lambda n: (0, 0))] * 2
        + [pl.BlockSpec((1, depth, tile), lambda n: (chunk, 0, n))],
        out_specs=[pl.BlockSpec(out.shape, lambda n: (0, 0, 0))] * 4,
        compiler_params=pltpu.CompilerParams(vmem_limit_bytes=42 * MIB),
        cost_estimate=pl.CostEstimate(
            flops=2 * count * depth * width,
            bytes_accessed=2 * (depth * width + count * (depth + width)),
            transcendentals=0,
        ),
        name=f"gate_up_{chunk}",
    )(own, other, dense)


def down_product_kernel(flips, own, other, weight, *refs, added):
    before, outs, held = refs[:added], refs[added:-1], refs[-1]
    panels, _, depth = own.shape

    @pl.when(pl.program_id(0) == 0)
    def _():
        for i in range(panels):
            held[:, i * depth:(i + 1) * depth] = own[i]
            held[:, (panels + i) * depth:(panels + i + 1) * depth] = other[i]

    if len(outs) == 1:
        product = jnp.dot(held[...], weight[0], preferred_element_type=jnp.float32)
        for term in before:
            product += term[...]
        outs[0][...] = product
        return
    count = outs[0].shape[0]
    order = []
    for step, out in enumerate(outs):
        at = pl.multiple_of((flips[0] ^ step) * count, count)
        order.append(at)
    for step, out in enumerate(outs):
        rows = pl.ds(order[step], count)
        product = jnp.dot(held[rows], weight[0], preferred_element_type=jnp.float32)
        for term in before:
            product += term[rows]
        out[...] = product.astype(out.dtype)


def down_product(own, other, dense, before, chunk, flips):
    panels, count, depth = own.shape
    _, total, width = dense.shape
    tile = width // 2
    tiles = pl.BlockSpec((count, tile), lambda n, *_: (0, n))
    whole = pl.BlockSpec((panels, count, depth), lambda n, *_: (0, 0, 0))
    added = [] if before is None else [before]
    out, out_tiles = jax.ShapeDtypeStruct((count, width), jnp.float32), tiles
    if flips is not None:
        out = [jax.ShapeDtypeStruct((count // panels, width), own.dtype)] * panels
        out_tiles = [pl.BlockSpec((count // panels, tile), lambda n, *_: (0, n))] * panels
    return pl.pallas_call(
        functools.partial(down_product_kernel, added=len(added)),
        out_shape=out,
        grid_spec=pltpu.PrefetchScalarGridSpec(
            num_scalar_prefetch=1,
            grid=(width // tile,),
            in_specs=[whole, whole, pl.BlockSpec((1, total, tile), lambda n, *_: (chunk, 0, n))]
            + [tiles] * len(added),
            out_specs=out_tiles,
            scratch_shapes=[pltpu.VMEM((count, total), own.dtype)],
        ),
        compiler_params=pltpu.CompilerParams(vmem_limit_bytes=24 * MIB),
        cost_estimate=pl.CostEstimate(
            flops=2 * count * total * width,
            bytes_accessed=2 * total * (width + count) + 8 * count * width,
            transcendentals=0,
        ),
        name=f"down_{chunk}",
    )(jnp.int32(0)[None] if flips is None else flips[None], own, other, dense, *added)


def by_columns(
    tokens,
    norm_gain,
    gate_block_entries,
    gate_block_places,
    up_block_entries,
    up_block_places,
    down_values,
    down_slots,
):
    edge = gate_block_entries.shape[-1]
    tok_size = lax.axis_size("tok")
    col_size = lax.axis_size("col")
    rows_per = MODEL_WIDTH // edge // tok_size
    cols_per = HIDDEN_UNITS // edge // col_size
    width_blocks = MODEL_WIDTH // edge // col_size
    share = cols_per // tok_size
    chunks = 3 if share % 3 == 0 else 1
    cols = share // chunks
    count, half = tokens.shape
    tok, col = lax.axis_index("tok"), lax.axis_index("col")
    chip, side = col // 2, col % 2
    parts = range(tok_size)

    def swap_tok(array, step):
        return lax.ppermute(array, "tok", [(i, i ^ step) for i in parts])

    def swap_chip(array, step):
        return lax.ppermute(array, "col", [(i, i ^ (2 * step)) for i in range(col_size)])

    def swap_core(array):
        return lax.ppermute(array, "col", [(i, i ^ 1) for i in range(col_size)])

    def to_users(array, part):
        pairs = []
        for i in parts:
            for j in range(col_size):
                user = (j // 2) * col_size + 2 * (i ^ part) + j % 2
                pairs.append((i * col_size + j, user))
        return lax.ppermute(array, ("tok", "col"), pairs)

    pieces = [to_users(tokens, part) for part in parts]
    k, r, p, q = jnp.meshgrid(
        jnp.arange(chunks), jnp.arange(rows_per), jnp.arange(tok_size), jnp.arange(cols),
        indexing="ij",
    )
    row = (r + side * (rows_per // 2)) % rows_per
    slots = (row * cols_per + (p ^ tok) * share + k * cols + q).reshape(-1).astype(jnp.int32)
    gate_at = lookup(gate_block_places[0], slots)
    up_at = lookup(up_block_places[0], slots)
    m = jnp.arange(col_size, dtype=jnp.int32)
    panels = 2 * ((m % tok_size) ^ chip) + (side ^ (m // tok_size))
    slots = tok * share * width_blocks + jnp.arange(share * width_blocks, dtype=jnp.int32)
    down_at = jnp.take(lookup(down_slots, slots), panels, axis=0).reshape(-1)

    dense = spread_shares(
        gate_at, up_at, gate_block_entries, up_block_entries, chunks, rows_per, tok_size, cols
    )
    down_dense = spread_panels(down_at, panels, down_values, chunks, cols, width_blocks)

    squares = sum_squares(tokens, dense)
    squares += swap_core(squares)
    squares += swap_chip(squares, 1)
    squares += swap_chip(squares, 2)
    squares = jnp.concatenate([squares, swap_tok(squares, 1)])
    squares = jnp.concatenate([squares, swap_tok(squares, 2)])

    gain = lax.dynamic_slice_in_dim(norm_gain, (tok * 2 + side) * half, half, 0)[None]
    scale = lax.rsqrt(squares / MODEL_WIDTH + EPSILON)
    scale = jnp.take(scale, jnp.arange(tok_size) ^ chip ^ tok, axis=0).reshape(-1, 1)
    own = pack(pieces, scale, gain, [down_dense])
    other = swap_core(own)

    sums = [panel_product(own, other, dense, chunk) for chunk in range(chunks)]
    hiddens, halves = [], []
    for chunk in range(chunks):
        kept_a, sent_a, kept_b, sent_b = sums[chunk]
        came_a, came_b = swap_tok(sent_a, 1), swap_tok(sent_b, 2)
        ahead = sums[min(chunk + 1, chunks - 1)][0]
        last_a, last_b = halfway(kept_a, came_a, kept_b, came_b, ahead, chunk)
        halves.append(last_a)
        last_a, last_b = swap_tok(last_a, 2), swap_tok(last_b, 1)
        hidden = combine(kept_a, came_a, last_a, kept_b, came_b, last_b, sums[-1][0], chunk)
        hiddens.append(hidden)

    mixed = None
    for chunk in range(chunks):
        held = [hiddens[chunk]] + [swap_chip(hiddens[chunk], step) for step in parts[1:]]
        ahead = hiddens[chunk + 1:chunk + 2] + halves[chunk + 2:chunk + 3]
        ahead += [] if mixed is None else [mixed]
        held = pack_hidden(held, ahead)
        last = chip ^ tok if chunk == chunks - 1 else None
        mixed = down_product(held, swap_core(held), down_dense, mixed, chunk, last)

    total = mixed[0].astype(jnp.float32)
    for step in parts[1:]:
        total += swap_tok(mixed[step], step).astype(jnp.float32)
    return total.astype(jnp.bfloat16)


def shards(*arrays):
    tok_size = lax.axis_size("tok")
    col_size = lax.axis_size("col")
    blocks = HIDDEN_UNITS // arrays[2].shape[-1]
    even = blocks % (col_size * tok_size) == 0 and col_size == 2 * tok_size == 8
    return (by_columns if even else by_tokens)(*arrays)


def solution(mesh):
    return jax.shard_map(
        shards,
        mesh=mesh,
        in_specs=(
            P("tok", "col"),
            P(),
            P("tok", "col", None, None),
            P("tok", "col"),
            P("tok", "col", None, None),
            P("tok", "col"),
            P(None, "col", None, None),
            P(None, "col"),
        ),
        out_specs=P("tok", "col"),
        check_vma=False,
    )
```

```python
import functools

import jax
import jax.numpy as jnp
from jax import lax
from jax.experimental import pallas as pl
from jax.experimental.pallas import tpu as pltpu
from jax.sharding import PartitionSpec as P

MODEL_WIDTH = 8192
HIDDEN_UNITS = 24576

EPSILON = 1e-05
MIB = 1 << 20
MARK = jax.ShapeDtypeStruct((8, 128), jnp.float32)
MARK_SPEC = pl.BlockSpec(MARK.shape, lambda *_: (0, 0))
ANY_SPEC = pl.BlockSpec(memory_space=pl.ANY)


def leave(mark):
    mark[...] = jnp.zeros_like(mark)


def lookup(places, slots):
    hit = places[..., None, :] == slots[:, None]
    entry = jnp.arange(places.shape[-1], dtype=jnp.int32)
    return jnp.max(jnp.where(hit, entry, -1), axis=-1)


def put(out_ref, row, col, source_ref, entry):
    edge = source_ref.shape[-1]
    block = source_ref[0, jnp.maximum(entry, 0)]
    block = jnp.where(entry >= 0, block, jnp.zeros_like(block))
    out_ref[0, pl.ds(pl.multiple_of(row * edge, edge), edge), col * edge:(col + 1) * edge] = block


def spread_gate_up_kernel(gate_at, up_at, gate_ref, up_ref, out_ref, *, rows, cols):
    chunk = pl.program_id(0)

    @pl.loop(0, rows)
    def _(row):
        for col in range(cols):
            at = (chunk * rows + row) * cols + col
            put(out_ref, row, col, gate_ref, gate_at[at])
            put(out_ref, row, cols + col, up_ref, up_at[at])


def spread_gate_up(gate_at, up_at, gate, up, chunks, rows, cols):
    edge = gate.shape[-1]
    whole = pl.BlockSpec(gate.shape, lambda k, *_: (0, 0, 0, 0), pipeline_mode=pl.Buffered(1))
    out = jax.ShapeDtypeStruct((chunks, rows * edge, 2 * cols * edge), gate.dtype)
    return pl.pallas_call(
        functools.partial(spread_gate_up_kernel, rows=rows, cols=cols),
        out_shape=out,
        grid_spec=pltpu.PrefetchScalarGridSpec(
            num_scalar_prefetch=2,
            grid=(chunks,),
            in_specs=[whole, whole],
            out_specs=pl.BlockSpec((1,) + out.shape[1:], lambda k, *_: (k, 0, 0)),
        ),
        compiler_params=pltpu.CompilerParams(vmem_limit_bytes=48 * MIB),
        cost_estimate=pl.CostEstimate(
            flops=0, bytes_accessed=2 * (2 * gate.size + out.size), transcendentals=0
        ),
        name="spread_gate_up",
    )(gate_at, up_at, gate, up)


def spread_down_kernel(at_ref, values_ref, out_ref, *, rows, cols):
    panel, chunk = pl.program_id(0), pl.program_id(1)
    base = (panel * pl.num_programs(1) + chunk) * rows * cols

    @pl.loop(0, rows)
    def _(row):
        for col in range(cols):
            put(out_ref.at[0], row, col, values_ref, at_ref[base + row * cols + col])


def spread_down(at, values, chunks, rows, cols):
    panels, _, edge, _ = values.shape
    out = jax.ShapeDtypeStruct((chunks, panels, rows * edge, cols * edge), values.dtype)
    return pl.pallas_call(
        functools.partial(spread_down_kernel, rows=rows, cols=cols),
        out_shape=out,
        grid_spec=pltpu.PrefetchScalarGridSpec(
            num_scalar_prefetch=1,
            grid=(panels, chunks),
            in_specs=[pl.BlockSpec((1,) + values.shape[1:], lambda g, k, *_: (g, 0, 0, 0))],
            out_specs=pl.BlockSpec((1, 1) + out.shape[2:], lambda g, k, *_: (k, g, 0, 0)),
        ),
        compiler_params=pltpu.CompilerParams(vmem_limit_bytes=48 * MIB),
        cost_estimate=pl.CostEstimate(
            flops=0, bytes_accessed=2 * (values.size + out.size), transcendentals=0
        ),
        name="spread_down",
    )(at, values)


def gate_up_kernel(*refs, parts):
    own, other = refs[:parts], refs[parts:2 * parts]
    weight = refs[2 * parts]
    outs, held = refs[2 * parts + 1:3 * parts + 1], refs[-1]
    count, half = own[0].shape

    @pl.when(pl.program_id(0) == 0)
    def _():
        for part in range(parts):
            rows = slice(part * count, (part + 1) * count)
            held[rows, :half] = own[part][...]
            held[rows, half:] = other[part][...]

    product = jnp.dot(held[...], weight[0], preferred_element_type=jnp.float32)
    for part in range(parts):
        outs[part][...] = product[part * count:(part + 1) * count].astype(outs[part].dtype)


def gate_up(own, other, dense, chunk):
    parts = len(own)
    count, half = own[0].shape
    _, depth, width = dense.shape
    tile = 256
    out = jax.ShapeDtypeStruct((count, width), own[0].dtype)
    return pl.pallas_call(
        functools.partial(gate_up_kernel, parts=parts),
        out_shape=[out] * parts,
        grid=(width // tile,),
        in_specs=[pl.BlockSpec((count, half), lambda n: (0, 0))] * (2 * parts)
        + [pl.BlockSpec((1, depth, tile), lambda n: (chunk, 0, n))],
        out_specs=[pl.BlockSpec((count, tile), lambda n: (0, n))] * parts,
        scratch_shapes=[pltpu.VMEM((parts * count, 2 * half), own[0].dtype)],
        compiler_params=pltpu.CompilerParams(vmem_limit_bytes=32 * MIB),
        cost_estimate=pl.CostEstimate(
            flops=2 * parts * count * depth * width,
            bytes_accessed=2 * (depth * width + parts * count * (depth + width)),
            transcendentals=0,
        ),
        name=f"gate_up_{chunk}",
    )(*own, *other, dense)


def down_kernel(hidden_ref, weight_ref, before_ref, out_ref, total):
    panel = pl.program_id(0)

    @pl.when(panel == 0)
    def _():
        total[...] = before_ref[...]

    total[...] += jnp.dot(hidden_ref[0], weight_ref[0, 0], preferred_element_type=jnp.float32)

    @pl.when(panel == pl.num_programs(0) - 1)
    def _():
        out_ref[...] = total[...].astype(out_ref.dtype)


def down(hidden, dense, before, chunk, dtype):
    panels, count, depth = hidden.shape
    width = dense.shape[-1]
    return pl.pallas_call(
        down_kernel,
        out_shape=jax.ShapeDtypeStruct((count, width), dtype),
        grid=(panels,),
        in_specs=[
            pl.BlockSpec((1, count, depth), lambda g: (g, 0, 0)),
            pl.BlockSpec((1, 1, depth, width), lambda g: (chunk, g, 0, 0)),
            pl.BlockSpec((count, width), lambda g: (0, 0)),
        ],
        out_specs=pl.BlockSpec((count, width), lambda g: (0, 0)),
        scratch_shapes=[pltpu.VMEM((count, width), jnp.float32)],
        compiler_params=pltpu.CompilerParams(vmem_limit_bytes=32 * MIB),
        cost_estimate=pl.CostEstimate(
            flops=2 * panels * count * depth * width,
            bytes_accessed=2 * panels * depth * (width + count) + 6 * count * width,
            transcendentals=0,
        ),
        name=f"down_{chunk}",
    )(hidden, dense, before)


def by_tokens(
    tokens,
    norm_gain,
    gate_block_entries,
    gate_block_places,
    up_block_entries,
    up_block_places,
    down_values,
    down_slots,
):
    edge = gate_block_entries.shape[-1]
    tok_size = lax.axis_size("tok")
    col_size = lax.axis_size("col")
    rows_per = MODEL_WIDTH // edge // tok_size
    cols_per = HIDDEN_UNITS // edge // col_size
    width_blocks = MODEL_WIDTH // edge // col_size
    chunks = 4 if cols_per % 4 == 0 else 1
    chunk_cols = cols_per // chunks
    count, features = tokens.shape
    half = MODEL_WIDTH // tok_size // 2
    tok, col = lax.axis_index("tok"), lax.axis_index("col")
    side = col % 2

    def swap_tok(array, step):
        return lax.ppermute(array, "tok", [(i, i ^ step) for i in range(tok_size)])

    def swap_core(array):
        return lax.ppermute(array, "col", [(i, i ^ 1) for i in range(col_size)])

    k, r, q = jnp.meshgrid(
        jnp.arange(chunks), jnp.arange(rows_per), jnp.arange(chunk_cols), indexing="ij"
    )
    row = (r + side * (rows_per // 2)) % rows_per
    slots = (row * cols_per + k * chunk_cols + q).reshape(-1).astype(jnp.int32)
    gate_at = lookup(gate_block_places[0], slots)
    up_at = lookup(up_block_places[0], slots)
    down_at = lookup(down_slots, jnp.arange(cols_per * width_blocks, dtype=jnp.int32)).reshape(-1)

    gathered = lax.all_gather(tokens, "col")
    dense = spread_gate_up(
        gate_at, up_at, gate_block_entries, up_block_entries, chunks, rows_per, chunk_cols
    )
    down_dense = spread_down(down_at, down_values, chunks, chunk_cols, width_blocks)

    widened = gathered.astype(jnp.float32)
    mean_square = jnp.mean(widened * widened, axis=(0, 2))[:, None]
    scale = lax.rsqrt(mean_square + EPSILON)
    subs = half // features

    def normed(panel):
        at = panel * 2 + side
        piece = lax.dynamic_slice_in_dim(gathered, at * subs, subs, 0)
        piece = piece.transpose(1, 0, 2).reshape(count, half).astype(jnp.float32)
        gain = lax.dynamic_slice_in_dim(norm_gain, at * half, half, 0)
        return (piece * scale * gain).astype(jnp.bfloat16)

    own = [normed(tok ^ part) for part in range(tok_size)]
    own = [own[0]] + [swap_tok(own[part], part) for part in range(1, tok_size)]
    other = [swap_core(part) for part in own]

    hiddens, halves = [], []
    for chunk in range(chunks):
        sums = gate_up(own, other, dense, chunk)
        terms = [sums[0]] + [swap_tok(sums[part], part) for part in range(1, tok_size)]
        total = functools.reduce(jnp.add, [term.astype(jnp.float32) for term in terms])
        gate_sum, up_sum = jnp.split(total, 2, axis=1)
        hiddens.append((jax.nn.silu(gate_sum) * up_sum).astype(jnp.bfloat16))

    mixed = jnp.zeros((count, width_blocks * edge), jnp.float32)
    for chunk in range(chunks):
        hidden = lax.all_gather(hiddens[chunk], "col")
        last = chunk == chunks - 1
        mixed = down(hidden, down_dense, mixed, chunk, jnp.bfloat16 if last else jnp.float32)
    return mixed

def spread_shares_kernel(gate_at, up_at, *refs, rows, shares, cols):
    (gate_ref, up_ref), (out_ref, mark) = refs[:2], refs[-2:]
    step = pl.program_id(0)
    leave(mark)

    @pl.loop(0, rows)
    def _(row):
        for share in range(shares):
            for col in range(cols):
                at = ((step * rows + row) * shares + share) * cols + col
                put(out_ref, row, 2 * share * cols + col, gate_ref, gate_at[at])
                put(out_ref, row, (2 * share + 1) * cols + col, up_ref, up_at[at])


def spread_shares(gate_at, up_at, gate, up, rows, shares, cols, after, chunk):
    edge = gate.shape[-1]
    steps = 4
    whole = pl.BlockSpec(gate.shape, lambda k, *_: (0, 0, 0, 0), pipeline_mode=pl.Buffered(1))
    out = jax.ShapeDtypeStruct((1, rows * edge, 2 * shares * cols * edge), gate.dtype)
    block = (1, out.shape[1] // steps, out.shape[2])
    return pl.pallas_call(
        functools.partial(spread_shares_kernel, rows=rows // steps, shares=shares, cols=cols),
        out_shape=[out, MARK],
        grid_spec=pltpu.PrefetchScalarGridSpec(
            num_scalar_prefetch=2,
            grid=(steps,),
            in_specs=[whole, whole] + [ANY_SPEC] * len(after),
            out_specs=[pl.BlockSpec(block, lambda k, *_: (0, k, 0)), MARK_SPEC],
        ),
        compiler_params=pltpu.CompilerParams(vmem_limit_bytes=54 * MIB),
        cost_estimate=pl.CostEstimate(
            flops=0, bytes_accessed=2 * (2 * gate.size + out.size), transcendentals=0
        ),
        name=f"spread_gate_up_{chunk}",
    )(gate_at, up_at, gate, up, *after)


def spread_panels_kernel(at_ref, values_ref, *refs, chunks, rows, cols):
    out_ref, mark = refs[-2:]
    panel = pl.program_id(0)
    leave(mark)
    for chunk in range(chunks):
        for row in range(rows):
            for col in range(cols):
                at = ((panel * chunks + chunk) * rows + row) * cols + col
                put(out_ref.at[pl.ds(chunk, 1)], row, col, values_ref, at_ref[at])


def spread_panels(at, values, chunks, rows, cols, after):
    count, _, edge, _ = values.shape
    out = jax.ShapeDtypeStruct((chunks, count * rows * edge, cols * edge), values.dtype)
    return pl.pallas_call(
        functools.partial(spread_panels_kernel, chunks=chunks, rows=rows, cols=cols),
        out_shape=[out, MARK],
        grid_spec=pltpu.PrefetchScalarGridSpec(
            num_scalar_prefetch=1,
            grid=(count,),
            in_specs=[
                pl.BlockSpec((1,) + values.shape[1:], lambda m, *_: (m, 0, 0, 0))
            ]
            + [ANY_SPEC] * len(after),
            out_specs=[
                pl.BlockSpec((chunks, rows * edge, cols * edge), lambda m, *_: (0, m, 0)),
                MARK_SPEC,
            ],
        ),
        compiler_params=pltpu.CompilerParams(vmem_limit_bytes=50 * MIB),
        cost_estimate=pl.CostEstimate(
            flops=0, bytes_accessed=2 * (values.size + out.size), transcendentals=0
        ),
        name="spread_down",
    )(at, values, *after)

def sum_squares_kernel(tokens, out):
    widened = tokens[...].astype(jnp.float32)
    out[...] = jnp.sum(widened * widened, axis=1)[None]


def sum_squares(tokens):
    return pl.pallas_call(
        sum_squares_kernel,
        out_shape=jax.ShapeDtypeStruct((1, tokens.shape[0]), jnp.float32),
        in_specs=[pl.BlockSpec(memory_space=pltpu.VMEM)],
        out_specs=pl.BlockSpec(memory_space=pltpu.VMEM),
        compiler_params=pltpu.CompilerParams(vmem_limit_bytes=4 * MIB),
        name="sum_squares",
    )(tokens)


def pack_kernel(*refs, parts):
    pieces, scale, gain, out = refs[:parts], refs[parts], refs[parts + 1], refs[-1]
    count = pieces[0].shape[0]
    for part in range(parts):
        rows = slice(part * count, (part + 1) * count)
        piece = pieces[part][...].astype(jnp.float32)
        out[rows] = (piece * scale[rows] * gain[...]).astype(out.dtype)


def pack(pieces, scale, gain, after):
    parts = len(pieces)
    count, width = pieces[0].shape
    return pl.pallas_call(
        functools.partial(pack_kernel, parts=parts),
        out_shape=jax.ShapeDtypeStruct((parts * count, width), pieces[0].dtype),
        in_specs=[pl.BlockSpec(memory_space=pltpu.VMEM)] * (parts + 2)
        + [pl.BlockSpec(memory_space=pl.ANY)] * len(after),
        out_specs=pl.BlockSpec(memory_space=pltpu.VMEM),
        compiler_params=pltpu.CompilerParams(vmem_limit_bytes=16 * MIB),
        cost_estimate=pl.CostEstimate(
            flops=0, bytes_accessed=4 * parts * count * width, transcendentals=0
        ),
        name="pack",
    )(*pieces, scale, gain, *after)


def halfway_kernel(kept_a, came_a, kept_b, came_b, *refs):
    out_a, out_b, mark = refs[-3:]
    leave(mark)
    for kept, came, out in ((kept_a, came_a, out_a), (kept_b, came_b, out_b)):
        out[...] = (kept[0].astype(jnp.float32) + came[0].astype(jnp.float32)).astype(out.dtype)


def halfway(kept_a, came_a, kept_b, came_b, after, chunk):
    _, count, width = kept_a.shape
    second = pl.BlockSpec((1, count, width), lambda i: (1, 0, 0))
    whole = pl.BlockSpec((count, width), lambda i: (0, 0))
    out = jax.ShapeDtypeStruct((count, width), kept_a.dtype)
    return pl.pallas_call(
        halfway_kernel,
        out_shape=[out, out, MARK],
        grid=(1,),
        in_specs=[second] * 4 + [ANY_SPEC] * len(after),
        out_specs=[whole, whole, MARK_SPEC],
        compiler_params=pltpu.CompilerParams(vmem_limit_bytes=8 * MIB),
        cost_estimate=pl.CostEstimate(
            flops=2 * count * width, bytes_accessed=12 * count * width, transcendentals=0
        ),
        name=f"halfway_{chunk}",
    )(kept_a, came_a, kept_b, came_b, *after)


def combine_kernel(*refs):
    terms, out, mark = refs[:6], refs[-2], refs[-1]
    leave(mark)
    count = out.shape[0] // 2
    width = out.shape[1]
    for i in range(2):
        kept, came, last = terms[3 * i:3 * i + 3]
        total = kept[0].astype(jnp.float32) + came[0].astype(jnp.float32)
        total += last[...].astype(jnp.float32)
        gate_sum, up_sum = total[:, :width], total[:, width:]
        hidden = gate_sum / (1.0 + jnp.exp(-gate_sum)) * up_sum
        out[i * count:(i + 1) * count] = hidden.astype(out.dtype)


def combine(kept_a, came_a, last_a, kept_b, came_b, last_b, after, chunk):
    count, width = last_a.shape
    first = pl.BlockSpec((1, count, width), lambda i: (0, 0, 0))
    whole = pl.BlockSpec((count, width), lambda i: (0, 0))
    return pl.pallas_call(
        combine_kernel,
        out_shape=[jax.ShapeDtypeStruct((2 * count, width // 2), last_a.dtype), MARK],
        grid=(1,),
        in_specs=[first, first, whole] * 2 + [ANY_SPEC] * len(after),
        out_specs=[pl.BlockSpec((2 * count, width // 2), lambda i: (0, 0)), MARK_SPEC],
        compiler_params=pltpu.CompilerParams(vmem_limit_bytes=10 * MIB),
        cost_estimate=pl.CostEstimate(
            flops=8 * count * width,
            bytes_accessed=14 * count * width,
            transcendentals=count * width // 2,
        ),
        name=f"combine_{chunk}",
    )(kept_a, came_a, last_a, kept_b, came_b, last_b, *after)


def panel_product_kernel(own, other, weight, *refs):
    kept_a, sent_a, kept_b, sent_b, mark = refs[-5:]
    leave(mark)
    half = own.shape[1]
    product = jnp.dot(own[...], weight[0, :half], preferred_element_type=jnp.float32)
    product += jnp.dot(other[...], weight[0, half:], preferred_element_type=jnp.float32)
    product = product.astype(kept_a.dtype)
    count = product.shape[0] // 2
    part = pl.program_id(0)
    for flip in range(2):

        @pl.when(part % 2 == flip)
        def _():
            (sent_a if flip else kept_a)[part // 2] = product[:count]

        @pl.when(part // 2 == flip)
        def _():
            (sent_b if flip else kept_b)[part % 2] = product[count:]


def panel_product(own, other, dense, after, chunk):
    count, half = own.shape
    _, depth, width = dense.shape
    tile = width // 4
    out = jax.ShapeDtypeStruct((2, count // 2, tile), own.dtype)
    return pl.pallas_call(
        panel_product_kernel,
        out_shape=[out] * 4 + [MARK],
        grid=(4,),
        in_specs=[pl.BlockSpec((count, half), lambda n: (0, 0))] * 2
        + [pl.BlockSpec((1, depth, tile), lambda n: (0, 0, n))]
        + [ANY_SPEC] * len(after),
        out_specs=[pl.BlockSpec(out.shape, lambda n: (0, 0, 0))] * 4 + [MARK_SPEC],
        compiler_params=pltpu.CompilerParams(vmem_limit_bytes=54 * MIB),
        cost_estimate=pl.CostEstimate(
            flops=2 * count * depth * width,
            bytes_accessed=2 * (depth * width + count * (depth + width)),
            transcendentals=0,
        ),
        name=f"gate_up_{chunk}",
    )(own, other, dense, *after)


def down_product_kernel(place, hidden, weight, *refs, added):
    before, outs, mark, held = refs[:added], refs[added:-2], refs[-2], refs[-1]
    leave(mark)
    panels, parts, count, depth = hidden.shape
    chip, flips = place[0], place[1]

    @pl.when(pl.program_id(0) == 0)
    def _():
        for panel in range(panels):
            columns = slice(panel * depth, (panel + 1) * depth)
            for part in range(parts):
                there = part ^ chip ^ (panel // 2)
                held[part * count:(part + 1) * count, columns] = hidden[panel, there]

    if len(outs) == 1:
        product = jnp.dot(held[...], weight[0], preferred_element_type=jnp.float32)
        for term in before:
            product += term[...]
        outs[0][...] = product
        return
    for step, out in enumerate(outs):
        rows = pl.ds(pl.multiple_of((flips ^ step) * count, count), count)
        product = jnp.dot(held[rows], weight[0], preferred_element_type=jnp.float32)
        for term in before:
            product += term[rows]
        out[...] = product.astype(out.dtype)


def down_product(place, hidden, dense, before, chunk, last):
    panels, parts, count, depth = hidden.shape
    _, total, width = dense.shape
    tile = width // 2
    tiles = pl.BlockSpec((parts * count, tile), lambda n, *_: (0, n))
    added = [] if before is None else [before]
    if last:
        out = [jax.ShapeDtypeStruct((count, width), hidden.dtype)] * parts
        out_tiles = [pl.BlockSpec((count, tile), lambda n, *_: (0, n))] * parts
    else:
        out, out_tiles = [jax.ShapeDtypeStruct((parts * count, width), jnp.float32)], [tiles]
    return pl.pallas_call(
        functools.partial(down_product_kernel, added=len(added)),
        out_shape=out + [MARK],
        grid_spec=pltpu.PrefetchScalarGridSpec(
            num_scalar_prefetch=1,
            grid=(width // tile,),
            in_specs=[
                pl.BlockSpec(hidden.shape, lambda n, *_: (0, 0, 0, 0)),
                pl.BlockSpec((1, total, tile), lambda n, *_: (chunk, 0, n)),
            ]
            + [tiles] * len(added),
            out_specs=out_tiles + [MARK_SPEC],
            scratch_shapes=[pltpu.VMEM((parts * count, total), hidden.dtype)],
        ),
        compiler_params=pltpu.CompilerParams(vmem_limit_bytes=50 * MIB),
        cost_estimate=pl.CostEstimate(
            flops=2 * parts * count * total * width,
            bytes_accessed=2 * total * (width + parts * count) + 8 * parts * count * width,
            transcendentals=0,
        ),
        name=f"down_{chunk}",
    )(place, hidden, dense, *added)


def by_columns(
    tokens,
    norm_gain,
    gate_block_entries,
    gate_block_places,
    up_block_entries,
    up_block_places,
    down_values,
    down_slots,
):
    edge = gate_block_entries.shape[-1]
    tok_size = lax.axis_size("tok")
    col_size = lax.axis_size("col")
    rows_per = MODEL_WIDTH // edge // tok_size
    cols_per = HIDDEN_UNITS // edge // col_size
    width_blocks = MODEL_WIDTH // edge // col_size
    share = cols_per // tok_size
    chunks = 2 if share % 2 == 0 else 1
    cols = share // chunks
    count, half = tokens.shape
    tok, col = lax.axis_index("tok"), lax.axis_index("col")
    chip, side = col // 2, col % 2
    parts = range(tok_size)

    def swap_tok(array, step):
        return lax.ppermute(array, "tok", [(i, i ^ step) for i in parts])

    def swap_chip(array, step):
        return lax.ppermute(array, "col", [(i, i ^ (2 * step)) for i in range(col_size)])

    def swap_core(array):
        return lax.ppermute(array, "col", [(i, i ^ 1) for i in range(col_size)])

    def to_users(array, part):
        pairs = []
        for i in parts:
            for j in range(col_size):
                user = (j // 2) * col_size + 2 * (i ^ part) + j % 2
                pairs.append((i * col_size + j, user))
        return lax.ppermute(array, ("tok", "col"), pairs)

    pieces = [to_users(tokens, part) for part in parts]
    k, r, p, q = jnp.meshgrid(
        jnp.arange(chunks), jnp.arange(rows_per), jnp.arange(tok_size), jnp.arange(cols),
        indexing="ij",
    )
    row = (r + side * (rows_per // 2)) % rows_per
    slots = (row * cols_per + (p ^ tok) * share + k * cols + q).reshape(-1).astype(jnp.int32)
    gate_at = lookup(gate_block_places[0], slots)
    up_at = lookup(up_block_places[0], slots)
    slots = tok * share * width_blocks + jnp.arange(share * width_blocks, dtype=jnp.int32)
    down_at = lookup(down_slots, slots).reshape(-1)
    gate_at, up_at = gate_at.reshape(chunks, -1), up_at.reshape(chunks, -1)

    def spread(chunk, after):
        return spread_shares(
            gate_at[chunk], up_at[chunk], gate_block_entries, up_block_entries,
            rows_per, tok_size, cols, after, chunk,
        )

    squares = sum_squares(tokens)
    squares += swap_core(squares)
    squares += swap_chip(squares, 1)
    squares += swap_chip(squares, 2)
    squares = jnp.concatenate([squares, swap_tok(squares, 1)])
    squares = jnp.concatenate([squares, swap_tok(squares, 2)])

    gain = lax.dynamic_slice_in_dim(norm_gain, (tok * 2 + side) * half, half, 0)[None]
    scale = lax.rsqrt(squares / MODEL_WIDTH + EPSILON)
    scale = jnp.take(scale, jnp.arange(tok_size) ^ chip ^ tok, axis=0).reshape(-1, 1)
    dense, mark = spread(0, [])
    own = pack(pieces, scale, gain, [mark])
    other = swap_core(own)

    place = jnp.stack([chip, chip ^ tok])
    hiddens = []
    *sums, mark = panel_product(own, other, dense, [], 0)
    if chunks > 1:
        dense, mark = spread(1, [mark])
    for chunk in range(chunks):
        kept_a, sent_a, kept_b, sent_b = sums
        came_a, came_b = swap_tok(sent_a, 1), swap_tok(sent_b, 2)
        if chunk + 1 < chunks:
            *sums, mark = panel_product(own, other, dense, [mark], chunk + 1)
        last_a, last_b, mark = halfway(kept_a, came_a, kept_b, came_b, [mark], chunk)
        last_a, last_b = swap_tok(last_a, 2), swap_tok(last_b, 1)
        if chunk + 2 < chunks:
            dense, mark = spread(chunk + 2, [mark])
        elif chunk == max(chunks - 2, 0):
            down_dense, mark = spread_panels(
                down_at, down_values, chunks, cols, width_blocks, [mark]
            )
        hidden, mark = combine(kept_a, came_a, last_a, kept_b, came_b, last_b, [mark], chunk)
        hiddens.append(lax.all_gather(hidden.reshape(tok_size, count, -1), "col"))

    mixed = [None]
    for chunk in range(chunks):
        last = chunk == chunks - 1
        *mixed, _ = down_product(place, hiddens[chunk], down_dense, mixed[0], chunk, last)

    total = mixed[0].astype(jnp.float32)
    for step in parts[1:]:
        total += swap_tok(mixed[step], step).astype(jnp.float32)
    return total.astype(jnp.bfloat16)


def shards(*arrays):
    tok_size = lax.axis_size("tok")
    col_size = lax.axis_size("col")
    blocks = HIDDEN_UNITS // arrays[2].shape[-1]
    even = blocks % (col_size * tok_size) == 0 and col_size == 2 * tok_size == 8
    return (by_columns if even else by_tokens)(*arrays)


def solution(mesh):
    return jax.shard_map(
        shards,
        mesh=mesh,
        in_specs=(
            P("tok", "col"),
            P(),
            P("tok", "col", None, None),
            P("tok", "col"),
            P("tok", "col", None, None),
            P("tok", "col"),
            P(None, "col", None, None),
            P(None, "col"),
        ),
        out_specs=P("tok", "col"),
        check_vma=False,
    )
```

```python
import functools

import jax
import jax.numpy as jnp
from jax import lax
from jax.experimental import pallas as pl
from jax.experimental.pallas import tpu as pltpu
from jax.sharding import PartitionSpec as P

MODEL_WIDTH = 8192
HIDDEN_UNITS = 24576

EPSILON = 1e-05
MIB = 1 << 20
MARK = jax.ShapeDtypeStruct((8, 128), jnp.float32)
MARK_SPEC = pl.BlockSpec(MARK.shape, lambda *_: (0, 0))
ANY_SPEC = pl.BlockSpec(memory_space=pl.ANY)


def leave(mark):
    mark[...] = jnp.zeros_like(mark)


def lookup(places, slots):
    hit = places[..., None, :] == slots[:, None]
    entry = jnp.arange(places.shape[-1], dtype=jnp.int32)
    return jnp.max(jnp.where(hit, entry, -1), axis=-1)


def put(out_ref, row, col, source_ref, entry):
    edge = source_ref.shape[-1]
    block = source_ref[0, jnp.maximum(entry, 0)]
    block = jnp.where(entry >= 0, block, jnp.zeros_like(block))
    out_ref[0, pl.ds(pl.multiple_of(row * edge, edge), edge), col * edge:(col + 1) * edge] = block


def spread_gate_up_kernel(gate_at, up_at, gate_ref, up_ref, out_ref, *, rows, cols):
    chunk = pl.program_id(0)

    @pl.loop(0, rows)
    def _(row):
        for col in range(cols):
            at = (chunk * rows + row) * cols + col
            put(out_ref, row, col, gate_ref, gate_at[at])
            put(out_ref, row, cols + col, up_ref, up_at[at])


def spread_gate_up(gate_at, up_at, gate, up, chunks, rows, cols):
    edge = gate.shape[-1]
    whole = pl.BlockSpec(gate.shape, lambda k, *_: (0, 0, 0, 0), pipeline_mode=pl.Buffered(1))
    out = jax.ShapeDtypeStruct((chunks, rows * edge, 2 * cols * edge), gate.dtype)
    return pl.pallas_call(
        functools.partial(spread_gate_up_kernel, rows=rows, cols=cols),
        out_shape=out,
        grid_spec=pltpu.PrefetchScalarGridSpec(
            num_scalar_prefetch=2,
            grid=(chunks,),
            in_specs=[whole, whole],
            out_specs=pl.BlockSpec((1,) + out.shape[1:], lambda k, *_: (k, 0, 0)),
        ),
        compiler_params=pltpu.CompilerParams(vmem_limit_bytes=48 * MIB),
        cost_estimate=pl.CostEstimate(
            flops=0, bytes_accessed=2 * (2 * gate.size + out.size), transcendentals=0
        ),
        name="spread_gate_up",
    )(gate_at, up_at, gate, up)


def spread_down_kernel(at_ref, values_ref, out_ref, *, rows, cols):
    panel, chunk = pl.program_id(0), pl.program_id(1)
    base = (panel * pl.num_programs(1) + chunk) * rows * cols

    @pl.loop(0, rows)
    def _(row):
        for col in range(cols):
            put(out_ref.at[0], row, col, values_ref, at_ref[base + row * cols + col])


def spread_down(at, values, chunks, rows, cols):
    panels, _, edge, _ = values.shape
    out = jax.ShapeDtypeStruct((chunks, panels, rows * edge, cols * edge), values.dtype)
    return pl.pallas_call(
        functools.partial(spread_down_kernel, rows=rows, cols=cols),
        out_shape=out,
        grid_spec=pltpu.PrefetchScalarGridSpec(
            num_scalar_prefetch=1,
            grid=(panels, chunks),
            in_specs=[pl.BlockSpec((1,) + values.shape[1:], lambda g, k, *_: (g, 0, 0, 0))],
            out_specs=pl.BlockSpec((1, 1) + out.shape[2:], lambda g, k, *_: (k, g, 0, 0)),
        ),
        compiler_params=pltpu.CompilerParams(vmem_limit_bytes=48 * MIB),
        cost_estimate=pl.CostEstimate(
            flops=0, bytes_accessed=2 * (values.size + out.size), transcendentals=0
        ),
        name="spread_down",
    )(at, values)


def gate_up_kernel(*refs, parts):
    own, other = refs[:parts], refs[parts:2 * parts]
    weight = refs[2 * parts]
    outs, held = refs[2 * parts + 1:3 * parts + 1], refs[-1]
    count, half = own[0].shape

    @pl.when(pl.program_id(0) == 0)
    def _():
        for part in range(parts):
            rows = slice(part * count, (part + 1) * count)
            held[rows, :half] = own[part][...]
            held[rows, half:] = other[part][...]

    product = jnp.dot(held[...], weight[0], preferred_element_type=jnp.float32)
    for part in range(parts):
        outs[part][...] = product[part * count:(part + 1) * count].astype(outs[part].dtype)


def gate_up(own, other, dense, chunk):
    parts = len(own)
    count, half = own[0].shape
    _, depth, width = dense.shape
    tile = 256
    out = jax.ShapeDtypeStruct((count, width), own[0].dtype)
    return pl.pallas_call(
        functools.partial(gate_up_kernel, parts=parts),
        out_shape=[out] * parts,
        grid=(width // tile,),
        in_specs=[pl.BlockSpec((count, half), lambda n: (0, 0))] * (2 * parts)
        + [pl.BlockSpec((1, depth, tile), lambda n: (chunk, 0, n))],
        out_specs=[pl.BlockSpec((count, tile), lambda n: (0, n))] * parts,
        scratch_shapes=[pltpu.VMEM((parts * count, 2 * half), own[0].dtype)],
        compiler_params=pltpu.CompilerParams(vmem_limit_bytes=32 * MIB),
        cost_estimate=pl.CostEstimate(
            flops=2 * parts * count * depth * width,
            bytes_accessed=2 * (depth * width + parts * count * (depth + width)),
            transcendentals=0,
        ),
        name=f"gate_up_{chunk}",
    )(*own, *other, dense)


def down_kernel(hidden_ref, weight_ref, before_ref, out_ref, total):
    panel = pl.program_id(0)

    @pl.when(panel == 0)
    def _():
        total[...] = before_ref[...]

    total[...] += jnp.dot(hidden_ref[0], weight_ref[0, 0], preferred_element_type=jnp.float32)

    @pl.when(panel == pl.num_programs(0) - 1)
    def _():
        out_ref[...] = total[...].astype(out_ref.dtype)


def down(hidden, dense, before, chunk, dtype):
    panels, count, depth = hidden.shape
    width = dense.shape[-1]
    return pl.pallas_call(
        down_kernel,
        out_shape=jax.ShapeDtypeStruct((count, width), dtype),
        grid=(panels,),
        in_specs=[
            pl.BlockSpec((1, count, depth), lambda g: (g, 0, 0)),
            pl.BlockSpec((1, 1, depth, width), lambda g: (chunk, g, 0, 0)),
            pl.BlockSpec((count, width), lambda g: (0, 0)),
        ],
        out_specs=pl.BlockSpec((count, width), lambda g: (0, 0)),
        scratch_shapes=[pltpu.VMEM((count, width), jnp.float32)],
        compiler_params=pltpu.CompilerParams(vmem_limit_bytes=32 * MIB),
        cost_estimate=pl.CostEstimate(
            flops=2 * panels * count * depth * width,
            bytes_accessed=2 * panels * depth * (width + count) + 6 * count * width,
            transcendentals=0,
        ),
        name=f"down_{chunk}",
    )(hidden, dense, before)


def by_tokens(
    tokens,
    norm_gain,
    gate_block_entries,
    gate_block_places,
    up_block_entries,
    up_block_places,
    down_values,
    down_slots,
):
    edge = gate_block_entries.shape[-1]
    tok_size = lax.axis_size("tok")
    col_size = lax.axis_size("col")
    rows_per = MODEL_WIDTH // edge // tok_size
    cols_per = HIDDEN_UNITS // edge // col_size
    width_blocks = MODEL_WIDTH // edge // col_size
    chunks = 4 if cols_per % 4 == 0 else 1
    chunk_cols = cols_per // chunks
    count, features = tokens.shape
    half = MODEL_WIDTH // tok_size // 2
    tok, col = lax.axis_index("tok"), lax.axis_index("col")
    side = col % 2

    def swap_tok(array, step):
        return lax.ppermute(array, "tok", [(i, i ^ step) for i in range(tok_size)])

    def swap_core(array):
        return lax.ppermute(array, "col", [(i, i ^ 1) for i in range(col_size)])

    k, r, q = jnp.meshgrid(
        jnp.arange(chunks), jnp.arange(rows_per), jnp.arange(chunk_cols), indexing="ij"
    )
    row = (r + side * (rows_per // 2)) % rows_per
    slots = (row * cols_per + k * chunk_cols + q).reshape(-1).astype(jnp.int32)
    gate_at = lookup(gate_block_places[0], slots)
    up_at = lookup(up_block_places[0], slots)
    down_at = lookup(down_slots, jnp.arange(cols_per * width_blocks, dtype=jnp.int32)).reshape(-1)

    gathered = lax.all_gather(tokens, "col")
    dense = spread_gate_up(
        gate_at, up_at, gate_block_entries, up_block_entries, chunks, rows_per, chunk_cols
    )
    down_dense = spread_down(down_at, down_values, chunks, chunk_cols, width_blocks)

    widened = gathered.astype(jnp.float32)
    mean_square = jnp.mean(widened * widened, axis=(0, 2))[:, None]
    scale = lax.rsqrt(mean_square + EPSILON)
    subs = half // features

    def normed(panel):
        at = panel * 2 + side
        piece = lax.dynamic_slice_in_dim(gathered, at * subs, subs, 0)
        piece = piece.transpose(1, 0, 2).reshape(count, half).astype(jnp.float32)
        gain = lax.dynamic_slice_in_dim(norm_gain, at * half, half, 0)
        return (piece * scale * gain).astype(jnp.bfloat16)

    own = [normed(tok ^ part) for part in range(tok_size)]
    own = [own[0]] + [swap_tok(own[part], part) for part in range(1, tok_size)]
    other = [swap_core(part) for part in own]

    hiddens, halves = [], []
    for chunk in range(chunks):
        sums = gate_up(own, other, dense, chunk)
        terms = [sums[0]] + [swap_tok(sums[part], part) for part in range(1, tok_size)]
        total = functools.reduce(jnp.add, [term.astype(jnp.float32) for term in terms])
        gate_sum, up_sum = jnp.split(total, 2, axis=1)
        hiddens.append((jax.nn.silu(gate_sum) * up_sum).astype(jnp.bfloat16))

    mixed = jnp.zeros((count, width_blocks * edge), jnp.float32)
    for chunk in range(chunks):
        hidden = lax.all_gather(hiddens[chunk], "col")
        last = chunk == chunks - 1
        mixed = down(hidden, down_dense, mixed, chunk, jnp.bfloat16 if last else jnp.float32)
    return mixed

def spread_shares_kernel(gate_at, up_at, *refs, rows, shares, cols):
    (gate_ref, up_ref), (out_ref, mark) = refs[:2], refs[-2:]
    step = pl.program_id(0)
    leave(mark)

    @pl.loop(0, rows)
    def _(row):
        for share in range(shares):
            for col in range(cols):
                at = ((step * rows + row) * shares + share) * cols + col
                put(out_ref, row, 2 * share * cols + col, gate_ref, gate_at[at])
                put(out_ref, row, (2 * share + 1) * cols + col, up_ref, up_at[at])


def spread_shares(gate_at, up_at, gate, up, rows, shares, cols, after, chunk):
    edge = gate.shape[-1]
    steps = 4
    whole = pl.BlockSpec(gate.shape, lambda k, *_: (0, 0, 0, 0), pipeline_mode=pl.Buffered(1))
    out = jax.ShapeDtypeStruct((1, rows * edge, 2 * shares * cols * edge), gate.dtype)
    block = (1, out.shape[1] // steps, out.shape[2])
    return pl.pallas_call(
        functools.partial(spread_shares_kernel, rows=rows // steps, shares=shares, cols=cols),
        out_shape=[out, MARK],
        grid_spec=pltpu.PrefetchScalarGridSpec(
            num_scalar_prefetch=2,
            grid=(steps,),
            in_specs=[whole, whole] + [ANY_SPEC] * len(after),
            out_specs=[pl.BlockSpec(block, lambda k, *_: (0, k, 0)), MARK_SPEC],
        ),
        compiler_params=pltpu.CompilerParams(vmem_limit_bytes=54 * MIB),
        cost_estimate=pl.CostEstimate(
            flops=0, bytes_accessed=2 * (2 * gate.size + out.size), transcendentals=0
        ),
        name=f"spread_gate_up_{chunk}",
    )(gate_at, up_at, gate, up, *after)


def spread_panels_kernel(at_ref, values_ref, *refs, chunks, rows, cols):
    out_ref, mark = refs[-2:]
    panel = pl.program_id(0)
    leave(mark)
    for chunk in range(chunks):
        for row in range(rows):
            for col in range(cols):
                at = ((panel * chunks + chunk) * rows + row) * cols + col
                put(out_ref.at[pl.ds(chunk, 1)], row, col, values_ref, at_ref[at])


def spread_panels(at, values, chunks, rows, cols, after):
    count, _, edge, _ = values.shape
    out = jax.ShapeDtypeStruct((chunks, count * rows * edge, cols * edge), values.dtype)
    return pl.pallas_call(
        functools.partial(spread_panels_kernel, chunks=chunks, rows=rows, cols=cols),
        out_shape=[out, MARK],
        grid_spec=pltpu.PrefetchScalarGridSpec(
            num_scalar_prefetch=1,
            grid=(count,),
            in_specs=[
                pl.BlockSpec((1,) + values.shape[1:], lambda m, *_: (m, 0, 0, 0))
            ]
            + [ANY_SPEC] * len(after),
            out_specs=[
                pl.BlockSpec((chunks, rows * edge, cols * edge), lambda m, *_: (0, m, 0)),
                MARK_SPEC,
            ],
        ),
        compiler_params=pltpu.CompilerParams(vmem_limit_bytes=50 * MIB),
        cost_estimate=pl.CostEstimate(
            flops=0, bytes_accessed=2 * (values.size + out.size), transcendentals=0
        ),
        name="spread_down",
    )(at, values, *after)

def sum_squares_kernel(tokens, out):
    widened = tokens[...].astype(jnp.float32)
    out[...] = jnp.sum(widened * widened, axis=1)[None]


def sum_squares(tokens):
    return pl.pallas_call(
        sum_squares_kernel,
        out_shape=jax.ShapeDtypeStruct((1, tokens.shape[0]), jnp.float32),
        in_specs=[pl.BlockSpec(memory_space=pltpu.VMEM)],
        out_specs=pl.BlockSpec(memory_space=pltpu.VMEM),
        compiler_params=pltpu.CompilerParams(vmem_limit_bytes=4 * MIB),
        name="sum_squares",
    )(tokens)


def pack_kernel(*refs, parts):
    pieces, scale, gain, out = refs[:parts], refs[parts], refs[parts + 1], refs[-1]
    count = pieces[0].shape[0]
    for part in range(parts):
        rows = slice(part * count, (part + 1) * count)
        piece = pieces[part][...].astype(jnp.float32)
        out[rows] = (piece * scale[rows] * gain[...]).astype(out.dtype)


def pack(pieces, scale, gain, after):
    parts = len(pieces)
    count, width = pieces[0].shape
    return pl.pallas_call(
        functools.partial(pack_kernel, parts=parts),
        out_shape=jax.ShapeDtypeStruct((parts * count, width), pieces[0].dtype),
        in_specs=[pl.BlockSpec(memory_space=pltpu.VMEM)] * (parts + 2)
        + [pl.BlockSpec(memory_space=pl.ANY)] * len(after),
        out_specs=pl.BlockSpec(memory_space=pltpu.VMEM),
        compiler_params=pltpu.CompilerParams(vmem_limit_bytes=16 * MIB),
        cost_estimate=pl.CostEstimate(
            flops=0, bytes_accessed=4 * parts * count * width, transcendentals=0
        ),
        name="pack",
    )(*pieces, scale, gain, *after)


def halfway_kernel(kept_a, came_a, kept_b, came_b, *refs):
    out_a, out_b, mark = refs[-3:]
    leave(mark)
    for kept, came, out in ((kept_a, came_a, out_a), (kept_b, came_b, out_b)):
        out[...] = (kept[0].astype(jnp.float32) + came[0].astype(jnp.float32)).astype(out.dtype)


def halfway(kept_a, came_a, kept_b, came_b, after, chunk):
    _, count, width = kept_a.shape
    second = pl.BlockSpec((1, count, width), lambda i: (1, 0, 0))
    whole = pl.BlockSpec((count, width), lambda i: (0, 0))
    out = jax.ShapeDtypeStruct((count, width), kept_a.dtype)
    return pl.pallas_call(
        halfway_kernel,
        out_shape=[out, out, MARK],
        grid=(1,),
        in_specs=[second] * 4 + [ANY_SPEC] * len(after),
        out_specs=[whole, whole, MARK_SPEC],
        compiler_params=pltpu.CompilerParams(vmem_limit_bytes=8 * MIB),
        cost_estimate=pl.CostEstimate(
            flops=2 * count * width, bytes_accessed=12 * count * width, transcendentals=0
        ),
        name=f"halfway_{chunk}",
    )(kept_a, came_a, kept_b, came_b, *after)


def combine_kernel(*refs):
    terms, out, mark = refs[:6], refs[-2], refs[-1]
    leave(mark)
    count = out.shape[0] // 2
    width = out.shape[1]
    for i in range(2):
        kept, came, last = terms[3 * i:3 * i + 3]
        total = kept[0].astype(jnp.float32) + came[0].astype(jnp.float32)
        total += last[...].astype(jnp.float32)
        gate_sum, up_sum = total[:, :width], total[:, width:]
        hidden = gate_sum / (1.0 + jnp.exp(-gate_sum)) * up_sum
        out[i * count:(i + 1) * count] = hidden.astype(out.dtype)


def combine(kept_a, came_a, last_a, kept_b, came_b, last_b, after, chunk):
    count, width = last_a.shape
    first = pl.BlockSpec((1, count, width), lambda i: (0, 0, 0))
    whole = pl.BlockSpec((count, width), lambda i: (0, 0))
    return pl.pallas_call(
        combine_kernel,
        out_shape=[jax.ShapeDtypeStruct((2 * count, width // 2), last_a.dtype), MARK],
        grid=(1,),
        in_specs=[first, first, whole] * 2 + [ANY_SPEC] * len(after),
        out_specs=[pl.BlockSpec((2 * count, width // 2), lambda i: (0, 0)), MARK_SPEC],
        compiler_params=pltpu.CompilerParams(vmem_limit_bytes=10 * MIB),
        cost_estimate=pl.CostEstimate(
            flops=8 * count * width,
            bytes_accessed=14 * count * width,
            transcendentals=count * width // 2,
        ),
        name=f"combine_{chunk}",
    )(kept_a, came_a, last_a, kept_b, came_b, last_b, *after)


def panel_product_kernel(own, other, weight, *refs):
    kept_a, sent_a, kept_b, sent_b, mark = refs[-5:]
    leave(mark)
    half = own.shape[1]
    product = jnp.dot(own[...], weight[0, :half], preferred_element_type=jnp.float32)
    product += jnp.dot(other[...], weight[0, half:], preferred_element_type=jnp.float32)
    product = product.astype(kept_a.dtype)
    count = product.shape[0] // 2
    part = pl.program_id(0)
    for flip in range(2):

        @pl.when(part % 2 == flip)
        def _():
            (sent_a if flip else kept_a)[part // 2] = product[:count]

        @pl.when(part // 2 == flip)
        def _():
            (sent_b if flip else kept_b)[part % 2] = product[count:]


def panel_product(own, other, dense, after, chunk):
    count, half = own.shape
    _, depth, width = dense.shape
    tile = width // 4
    out = jax.ShapeDtypeStruct((2, count // 2, tile), own.dtype)
    return pl.pallas_call(
        panel_product_kernel,
        out_shape=[out] * 4 + [MARK],
        grid=(4,),
        in_specs=[pl.BlockSpec((count, half), lambda n: (0, 0))] * 2
        + [pl.BlockSpec((1, depth, tile), lambda n: (0, 0, n))]
        + [ANY_SPEC] * len(after),
        out_specs=[pl.BlockSpec(out.shape, lambda n: (0, 0, 0))] * 4 + [MARK_SPEC],
        compiler_params=pltpu.CompilerParams(vmem_limit_bytes=54 * MIB),
        cost_estimate=pl.CostEstimate(
            flops=2 * count * depth * width,
            bytes_accessed=2 * (depth * width + count * (depth + width)),
            transcendentals=0,
        ),
        name=f"gate_up_{chunk}",
    )(own, other, dense, *after)


def down_product_kernel(place, hidden, weight, *refs, added):
    before, outs, mark, held = refs[:added], refs[added:-2], refs[-2], refs[-1]
    leave(mark)
    panels, parts, count, depth = hidden.shape
    chip, flips = place[0], place[1]

    @pl.when(pl.program_id(0) == 0)
    def _():
        for panel in range(panels):
            columns = slice(panel * depth, (panel + 1) * depth)
            for part in range(parts):
                there = part ^ chip ^ (panel // 2)
                held[part * count:(part + 1) * count, columns] = hidden[panel, there]

    if len(outs) == 1:
        product = jnp.dot(held[...], weight[0], preferred_element_type=jnp.float32)
        for term in before:
            product += term[...]
        outs[0][...] = product
        return
    for step, out in enumerate(outs):
        rows = pl.ds(pl.multiple_of((flips ^ step) * count, count), count)
        product = jnp.dot(held[rows], weight[0], preferred_element_type=jnp.float32)
        for term in before:
            product += term[rows]
        out[...] = product.astype(out.dtype)


def down_product(place, hidden, dense, before, chunk, last):
    panels, parts, count, depth = hidden.shape
    _, total, width = dense.shape
    tile = width // 2
    tiles = pl.BlockSpec((parts * count, tile), lambda n, *_: (0, n))
    added = [] if before is None else [before]
    if last:
        out = [jax.ShapeDtypeStruct((count, width), hidden.dtype)] * parts
        out_tiles = [pl.BlockSpec((count, tile), lambda n, *_: (0, n))] * parts
    else:
        out, out_tiles = [jax.ShapeDtypeStruct((parts * count, width), jnp.float32)], [tiles]
    return pl.pallas_call(
        functools.partial(down_product_kernel, added=len(added)),
        out_shape=out + [MARK],
        grid_spec=pltpu.PrefetchScalarGridSpec(
            num_scalar_prefetch=1,
            grid=(width // tile,),
            in_specs=[
                pl.BlockSpec(hidden.shape, lambda n, *_: (0, 0, 0, 0)),
                pl.BlockSpec((1, total, tile), lambda n, *_: (chunk, 0, n)),
            ]
            + [tiles] * len(added),
            out_specs=out_tiles + [MARK_SPEC],
            scratch_shapes=[pltpu.VMEM((parts * count, total), hidden.dtype)],
        ),
        compiler_params=pltpu.CompilerParams(vmem_limit_bytes=50 * MIB),
        cost_estimate=pl.CostEstimate(
            flops=2 * parts * count * total * width,
            bytes_accessed=2 * total * (width + parts * count) + 8 * parts * count * width,
            transcendentals=0,
        ),
        name=f"down_{chunk}",
    )(place, hidden, dense, *added)


def by_columns(
    tokens,
    norm_gain,
    gate_block_entries,
    gate_block_places,
    up_block_entries,
    up_block_places,
    down_values,
    down_slots,
):
    edge = gate_block_entries.shape[-1]
    tok_size = lax.axis_size("tok")
    col_size = lax.axis_size("col")
    rows_per = MODEL_WIDTH // edge // tok_size
    cols_per = HIDDEN_UNITS // edge // col_size
    width_blocks = MODEL_WIDTH // edge // col_size
    share = cols_per // tok_size
    chunks = 2 if share % 2 == 0 else 1
    cols = share // chunks
    count, half = tokens.shape
    tok, col = lax.axis_index("tok"), lax.axis_index("col")
    chip, side = col // 2, col % 2
    parts = range(tok_size)

    def swap_tok(array, step):
        return lax.ppermute(array, "tok", [(i, i ^ step) for i in parts])

    def swap_chip(array, step):
        return lax.ppermute(array, "col", [(i, i ^ (2 * step)) for i in range(col_size)])

    def swap_core(array):
        return lax.ppermute(array, "col", [(i, i ^ 1) for i in range(col_size)])

    def to_users(array, part):
        pairs = []
        for i in parts:
            for j in range(col_size):
                user = (j // 2) * col_size + 2 * (i ^ part) + j % 2
                pairs.append((i * col_size + j, user))
        return lax.ppermute(array, ("tok", "col"), pairs)

    pieces = [to_users(tokens, part) for part in parts]
    k, r, p, q = jnp.meshgrid(
        jnp.arange(chunks), jnp.arange(rows_per), jnp.arange(tok_size), jnp.arange(cols),
        indexing="ij",
    )
    row = (r + side * (rows_per // 2)) % rows_per
    slots = (row * cols_per + (p ^ tok) * share + k * cols + q).reshape(-1).astype(jnp.int32)
    gate_at = lookup(gate_block_places[0], slots)
    up_at = lookup(up_block_places[0], slots)
    slots = tok * share * width_blocks + jnp.arange(share * width_blocks, dtype=jnp.int32)
    down_at = lookup(down_slots, slots).reshape(-1)
    gate_at, up_at = gate_at.reshape(chunks, -1), up_at.reshape(chunks, -1)

    def spread(chunk, after):
        return spread_shares(
            gate_at[chunk], up_at[chunk], gate_block_entries, up_block_entries,
            rows_per, tok_size, cols, after, chunk,
        )

    squares = sum_squares(tokens)
    squares += swap_core(squares)
    dense, mark = spread(0, [])
    squares += mark[:1, :1]
    squares += swap_chip(squares, 1)
    squares += swap_chip(squares, 2)
    squares = jnp.concatenate([squares, swap_tok(squares, 1)])
    squares = jnp.concatenate([squares, swap_tok(squares, 2)])

    gain = lax.dynamic_slice_in_dim(norm_gain, (tok * 2 + side) * half, half, 0)[None]
    scale = lax.rsqrt(squares / MODEL_WIDTH + EPSILON)
    scale = jnp.take(scale, jnp.arange(tok_size) ^ chip ^ tok, axis=0).reshape(-1, 1)
    own = pack(pieces, scale, gain, [])
    other = swap_core(own)

    place = jnp.stack([chip, chip ^ tok])
    hiddens = []
    *sums, mark = panel_product(own, other, dense, [], 0)
    if chunks > 1:
        dense, mark = spread(1, [mark])
    for chunk in range(chunks):
        kept_a, sent_a, kept_b, sent_b = sums
        came_a, came_b = swap_tok(sent_a, 1), swap_tok(sent_b, 2)
        last_a, last_b, mark = halfway(kept_a, came_a, kept_b, came_b, [mark], chunk)
        last_a, last_b = swap_tok(last_a, 2), swap_tok(last_b, 1)
        if chunk + 1 < chunks:
            *sums, mark = panel_product(own, other, dense, [mark], chunk + 1)
        hidden, mark = combine(kept_a, came_a, last_a, kept_b, came_b, last_b, [mark], chunk)
        if chunk + 2 < chunks:
            dense, mark = spread(chunk + 2, [mark])
        elif chunk == max(chunks - 2, 0):
            down_dense, mark = spread_panels(
                down_at, down_values, chunks, cols, width_blocks, [mark]
            )
        hiddens.append(lax.all_gather(hidden.reshape(tok_size, count, -1), "col"))

    mixed = [None]
    for chunk in range(chunks):
        last = chunk == chunks - 1
        *mixed, _ = down_product(place, hiddens[chunk], down_dense, mixed[0], chunk, last)

    total = mixed[0].astype(jnp.float32)
    for step in parts[1:]:
        total += swap_tok(mixed[step], step).astype(jnp.float32)
    return total.astype(jnp.bfloat16)


def shards(*arrays):
    tok_size = lax.axis_size("tok")
    col_size = lax.axis_size("col")
    blocks = HIDDEN_UNITS // arrays[2].shape[-1]
    even = blocks % (col_size * tok_size) == 0 and col_size == 2 * tok_size == 8
    return (by_columns if even else by_tokens)(*arrays)


def solution(mesh):
    return jax.shard_map(
        shards,
        mesh=mesh,
        in_specs=(
            P("tok", "col"),
            P(),
            P("tok", "col", None, None),
            P("tok", "col"),
            P("tok", "col", None, None),
            P("tok", "col"),
            P(None, "col", None, None),
            P(None, "col"),
        ),
        out_specs=P("tok", "col"),
        check_vma=False,
    )
```

```python
import functools

import jax
import jax.numpy as jnp
from jax import lax
from jax.experimental import pallas as pl
from jax.experimental.pallas import tpu as pltpu
from jax.sharding import PartitionSpec as P

MODEL_WIDTH = 8192
HIDDEN_UNITS = 24576

EPSILON = 1e-05
MIB = 1 << 20
MARK = jax.ShapeDtypeStruct((8, 128), jnp.float32)
MARK_SPEC = pl.BlockSpec(MARK.shape, lambda *_: (0, 0))
ANY_SPEC = pl.BlockSpec(memory_space=pl.ANY)


def leave(mark):
    mark[...] = jnp.zeros_like(mark)


def lookup(places, slots):
    hit = places[..., None, :] == slots[:, None]
    entry = jnp.arange(places.shape[-1], dtype=jnp.int32)
    return jnp.max(jnp.where(hit, entry, -1), axis=-1)


def put(out_ref, row, col, source_ref, entry):
    edge = source_ref.shape[-1]
    block = source_ref[0, jnp.maximum(entry, 0)]
    block = jnp.where(entry >= 0, block, jnp.zeros_like(block))
    out_ref[0, pl.ds(pl.multiple_of(row * edge, edge), edge), col * edge:(col + 1) * edge] = block


def spread_gate_up_kernel(gate_at, up_at, gate_ref, up_ref, out_ref, *, rows, cols):
    chunk = pl.program_id(0)

    @pl.loop(0, rows)
    def _(row):
        for col in range(cols):
            at = (chunk * rows + row) * cols + col
            put(out_ref, row, col, gate_ref, gate_at[at])
            put(out_ref, row, cols + col, up_ref, up_at[at])


def spread_gate_up(gate_at, up_at, gate, up, chunks, rows, cols):
    edge = gate.shape[-1]
    whole = pl.BlockSpec(gate.shape, lambda k, *_: (0, 0, 0, 0), pipeline_mode=pl.Buffered(1))
    out = jax.ShapeDtypeStruct((chunks, rows * edge, 2 * cols * edge), gate.dtype)
    return pl.pallas_call(
        functools.partial(spread_gate_up_kernel, rows=rows, cols=cols),
        out_shape=out,
        grid_spec=pltpu.PrefetchScalarGridSpec(
            num_scalar_prefetch=2,
            grid=(chunks,),
            in_specs=[whole, whole],
            out_specs=pl.BlockSpec((1,) + out.shape[1:], lambda k, *_: (k, 0, 0)),
        ),
        compiler_params=pltpu.CompilerParams(vmem_limit_bytes=48 * MIB),
        cost_estimate=pl.CostEstimate(
            flops=0, bytes_accessed=2 * (2 * gate.size + out.size), transcendentals=0
        ),
        name="spread_gate_up",
    )(gate_at, up_at, gate, up)


def spread_down_kernel(at_ref, values_ref, out_ref, *, rows, cols):
    panel, chunk = pl.program_id(0), pl.program_id(1)
    base = (panel * pl.num_programs(1) + chunk) * rows * cols

    @pl.loop(0, rows)
    def _(row):
        for col in range(cols):
            put(out_ref.at[0], row, col, values_ref, at_ref[base + row * cols + col])


def spread_down(at, values, chunks, rows, cols):
    panels, _, edge, _ = values.shape
    out = jax.ShapeDtypeStruct((chunks, panels, rows * edge, cols * edge), values.dtype)
    return pl.pallas_call(
        functools.partial(spread_down_kernel, rows=rows, cols=cols),
        out_shape=out,
        grid_spec=pltpu.PrefetchScalarGridSpec(
            num_scalar_prefetch=1,
            grid=(panels, chunks),
            in_specs=[pl.BlockSpec((1,) + values.shape[1:], lambda g, k, *_: (g, 0, 0, 0))],
            out_specs=pl.BlockSpec((1, 1) + out.shape[2:], lambda g, k, *_: (k, g, 0, 0)),
        ),
        compiler_params=pltpu.CompilerParams(vmem_limit_bytes=48 * MIB),
        cost_estimate=pl.CostEstimate(
            flops=0, bytes_accessed=2 * (values.size + out.size), transcendentals=0
        ),
        name="spread_down",
    )(at, values)


def gate_up_kernel(*refs, parts):
    own, other = refs[:parts], refs[parts:2 * parts]
    weight = refs[2 * parts]
    outs, held = refs[2 * parts + 1:3 * parts + 1], refs[-1]
    count, half = own[0].shape

    @pl.when(pl.program_id(0) == 0)
    def _():
        for part in range(parts):
            rows = slice(part * count, (part + 1) * count)
            held[rows, :half] = own[part][...]
            held[rows, half:] = other[part][...]

    product = jnp.dot(held[...], weight[0], preferred_element_type=jnp.float32)
    for part in range(parts):
        outs[part][...] = product[part * count:(part + 1) * count].astype(outs[part].dtype)


def gate_up(own, other, dense, chunk):
    parts = len(own)
    count, half = own[0].shape
    _, depth, width = dense.shape
    tile = 256
    out = jax.ShapeDtypeStruct((count, width), own[0].dtype)
    return pl.pallas_call(
        functools.partial(gate_up_kernel, parts=parts),
        out_shape=[out] * parts,
        grid=(width // tile,),
        in_specs=[pl.BlockSpec((count, half), lambda n: (0, 0))] * (2 * parts)
        + [pl.BlockSpec((1, depth, tile), lambda n: (chunk, 0, n))],
        out_specs=[pl.BlockSpec((count, tile), lambda n: (0, n))] * parts,
        scratch_shapes=[pltpu.VMEM((parts * count, 2 * half), own[0].dtype)],
        compiler_params=pltpu.CompilerParams(vmem_limit_bytes=32 * MIB),
        cost_estimate=pl.CostEstimate(
            flops=2 * parts * count * depth * width,
            bytes_accessed=2 * (depth * width + parts * count * (depth + width)),
            transcendentals=0,
        ),
        name=f"gate_up_{chunk}",
    )(*own, *other, dense)


def down_kernel(hidden_ref, weight_ref, before_ref, out_ref, total):
    panel = pl.program_id(0)

    @pl.when(panel == 0)
    def _():
        total[...] = before_ref[...]

    total[...] += jnp.dot(hidden_ref[0], weight_ref[0, 0], preferred_element_type=jnp.float32)

    @pl.when(panel == pl.num_programs(0) - 1)
    def _():
        out_ref[...] = total[...].astype(out_ref.dtype)


def down(hidden, dense, before, chunk, dtype):
    panels, count, depth = hidden.shape
    width = dense.shape[-1]
    return pl.pallas_call(
        down_kernel,
        out_shape=jax.ShapeDtypeStruct((count, width), dtype),
        grid=(panels,),
        in_specs=[
            pl.BlockSpec((1, count, depth), lambda g: (g, 0, 0)),
            pl.BlockSpec((1, 1, depth, width), lambda g: (chunk, g, 0, 0)),
            pl.BlockSpec((count, width), lambda g: (0, 0)),
        ],
        out_specs=pl.BlockSpec((count, width), lambda g: (0, 0)),
        scratch_shapes=[pltpu.VMEM((count, width), jnp.float32)],
        compiler_params=pltpu.CompilerParams(vmem_limit_bytes=32 * MIB),
        cost_estimate=pl.CostEstimate(
            flops=2 * panels * count * depth * width,
            bytes_accessed=2 * panels * depth * (width + count) + 6 * count * width,
            transcendentals=0,
        ),
        name=f"down_{chunk}",
    )(hidden, dense, before)


def by_tokens(
    tokens,
    norm_gain,
    gate_block_entries,
    gate_block_places,
    up_block_entries,
    up_block_places,
    down_values,
    down_slots,
):
    edge = gate_block_entries.shape[-1]
    tok_size = lax.axis_size("tok")
    col_size = lax.axis_size("col")
    rows_per = MODEL_WIDTH // edge // tok_size
    cols_per = HIDDEN_UNITS // edge // col_size
    width_blocks = MODEL_WIDTH // edge // col_size
    chunks = 4 if cols_per % 4 == 0 else 1
    chunk_cols = cols_per // chunks
    count, features = tokens.shape
    half = MODEL_WIDTH // tok_size // 2
    tok, col = lax.axis_index("tok"), lax.axis_index("col")
    side = col % 2

    def swap_tok(array, step):
        return lax.ppermute(array, "tok", [(i, i ^ step) for i in range(tok_size)])

    def swap_core(array):
        return lax.ppermute(array, "col", [(i, i ^ 1) for i in range(col_size)])

    k, r, q = jnp.meshgrid(
        jnp.arange(chunks), jnp.arange(rows_per), jnp.arange(chunk_cols), indexing="ij"
    )
    row = (r + side * (rows_per // 2)) % rows_per
    slots = (row * cols_per + k * chunk_cols + q).reshape(-1).astype(jnp.int32)
    gate_at = lookup(gate_block_places[0], slots)
    up_at = lookup(up_block_places[0], slots)
    down_at = lookup(down_slots, jnp.arange(cols_per * width_blocks, dtype=jnp.int32)).reshape(-1)

    gathered = lax.all_gather(tokens, "col")
    dense = spread_gate_up(
        gate_at, up_at, gate_block_entries, up_block_entries, chunks, rows_per, chunk_cols
    )
    down_dense = spread_down(down_at, down_values, chunks, chunk_cols, width_blocks)

    widened = gathered.astype(jnp.float32)
    mean_square = jnp.mean(widened * widened, axis=(0, 2))[:, None]
    scale = lax.rsqrt(mean_square + EPSILON)
    subs = half // features

    def normed(panel):
        at = panel * 2 + side
        piece = lax.dynamic_slice_in_dim(gathered, at * subs, subs, 0)
        piece = piece.transpose(1, 0, 2).reshape(count, half).astype(jnp.float32)
        gain = lax.dynamic_slice_in_dim(norm_gain, at * half, half, 0)
        return (piece * scale * gain).astype(jnp.bfloat16)

    own = [normed(tok ^ part) for part in range(tok_size)]
    own = [own[0]] + [swap_tok(own[part], part) for part in range(1, tok_size)]
    other = [swap_core(part) for part in own]

    hiddens, halves = [], []
    for chunk in range(chunks):
        sums = gate_up(own, other, dense, chunk)
        terms = [sums[0]] + [swap_tok(sums[part], part) for part in range(1, tok_size)]
        total = functools.reduce(jnp.add, [term.astype(jnp.float32) for term in terms])
        gate_sum, up_sum = jnp.split(total, 2, axis=1)
        hiddens.append((jax.nn.silu(gate_sum) * up_sum).astype(jnp.bfloat16))

    mixed = jnp.zeros((count, width_blocks * edge), jnp.float32)
    for chunk in range(chunks):
        hidden = lax.all_gather(hiddens[chunk], "col")
        last = chunk == chunks - 1
        mixed = down(hidden, down_dense, mixed, chunk, jnp.bfloat16 if last else jnp.float32)
    return mixed

def spread_shares_kernel(gate_at, up_at, *refs, rows, shares, cols):
    (gate_ref, up_ref), (out_ref, mark) = refs[:2], refs[-2:]
    step = pl.program_id(0)
    leave(mark)

    @pl.loop(0, rows)
    def _(row):
        for share in range(shares):
            for col in range(cols):
                at = ((step * rows + row) * shares + share) * cols + col
                put(out_ref, row, 2 * share * cols + col, gate_ref, gate_at[at])
                put(out_ref, row, (2 * share + 1) * cols + col, up_ref, up_at[at])


def spread_shares(gate_at, up_at, gate, up, rows, shares, cols, after, chunk):
    edge = gate.shape[-1]
    steps = 4
    whole = pl.BlockSpec(gate.shape, lambda k, *_: (0, 0, 0, 0), pipeline_mode=pl.Buffered(1))
    out = jax.ShapeDtypeStruct((1, rows * edge, 2 * shares * cols * edge), gate.dtype)
    block = (1, out.shape[1] // steps, out.shape[2])
    return pl.pallas_call(
        functools.partial(spread_shares_kernel, rows=rows // steps, shares=shares, cols=cols),
        out_shape=[out, MARK],
        grid_spec=pltpu.PrefetchScalarGridSpec(
            num_scalar_prefetch=2,
            grid=(steps,),
            in_specs=[whole, whole] + [ANY_SPEC] * len(after),
            out_specs=[pl.BlockSpec(block, lambda k, *_: (0, k, 0)), MARK_SPEC],
        ),
        compiler_params=pltpu.CompilerParams(vmem_limit_bytes=54 * MIB),
        cost_estimate=pl.CostEstimate(
            flops=0, bytes_accessed=2 * (2 * gate.size + out.size), transcendentals=0
        ),
        name=f"spread_gate_up_{chunk}",
    )(gate_at, up_at, gate, up, *after)


def spread_panels_kernel(at_ref, values_ref, *refs, chunks, rows, cols):
    out_ref, mark = refs[-2:]
    panel = pl.program_id(0)
    leave(mark)
    for chunk in range(chunks):
        for row in range(rows):
            for col in range(cols):
                at = ((panel * chunks + chunk) * rows + row) * cols + col
                put(out_ref.at[pl.ds(chunk, 1)], row, col, values_ref, at_ref[at])


def spread_panels(at, values, chunks, rows, cols, after):
    count, _, edge, _ = values.shape
    out = jax.ShapeDtypeStruct((chunks, count * rows * edge, cols * edge), values.dtype)
    return pl.pallas_call(
        functools.partial(spread_panels_kernel, chunks=chunks, rows=rows, cols=cols),
        out_shape=[out, MARK],
        grid_spec=pltpu.PrefetchScalarGridSpec(
            num_scalar_prefetch=1,
            grid=(count,),
            in_specs=[
                pl.BlockSpec((1,) + values.shape[1:], lambda m, *_: (m, 0, 0, 0))
            ]
            + [ANY_SPEC] * len(after),
            out_specs=[
                pl.BlockSpec((chunks, rows * edge, cols * edge), lambda m, *_: (0, m, 0)),
                MARK_SPEC,
            ],
        ),
        compiler_params=pltpu.CompilerParams(vmem_limit_bytes=50 * MIB),
        cost_estimate=pl.CostEstimate(
            flops=0, bytes_accessed=2 * (values.size + out.size), transcendentals=0
        ),
        name="spread_down",
    )(at, values, *after)

def sum_squares_kernel(tokens, out):
    widened = tokens[...].astype(jnp.float32)
    out[...] = jnp.sum(widened * widened, axis=1)[None]


def sum_squares(tokens):
    return pl.pallas_call(
        sum_squares_kernel,
        out_shape=jax.ShapeDtypeStruct((1, tokens.shape[0]), jnp.float32),
        in_specs=[pl.BlockSpec(memory_space=pltpu.VMEM)],
        out_specs=pl.BlockSpec(memory_space=pltpu.VMEM),
        compiler_params=pltpu.CompilerParams(vmem_limit_bytes=4 * MIB),
        name="sum_squares",
    )(tokens)


def pack_kernel(*refs, parts):
    count = refs[0].shape[0]
    for part in range(parts):
        refs[-1][part * count:(part + 1) * count] = refs[part][...]


def pack(pieces, after):
    parts = len(pieces)
    count, width = pieces[0].shape
    return pl.pallas_call(
        functools.partial(pack_kernel, parts=parts),
        out_shape=jax.ShapeDtypeStruct((parts * count, width), pieces[0].dtype),
        in_specs=[pl.BlockSpec(memory_space=pltpu.VMEM)] * parts + [ANY_SPEC] * len(after),
        out_specs=pl.BlockSpec(memory_space=pltpu.VMEM),
        compiler_params=pltpu.CompilerParams(vmem_limit_bytes=16 * MIB),
        cost_estimate=pl.CostEstimate(
            flops=0, bytes_accessed=4 * parts * count * width, transcendentals=0
        ),
        name="pack",
    )(*pieces, *after)


def pair_kernel(*refs, steps):
    out = refs[-1]
    count = out.shape[1] // 4
    for i, step in enumerate(steps):
        for part in range(4):
            there = slice((part ^ step) * count, ((part ^ step) + 1) * count)
            rows = refs[i][there]
            if i == 1 and steps == (2, 3):
                rows += refs[2][there]
            out[i, part * count:(part + 1) * count] = rows


def pair(pieces, steps, after):
    return pl.pallas_call(
        functools.partial(pair_kernel, steps=steps),
        out_shape=jax.ShapeDtypeStruct((2,) + pieces[0].shape, pieces[0].dtype),
        in_specs=[pl.BlockSpec(memory_space=pltpu.VMEM)] * len(pieces) + [ANY_SPEC],
        out_specs=pl.BlockSpec(memory_space=pltpu.VMEM),
        compiler_params=pltpu.CompilerParams(vmem_limit_bytes=16 * MIB),
        cost_estimate=pl.CostEstimate(
            flops=0, bytes_accessed=4 * len(pieces) * pieces[0].size, transcendentals=0
        ),
        name="pair",
    )(*pieces, after)


def halfway_kernel(kept_a, came_a, kept_b, came_b, *refs):
    out_a, out_b, mark = refs[-3:]
    leave(mark)
    for kept, came, out in ((kept_a, came_a, out_a), (kept_b, came_b, out_b)):
        out[...] = (kept[0].astype(jnp.float32) + came[0].astype(jnp.float32)).astype(out.dtype)


def halfway(kept_a, came_a, kept_b, came_b, after, chunk):
    _, count, width = kept_a.shape
    second = pl.BlockSpec((1, count, width), lambda i: (1, 0, 0))
    whole = pl.BlockSpec((count, width), lambda i: (0, 0))
    out = jax.ShapeDtypeStruct((count, width), kept_a.dtype)
    return pl.pallas_call(
        halfway_kernel,
        out_shape=[out, out, MARK],
        grid=(1,),
        in_specs=[second] * 4 + [ANY_SPEC] * len(after),
        out_specs=[whole, whole, MARK_SPEC],
        compiler_params=pltpu.CompilerParams(vmem_limit_bytes=8 * MIB),
        cost_estimate=pl.CostEstimate(
            flops=2 * count * width, bytes_accessed=12 * count * width, transcendentals=0
        ),
        name=f"halfway_{chunk}",
    )(kept_a, came_a, kept_b, came_b, *after)


def combine_kernel(*refs):
    terms, out, mark = refs[:6], refs[-2], refs[-1]
    leave(mark)
    count = out.shape[0] // 2
    width = out.shape[1]
    for i in range(2):
        kept, came, last = terms[3 * i:3 * i + 3]
        total = kept[0].astype(jnp.float32) + came[0].astype(jnp.float32)
        total += last[...].astype(jnp.float32)
        gate_sum, up_sum = total[:, :width], total[:, width:]
        hidden = gate_sum / (1.0 + jnp.exp(-gate_sum)) * up_sum
        out[i * count:(i + 1) * count] = hidden.astype(out.dtype)


def combine(kept_a, came_a, last_a, kept_b, came_b, last_b, after, chunk):
    count, width = last_a.shape
    first = pl.BlockSpec((1, count, width), lambda i: (0, 0, 0))
    whole = pl.BlockSpec((count, width), lambda i: (0, 0))
    return pl.pallas_call(
        combine_kernel,
        out_shape=[jax.ShapeDtypeStruct((2 * count, width // 2), last_a.dtype), MARK],
        grid=(1,),
        in_specs=[first, first, whole] * 2 + [ANY_SPEC] * len(after),
        out_specs=[pl.BlockSpec((2 * count, width // 2), lambda i: (0, 0)), MARK_SPEC],
        compiler_params=pltpu.CompilerParams(vmem_limit_bytes=10 * MIB),
        cost_estimate=pl.CostEstimate(
            flops=8 * count * width,
            bytes_accessed=14 * count * width,
            transcendentals=count * width // 2,
        ),
        name=f"combine_{chunk}",
    )(kept_a, came_a, last_a, kept_b, came_b, last_b, *after)


def panel_product_kernel(own, other, weight, *refs):
    kept_a, sent_a, kept_b, sent_b, mark = refs[-5:]
    leave(mark)
    half = own.shape[1]
    product = jnp.dot(own[...], weight[0, :half], preferred_element_type=jnp.float32)
    product += jnp.dot(other[...], weight[0, half:], preferred_element_type=jnp.float32)
    product = product.astype(kept_a.dtype)
    count = product.shape[0] // 2
    part = pl.program_id(0)
    for flip in range(2):

        @pl.when(part % 2 == flip)
        def _():
            (sent_a if flip else kept_a)[0] = product[:count]

        @pl.when(part // 2 == flip)
        def _():
            (sent_b if flip else kept_b)[0] = product[count:]


def panel_product(own, other, dense, after, chunk):
    count, half = own.shape
    _, depth, width = dense.shape
    tile = width // 4
    out = jax.ShapeDtypeStruct((2, count // 2, tile), own.dtype)
    return pl.pallas_call(
        panel_product_kernel,
        out_shape=[out] * 4 + [MARK],
        grid=(4,),
        in_specs=[pl.BlockSpec((count, half), lambda n: (0, 0))] * 2
        + [pl.BlockSpec((1, depth, tile), lambda n: (0, 0, n))]
        + [ANY_SPEC] * len(after),
        out_specs=[
            pl.BlockSpec((1,) + out.shape[1:], lambda n: (n // 2, 0, 0)),
            pl.BlockSpec((1,) + out.shape[1:], lambda n: (n // 2, 0, 0)),
            pl.BlockSpec((1,) + out.shape[1:], lambda n: (jnp.minimum(n, 1), 0, 0)),
            pl.BlockSpec((1,) + out.shape[1:], lambda n: (jnp.maximum(n - 2, 0), 0, 0)),
            MARK_SPEC,
        ],
        compiler_params=pltpu.CompilerParams(vmem_limit_bytes=54 * MIB),
        cost_estimate=pl.CostEstimate(
            flops=2 * count * depth * width,
            bytes_accessed=2 * (depth * width + count * (depth + width)),
            transcendentals=0,
        ),
        name=f"gate_up_{chunk}",
    )(own, other, dense, *after)


def down_product_kernel(place, hidden, weight, *refs, added):
    before, outs, mark, held = refs[:added], refs[added:-2], refs[-2], refs[-1]
    leave(mark)
    panels, parts, count, depth = hidden.shape
    chip, flips = place[0], place[1]

    @pl.when(pl.program_id(0) == 0)
    def _():
        for panel in range(panels):
            columns = slice(panel * depth, (panel + 1) * depth)
            for part in range(parts):
                there = part ^ chip ^ (panel // 2)
                held[part * count:(part + 1) * count, columns] = hidden[panel, there]

    if len(outs) == 1:
        product = jnp.dot(held[...], weight[0], preferred_element_type=jnp.float32)
        for term in before:
            product += term[...]
        outs[0][...] = product
        return
    for step, out in enumerate(outs):
        rows = pl.ds(pl.multiple_of((flips ^ step) * count, count), count)
        product = jnp.dot(held[rows], weight[0], preferred_element_type=jnp.float32)
        for term in before:
            product += term[rows]
        out[...] = product.astype(out.dtype)


def down_product(place, hidden, dense, before, chunk, last):
    panels, parts, count, depth = hidden.shape
    _, total, width = dense.shape
    tile = width // 2
    tiles = pl.BlockSpec((parts * count, tile), lambda n, *_: (0, n))
    added = [] if before is None else [before]
    if last:
        out = [jax.ShapeDtypeStruct((count, width), hidden.dtype)] * parts
        out_tiles = [pl.BlockSpec((count, tile), lambda n, *_: (0, n))] * parts
    else:
        out, out_tiles = [jax.ShapeDtypeStruct((parts * count, width), jnp.float32)], [tiles]
    return pl.pallas_call(
        functools.partial(down_product_kernel, added=len(added)),
        out_shape=out + [MARK],
        grid_spec=pltpu.PrefetchScalarGridSpec(
            num_scalar_prefetch=1,
            grid=(width // tile,),
            in_specs=[
                pl.BlockSpec(hidden.shape, lambda n, *_: (0, 0, 0, 0)),
                pl.BlockSpec((1, total, tile), lambda n, *_: (chunk, 0, n)),
            ]
            + [tiles] * len(added),
            out_specs=out_tiles + [MARK_SPEC],
            scratch_shapes=[pltpu.VMEM((parts * count, total), hidden.dtype)],
        ),
        compiler_params=pltpu.CompilerParams(vmem_limit_bytes=42 * MIB),
        cost_estimate=pl.CostEstimate(
            flops=2 * parts * count * total * width,
            bytes_accessed=2 * total * (width + parts * count) + 8 * parts * count * width,
            transcendentals=0,
        ),
        name=f"down_{chunk}",
    )(place, hidden, dense, *added)


def down_pair_kernel(place, own, other, *refs):
    weights, before, outs, mark = refs[:4], refs[4], refs[5:-1], refs[-1]
    leave(mark)
    count = before.shape[0] // len(outs)
    for step, out in enumerate(outs):
        at = 0 if len(outs) == 1 else (place[1] ^ step) * count
        rows = pl.ds(pl.multiple_of(at, count), count)
        total = before[rows]
        for i in range(2):
            for j, side in enumerate((own, other)):
                total += jnp.dot(
                    side[i, rows], weights[2 * i + j][0, 0], preferred_element_type=jnp.float32
                )
        out[...] = total.astype(out.dtype)


def down_pair(place, own, other, steps, dense, before, chunk, last):
    _, count, depth = own.shape
    width = dense.shape[-1]
    dense = dense.reshape(dense.shape[0], -1, depth, width)
    tile = width // 2
    tiles = pl.BlockSpec((count, tile), lambda n, *_: (0, n))
    whole = pl.BlockSpec(own.shape, lambda n, *_: (0, 0, 0))
    weights = []
    for step in steps:
        for flip in range(2):

            def at(n, place, step=step, flip=flip):
                return chunk, 2 * (place[0] ^ step) + (place[2] ^ flip), 0, n

            weights.append(pl.BlockSpec((1, 1, depth, tile), at))
    out, out_tiles = [jax.ShapeDtypeStruct((count, width), jnp.float32)], [tiles]
    if last:
        out = [jax.ShapeDtypeStruct((count // 4, width), own.dtype)] * 4
        out_tiles = [pl.BlockSpec((count // 4, tile), lambda n, *_: (0, n))] * 4
    return pl.pallas_call(
        down_pair_kernel,
        out_shape=out + [MARK],
        grid_spec=pltpu.PrefetchScalarGridSpec(
            num_scalar_prefetch=1,
            grid=(width // tile,),
            in_specs=[whole, whole] + weights + [tiles],
            out_specs=out_tiles + [MARK_SPEC],
        ),
        compiler_params=pltpu.CompilerParams(vmem_limit_bytes=42 * MIB),
        cost_estimate=pl.CostEstimate(
            flops=8 * count * depth * width,
            bytes_accessed=8 * depth * (width + count) + 8 * count * width,
            transcendentals=0,
        ),
        name=f"down_{chunk}_{steps[0]}",
    )(place, own, other, *[dense] * 4, before)


def by_columns(
    tokens,
    norm_gain,
    gate_block_entries,
    gate_block_places,
    up_block_entries,
    up_block_places,
    down_values,
    down_slots,
):
    edge = gate_block_entries.shape[-1]
    tok_size = lax.axis_size("tok")
    col_size = lax.axis_size("col")
    rows_per = MODEL_WIDTH // edge // tok_size
    cols_per = HIDDEN_UNITS // edge // col_size
    width_blocks = MODEL_WIDTH // edge // col_size
    share = cols_per // tok_size
    chunks = 2
    cols = share // chunks
    count, half = tokens.shape
    tok, col = lax.axis_index("tok"), lax.axis_index("col")
    chip, side = col // 2, col % 2
    parts = range(tok_size)

    def swap_tok(array, step):
        return lax.ppermute(array, "tok", [(i, i ^ step) for i in parts])

    def swap_chip(array, step):
        return lax.ppermute(array, "col", [(i, i ^ (2 * step)) for i in range(col_size)])

    def swap_core(array):
        return lax.ppermute(array, "col", [(i, i ^ 1) for i in range(col_size)])

    def to_users(array, part):
        pairs = []
        for i in parts:
            for j in range(col_size):
                user = (j // 2) * col_size + 2 * (i ^ part) + j % 2
                pairs.append((i * col_size + j, user))
        return lax.ppermute(array, ("tok", "col"), pairs)

    squares = sum_squares(tokens)
    squares += swap_core(squares)
    squares += functools.reduce(jnp.add, [swap_chip(squares, step) for step in parts[1:]])
    scale = lax.rsqrt(squares.reshape(-1, 1) / MODEL_WIDTH + EPSILON)
    gain = lax.dynamic_slice_in_dim(norm_gain, col * half, half, 0)
    normed = (tokens.astype(jnp.float32) * scale * gain).astype(jnp.bfloat16)
    pieces = [to_users(normed, part) for part in parts]

    k, r, p, q = jnp.meshgrid(
        jnp.arange(chunks), jnp.arange(rows_per), jnp.arange(tok_size), jnp.arange(cols),
        indexing="ij",
    )
    row = (r + side * (rows_per // 2)) % rows_per
    slots = (row * cols_per + (p ^ tok) * share + k * cols + q).reshape(-1).astype(jnp.int32)
    gate_at = lookup(gate_block_places[0], slots)
    up_at = lookup(up_block_places[0], slots)
    slots = tok * share * width_blocks + jnp.arange(share * width_blocks, dtype=jnp.int32)
    down_at = lookup(down_slots, slots).reshape(-1)
    gate_at, up_at = gate_at.reshape(chunks, -1), up_at.reshape(chunks, -1)

    def spread(chunk, after):
        return spread_shares(
            gate_at[chunk], up_at[chunk], gate_block_entries, up_block_entries,
            rows_per, tok_size, cols, after, chunk,
        )

    dense, mark = spread(0, [])
    own = pack(pieces, [mark])
    other = swap_core(own)

    place = jnp.stack([chip, chip ^ tok, side])
    mixed = [None]
    gathered = []
    *sums, mark = panel_product(own, other, dense, [], 0)
    if chunks > 1:
        dense, mark = spread(1, [mark])
    for chunk in range(chunks):
        kept_a, sent_a, kept_b, sent_b = sums
        came_a, came_b = swap_tok(sent_a, 1), swap_tok(sent_b, 2)
        last_a, last_b, mark = halfway(kept_a, came_a, kept_b, came_b, [mark], chunk)
        last_a, last_b = swap_tok(last_a, 2), swap_tok(last_b, 1)
        if chunk + 1 < chunks:
            *sums, mark = panel_product(own, other, dense, [mark], chunk + 1)
        hidden, mark = combine(kept_a, came_a, last_a, kept_b, came_b, last_b, [mark], chunk)
        if chunk + 2 < chunks:
            dense, mark = spread(chunk + 2, [mark])
        elif chunk == max(chunks - 2, 0):
            down_dense, mark = spread_panels(
                down_at, down_values, chunks, cols, width_blocks, [mark]
            )
        if chunk + 1 < chunks:
            gathered.append(lax.all_gather(hidden.reshape(tok_size, count, -1), "col"))

    far = swap_chip(hidden, 2)
    near = swap_chip(hidden, 1)
    inner = lax.ppermute(hidden, "col", [(i, i ^ 6) for i in range(2, 6)])
    ends = lax.ppermute(far, "col", [(i, i ^ 2) for i in range(2, 6)])
    for chunk in range(chunks - 1):
        *mixed, mark = down_product(place, gathered[chunk], down_dense, mixed[0], chunk, False)
    for steps, pieces in (((0, 1), [hidden, near]), ((2, 3), [far, inner, ends])):
        held = pair(pieces, steps, mark)
        *mixed, mark = down_pair(
            place, held, swap_core(held), steps, down_dense, mixed[0], chunks - 1, steps[0] == 2
        )

    total = mixed[0].astype(jnp.float32)
    for step in parts[1:]:
        total += swap_tok(mixed[step], step).astype(jnp.float32)
    return total.astype(jnp.bfloat16)


def shards(*arrays):
    tok_size = lax.axis_size("tok")
    col_size = lax.axis_size("col")
    blocks = HIDDEN_UNITS // arrays[2].shape[-1]
    even = blocks % (2 * col_size * tok_size) == 0 and col_size == 2 * tok_size == 8
    return (by_columns if even else by_tokens)(*arrays)


def solution(mesh):
    return jax.shard_map(
        shards,
        mesh=mesh,
        in_specs=(
            P("tok", "col"),
            P(),
            P("tok", "col", None, None),
            P("tok", "col"),
            P("tok", "col", None, None),
            P("tok", "col"),
            P(None, "col", None, None),
            P(None, "col"),
        ),
        out_specs=P("tok", "col"),
        check_vma=False,
    )
```

```python
import functools

import jax
import jax.numpy as jnp
from jax import lax
from jax.experimental import pallas as pl
from jax.experimental.pallas import tpu as pltpu
from jax.sharding import PartitionSpec as P

MODEL_WIDTH = 8192
HIDDEN_UNITS = 24576

EPSILON = 1e-05
MIB = 1 << 20
MARK = jax.ShapeDtypeStruct((8, 128), jnp.float32)
MARK_SPEC = pl.BlockSpec(MARK.shape, lambda *_: (0, 0))
ANY_SPEC = pl.BlockSpec(memory_space=pl.ANY)


def leave(mark):
    mark[...] = jnp.zeros_like(mark)


def lookup(places, slots):
    hit = places[..., None, :] == slots[:, None]
    entry = jnp.arange(places.shape[-1], dtype=jnp.int32)
    return jnp.max(jnp.where(hit, entry, -1), axis=-1)


def put(out_ref, row, col, source_ref, entry):
    edge = source_ref.shape[-1]
    block = source_ref[0, jnp.maximum(entry, 0)]
    block = jnp.where(entry >= 0, block, jnp.zeros_like(block))
    out_ref[0, pl.ds(pl.multiple_of(row * edge, edge), edge), col * edge:(col + 1) * edge] = block


def spread_gate_up_kernel(gate_at, up_at, gate_ref, up_ref, out_ref, *, rows, cols):
    chunk = pl.program_id(0)

    @pl.loop(0, rows)
    def _(row):
        for col in range(cols):
            at = (chunk * rows + row) * cols + col
            put(out_ref, row, col, gate_ref, gate_at[at])
            put(out_ref, row, cols + col, up_ref, up_at[at])


def spread_gate_up(gate_at, up_at, gate, up, chunks, rows, cols):
    edge = gate.shape[-1]
    whole = pl.BlockSpec(gate.shape, lambda k, *_: (0, 0, 0, 0), pipeline_mode=pl.Buffered(1))
    out = jax.ShapeDtypeStruct((chunks, rows * edge, 2 * cols * edge), gate.dtype)
    return pl.pallas_call(
        functools.partial(spread_gate_up_kernel, rows=rows, cols=cols),
        out_shape=out,
        grid_spec=pltpu.PrefetchScalarGridSpec(
            num_scalar_prefetch=2,
            grid=(chunks,),
            in_specs=[whole, whole],
            out_specs=pl.BlockSpec((1,) + out.shape[1:], lambda k, *_: (k, 0, 0)),
        ),
        compiler_params=pltpu.CompilerParams(vmem_limit_bytes=48 * MIB),
        cost_estimate=pl.CostEstimate(
            flops=0, bytes_accessed=2 * (2 * gate.size + out.size), transcendentals=0
        ),
        name="spread_gate_up",
    )(gate_at, up_at, gate, up)


def spread_down_kernel(at_ref, values_ref, out_ref, *, rows, cols):
    panel, chunk = pl.program_id(0), pl.program_id(1)
    base = (panel * pl.num_programs(1) + chunk) * rows * cols

    @pl.loop(0, rows)
    def _(row):
        for col in range(cols):
            put(out_ref.at[0], row, col, values_ref, at_ref[base + row * cols + col])


def spread_down(at, values, chunks, rows, cols):
    panels, _, edge, _ = values.shape
    out = jax.ShapeDtypeStruct((chunks, panels, rows * edge, cols * edge), values.dtype)
    return pl.pallas_call(
        functools.partial(spread_down_kernel, rows=rows, cols=cols),
        out_shape=out,
        grid_spec=pltpu.PrefetchScalarGridSpec(
            num_scalar_prefetch=1,
            grid=(panels, chunks),
            in_specs=[pl.BlockSpec((1,) + values.shape[1:], lambda g, k, *_: (g, 0, 0, 0))],
            out_specs=pl.BlockSpec((1, 1) + out.shape[2:], lambda g, k, *_: (k, g, 0, 0)),
        ),
        compiler_params=pltpu.CompilerParams(vmem_limit_bytes=48 * MIB),
        cost_estimate=pl.CostEstimate(
            flops=0, bytes_accessed=2 * (values.size + out.size), transcendentals=0
        ),
        name="spread_down",
    )(at, values)


def gate_up_kernel(*refs, parts):
    own, other = refs[:parts], refs[parts:2 * parts]
    weight = refs[2 * parts]
    outs, held = refs[2 * parts + 1:3 * parts + 1], refs[-1]
    count, half = own[0].shape

    @pl.when(pl.program_id(0) == 0)
    def _():
        for part in range(parts):
            rows = slice(part * count, (part + 1) * count)
            held[rows, :half] = own[part][...]
            held[rows, half:] = other[part][...]

    product = jnp.dot(held[...], weight[0], preferred_element_type=jnp.float32)
    for part in range(parts):
        outs[part][...] = product[part * count:(part + 1) * count].astype(outs[part].dtype)


def gate_up(own, other, dense, chunk):
    parts = len(own)
    count, half = own[0].shape
    _, depth, width = dense.shape
    tile = 256
    out = jax.ShapeDtypeStruct((count, width), own[0].dtype)
    return pl.pallas_call(
        functools.partial(gate_up_kernel, parts=parts),
        out_shape=[out] * parts,
        grid=(width // tile,),
        in_specs=[pl.BlockSpec((count, half), lambda n: (0, 0))] * (2 * parts)
        + [pl.BlockSpec((1, depth, tile), lambda n: (chunk, 0, n))],
        out_specs=[pl.BlockSpec((count, tile), lambda n: (0, n))] * parts,
        scratch_shapes=[pltpu.VMEM((parts * count, 2 * half), own[0].dtype)],
        compiler_params=pltpu.CompilerParams(vmem_limit_bytes=32 * MIB),
        cost_estimate=pl.CostEstimate(
            flops=2 * parts * count * depth * width,
            bytes_accessed=2 * (depth * width + parts * count * (depth + width)),
            transcendentals=0,
        ),
        name=f"gate_up_{chunk}",
    )(*own, *other, dense)


def down_kernel(hidden_ref, weight_ref, before_ref, out_ref, total):
    panel = pl.program_id(0)

    @pl.when(panel == 0)
    def _():
        total[...] = before_ref[...]

    total[...] += jnp.dot(hidden_ref[0], weight_ref[0, 0], preferred_element_type=jnp.float32)

    @pl.when(panel == pl.num_programs(0) - 1)
    def _():
        out_ref[...] = total[...].astype(out_ref.dtype)


def down(hidden, dense, before, chunk, dtype):
    panels, count, depth = hidden.shape
    width = dense.shape[-1]
    return pl.pallas_call(
        down_kernel,
        out_shape=jax.ShapeDtypeStruct((count, width), dtype),
        grid=(panels,),
        in_specs=[
            pl.BlockSpec((1, count, depth), lambda g: (g, 0, 0)),
            pl.BlockSpec((1, 1, depth, width), lambda g: (chunk, g, 0, 0)),
            pl.BlockSpec((count, width), lambda g: (0, 0)),
        ],
        out_specs=pl.BlockSpec((count, width), lambda g: (0, 0)),
        scratch_shapes=[pltpu.VMEM((count, width), jnp.float32)],
        compiler_params=pltpu.CompilerParams(vmem_limit_bytes=32 * MIB),
        cost_estimate=pl.CostEstimate(
            flops=2 * panels * count * depth * width,
            bytes_accessed=2 * panels * depth * (width + count) + 6 * count * width,
            transcendentals=0,
        ),
        name=f"down_{chunk}",
    )(hidden, dense, before)


def by_tokens(
    tokens,
    norm_gain,
    gate_block_entries,
    gate_block_places,
    up_block_entries,
    up_block_places,
    down_values,
    down_slots,
):
    edge = gate_block_entries.shape[-1]
    tok_size = lax.axis_size("tok")
    col_size = lax.axis_size("col")
    rows_per = MODEL_WIDTH // edge // tok_size
    cols_per = HIDDEN_UNITS // edge // col_size
    width_blocks = MODEL_WIDTH // edge // col_size
    chunks = 4 if cols_per % 4 == 0 else 1
    chunk_cols = cols_per // chunks
    count, features = tokens.shape
    half = MODEL_WIDTH // tok_size // 2
    tok, col = lax.axis_index("tok"), lax.axis_index("col")
    side = col % 2

    def swap_tok(array, step):
        return lax.ppermute(array, "tok", [(i, i ^ step) for i in range(tok_size)])

    def swap_core(array):
        return lax.ppermute(array, "col", [(i, i ^ 1) for i in range(col_size)])

    k, r, q = jnp.meshgrid(
        jnp.arange(chunks), jnp.arange(rows_per), jnp.arange(chunk_cols), indexing="ij"
    )
    row = (r + side * (rows_per // 2)) % rows_per
    slots = (row * cols_per + k * chunk_cols + q).reshape(-1).astype(jnp.int32)
    gate_at = lookup(gate_block_places[0], slots)
    up_at = lookup(up_block_places[0], slots)
    down_at = lookup(down_slots, jnp.arange(cols_per * width_blocks, dtype=jnp.int32)).reshape(-1)

    gathered = lax.all_gather(tokens, "col")
    dense = spread_gate_up(
        gate_at, up_at, gate_block_entries, up_block_entries, chunks, rows_per, chunk_cols
    )
    down_dense = spread_down(down_at, down_values, chunks, chunk_cols, width_blocks)

    widened = gathered.astype(jnp.float32)
    mean_square = jnp.mean(widened * widened, axis=(0, 2))[:, None]
    scale = lax.rsqrt(mean_square + EPSILON)
    subs = half // features

    def normed(panel):
        at = panel * 2 + side
        piece = lax.dynamic_slice_in_dim(gathered, at * subs, subs, 0)
        piece = piece.transpose(1, 0, 2).reshape(count, half).astype(jnp.float32)
        gain = lax.dynamic_slice_in_dim(norm_gain, at * half, half, 0)
        return (piece * scale * gain).astype(jnp.bfloat16)

    own = [normed(tok ^ part) for part in range(tok_size)]
    own = [own[0]] + [swap_tok(own[part], part) for part in range(1, tok_size)]
    other = [swap_core(part) for part in own]

    hiddens, halves = [], []
    for chunk in range(chunks):
        sums = gate_up(own, other, dense, chunk)
        terms = [sums[0]] + [swap_tok(sums[part], part) for part in range(1, tok_size)]
        total = functools.reduce(jnp.add, [term.astype(jnp.float32) for term in terms])
        gate_sum, up_sum = jnp.split(total, 2, axis=1)
        hiddens.append((jax.nn.silu(gate_sum) * up_sum).astype(jnp.bfloat16))

    mixed = jnp.zeros((count, width_blocks * edge), jnp.float32)
    for chunk in range(chunks):
        hidden = lax.all_gather(hiddens[chunk], "col")
        last = chunk == chunks - 1
        mixed = down(hidden, down_dense, mixed, chunk, jnp.bfloat16 if last else jnp.float32)
    return mixed

def spread_shares_kernel(gate_at, up_at, *refs, rows, shares, cols):
    (gate_ref, up_ref), (out_ref, mark) = refs[:2], refs[-2:]
    step = pl.program_id(0)
    leave(mark)

    @pl.loop(0, rows)
    def _(row):
        for share in range(shares):
            for col in range(cols):
                at = ((step * rows + row) * shares + share) * cols + col
                put(out_ref, row, 2 * share * cols + col, gate_ref, gate_at[at])
                put(out_ref, row, (2 * share + 1) * cols + col, up_ref, up_at[at])


def spread_shares(gate_at, up_at, gate, up, rows, shares, cols, after, chunk):
    edge = gate.shape[-1]
    steps = 4
    whole = pl.BlockSpec(gate.shape, lambda k, *_: (0, 0, 0, 0), pipeline_mode=pl.Buffered(1))
    out = jax.ShapeDtypeStruct((1, rows * edge, 2 * shares * cols * edge), gate.dtype)
    block = (1, out.shape[1] // steps, out.shape[2])
    return pl.pallas_call(
        functools.partial(spread_shares_kernel, rows=rows // steps, shares=shares, cols=cols),
        out_shape=[out, MARK],
        grid_spec=pltpu.PrefetchScalarGridSpec(
            num_scalar_prefetch=2,
            grid=(steps,),
            in_specs=[whole, whole] + [ANY_SPEC] * len(after),
            out_specs=[pl.BlockSpec(block, lambda k, *_: (0, k, 0)), MARK_SPEC],
        ),
        compiler_params=pltpu.CompilerParams(vmem_limit_bytes=54 * MIB),
        cost_estimate=pl.CostEstimate(
            flops=0, bytes_accessed=2 * (2 * gate.size + out.size), transcendentals=0
        ),
        name=f"spread_gate_up_{chunk}",
    )(gate_at, up_at, gate, up, *after)


def spread_panels_kernel(at_ref, values_ref, *refs, chunks, rows, cols):
    out_ref, mark = refs[-2:]
    panel = pl.program_id(0)
    leave(mark)
    for chunk in range(chunks):
        for row in range(rows):
            for col in range(cols):
                at = ((panel * chunks + chunk) * rows + row) * cols + col
                put(out_ref.at[pl.ds(chunk, 1)], row, col, values_ref, at_ref[at])


def spread_panels(at, values, chunks, rows, cols, after):
    count, _, edge, _ = values.shape
    out = jax.ShapeDtypeStruct((chunks, count * rows * edge, cols * edge), values.dtype)
    return pl.pallas_call(
        functools.partial(spread_panels_kernel, chunks=chunks, rows=rows, cols=cols),
        out_shape=[out, MARK],
        grid_spec=pltpu.PrefetchScalarGridSpec(
            num_scalar_prefetch=1,
            grid=(count,),
            in_specs=[
                pl.BlockSpec((1,) + values.shape[1:], lambda m, *_: (m, 0, 0, 0))
            ]
            + [ANY_SPEC] * len(after),
            out_specs=[
                pl.BlockSpec((chunks, rows * edge, cols * edge), lambda m, *_: (0, m, 0)),
                MARK_SPEC,
            ],
        ),
        compiler_params=pltpu.CompilerParams(vmem_limit_bytes=50 * MIB),
        cost_estimate=pl.CostEstimate(
            flops=0, bytes_accessed=2 * (values.size + out.size), transcendentals=0
        ),
        name="spread_down",
    )(at, values, *after)

def sum_squares_kernel(tokens, out):
    widened = tokens[...].astype(jnp.float32)
    out[...] = jnp.sum(widened * widened, axis=1)[None]


def sum_squares(tokens):
    return pl.pallas_call(
        sum_squares_kernel,
        out_shape=jax.ShapeDtypeStruct((1, tokens.shape[0]), jnp.float32),
        in_specs=[pl.BlockSpec(memory_space=pltpu.VMEM)],
        out_specs=pl.BlockSpec(memory_space=pltpu.VMEM),
        compiler_params=pltpu.CompilerParams(vmem_limit_bytes=4 * MIB),
        name="sum_squares",
    )(tokens)


def pack_kernel(*refs, parts):
    count = refs[0].shape[0]
    for part in range(parts):
        refs[-1][part * count:(part + 1) * count] = refs[part][...]


def pack(pieces, after):
    parts = len(pieces)
    count, width = pieces[0].shape
    return pl.pallas_call(
        functools.partial(pack_kernel, parts=parts),
        out_shape=jax.ShapeDtypeStruct((parts * count, width), pieces[0].dtype),
        in_specs=[pl.BlockSpec(memory_space=pltpu.VMEM)] * parts + [ANY_SPEC] * len(after),
        out_specs=pl.BlockSpec(memory_space=pltpu.VMEM),
        compiler_params=pltpu.CompilerParams(vmem_limit_bytes=16 * MIB),
        cost_estimate=pl.CostEstimate(
            flops=0, bytes_accessed=4 * parts * count * width, transcendentals=0
        ),
        name="pack",
    )(*pieces, *after)


def stack_kernel(*refs, steps):
    pieces, out = refs[:-2], refs[-1]
    count = out.shape[1] // 4
    for i, step in enumerate(steps):
        for part in range(4):
            there = slice((part ^ step) * count, ((part ^ step) + 1) * count)
            rows = pieces[i][there]
            if i + 1 == len(steps) < len(pieces):
                rows += pieces[i + 1][there]
            out[i, part * count:(part + 1) * count] = rows


def stack(pieces, steps, after):
    return pl.pallas_call(
        functools.partial(stack_kernel, steps=steps),
        out_shape=jax.ShapeDtypeStruct((len(steps),) + pieces[0].shape, pieces[0].dtype),
        in_specs=[pl.BlockSpec(memory_space=pltpu.VMEM)] * len(pieces) + [ANY_SPEC],
        out_specs=pl.BlockSpec(memory_space=pltpu.VMEM),
        compiler_params=pltpu.CompilerParams(vmem_limit_bytes=16 * MIB),
        cost_estimate=pl.CostEstimate(
            flops=0, bytes_accessed=4 * len(pieces) * pieces[0].size, transcendentals=0
        ),
        name="stack",
    )(*pieces, after)


def halfway_kernel(kept_a, came_a, kept_b, came_b, *refs):
    out_a, out_b, mark = refs[-3:]
    leave(mark)
    for kept, came, out in ((kept_a, came_a, out_a), (kept_b, came_b, out_b)):
        out[...] = (kept[0].astype(jnp.float32) + came[0].astype(jnp.float32)).astype(out.dtype)


def halfway(kept_a, came_a, kept_b, came_b, after, chunk):
    _, count, width = kept_a.shape
    second = pl.BlockSpec((1, count, width), lambda i: (1, 0, 0))
    whole = pl.BlockSpec((count, width), lambda i: (0, 0))
    out = jax.ShapeDtypeStruct((count, width), kept_a.dtype)
    return pl.pallas_call(
        halfway_kernel,
        out_shape=[out, out, MARK],
        grid=(1,),
        in_specs=[second] * 4 + [ANY_SPEC] * len(after),
        out_specs=[whole, whole, MARK_SPEC],
        compiler_params=pltpu.CompilerParams(vmem_limit_bytes=8 * MIB),
        cost_estimate=pl.CostEstimate(
            flops=2 * count * width, bytes_accessed=12 * count * width, transcendentals=0
        ),
        name=f"halfway_{chunk}",
    )(kept_a, came_a, kept_b, came_b, *after)


def combine_kernel(*refs):
    terms, out, mark = refs[:6], refs[-2], refs[-1]
    leave(mark)
    count = out.shape[0] // 2
    width = out.shape[1]
    for i in range(2):
        kept, came, last = terms[3 * i:3 * i + 3]
        total = kept[0].astype(jnp.float32) + came[0].astype(jnp.float32)
        total += last[...].astype(jnp.float32)
        gate_sum, up_sum = total[:, :width], total[:, width:]
        hidden = gate_sum / (1.0 + jnp.exp(-gate_sum)) * up_sum
        out[i * count:(i + 1) * count] = hidden.astype(out.dtype)


def combine(kept_a, came_a, last_a, kept_b, came_b, last_b, after, chunk):
    count, width = last_a.shape
    first = pl.BlockSpec((1, count, width), lambda i: (0, 0, 0))
    whole = pl.BlockSpec((count, width), lambda i: (0, 0))
    return pl.pallas_call(
        combine_kernel,
        out_shape=[jax.ShapeDtypeStruct((2 * count, width // 2), last_a.dtype), MARK],
        grid=(1,),
        in_specs=[first, first, whole] * 2 + [ANY_SPEC] * len(after),
        out_specs=[pl.BlockSpec((2 * count, width // 2), lambda i: (0, 0)), MARK_SPEC],
        compiler_params=pltpu.CompilerParams(vmem_limit_bytes=10 * MIB),
        cost_estimate=pl.CostEstimate(
            flops=8 * count * width,
            bytes_accessed=14 * count * width,
            transcendentals=count * width // 2,
        ),
        name=f"combine_{chunk}",
    )(kept_a, came_a, last_a, kept_b, came_b, last_b, *after)


def panel_product_kernel(own, other, weight, *refs):
    kept_a, sent_a, kept_b, sent_b, mark = refs[-5:]
    leave(mark)
    half = own.shape[1]
    product = jnp.dot(own[...], weight[0, :half], preferred_element_type=jnp.float32)
    product += jnp.dot(other[...], weight[0, half:], preferred_element_type=jnp.float32)
    product = product.astype(kept_a.dtype)
    count = product.shape[0] // 2
    part = pl.program_id(0)
    for flip in range(2):

        @pl.when(part % 2 == flip)
        def _():
            (sent_a if flip else kept_a)[0] = product[:count]

        @pl.when(part // 2 == flip)
        def _():
            (sent_b if flip else kept_b)[0] = product[count:]


def panel_product(own, other, dense, after, chunk):
    count, half = own.shape
    _, depth, width = dense.shape
    tile = width // 4
    out = jax.ShapeDtypeStruct((2, count // 2, tile), own.dtype)
    return pl.pallas_call(
        panel_product_kernel,
        out_shape=[out] * 4 + [MARK],
        grid=(4,),
        in_specs=[pl.BlockSpec((count, half), lambda n: (0, 0))] * 2
        + [pl.BlockSpec((1, depth, tile), lambda n: (0, 0, n))]
        + [ANY_SPEC] * len(after),
        out_specs=[
            pl.BlockSpec((1,) + out.shape[1:], lambda n: (n // 2, 0, 0)),
            pl.BlockSpec((1,) + out.shape[1:], lambda n: (n // 2, 0, 0)),
            pl.BlockSpec((1,) + out.shape[1:], lambda n: (jnp.minimum(n, 1), 0, 0)),
            pl.BlockSpec((1,) + out.shape[1:], lambda n: (jnp.maximum(n - 2, 0), 0, 0)),
            MARK_SPEC,
        ],
        compiler_params=pltpu.CompilerParams(vmem_limit_bytes=54 * MIB),
        cost_estimate=pl.CostEstimate(
            flops=2 * count * depth * width,
            bytes_accessed=2 * (depth * width + count * (depth + width)),
            transcendentals=0,
        ),
        name=f"gate_up_{chunk}",
    )(own, other, dense, *after)


def down_product_kernel(place, hidden, weight, *refs, added):
    before, outs, mark, held = refs[:added], refs[added:-2], refs[-2], refs[-1]
    leave(mark)
    panels, parts, count, depth = hidden.shape
    chip, flips = place[0], place[1]

    @pl.when(pl.program_id(0) == 0)
    def _():
        for panel in range(panels):
            columns = slice(panel * depth, (panel + 1) * depth)
            for part in range(parts):
                there = part ^ chip ^ (panel // 2)
                held[part * count:(part + 1) * count, columns] = hidden[panel, there]

    if len(outs) == 1:
        product = jnp.dot(held[...], weight[0], preferred_element_type=jnp.float32)
        for term in before:
            product += term[...]
        outs[0][...] = product
        return
    for step, out in enumerate(outs):
        rows = pl.ds(pl.multiple_of((flips ^ step) * count, count), count)
        product = jnp.dot(held[rows], weight[0], preferred_element_type=jnp.float32)
        for term in before:
            product += term[rows]
        out[...] = product.astype(out.dtype)


def down_product(place, hidden, dense, before, chunk, last):
    panels, parts, count, depth = hidden.shape
    _, total, width = dense.shape
    tile = width // 2
    tiles = pl.BlockSpec((parts * count, tile), lambda n, *_: (0, n))
    added = [] if before is None else [before]
    if last:
        out = [jax.ShapeDtypeStruct((count, width), hidden.dtype)] * parts
        out_tiles = [pl.BlockSpec((count, tile), lambda n, *_: (0, n))] * parts
    else:
        out, out_tiles = [jax.ShapeDtypeStruct((parts * count, width), jnp.float32)], [tiles]
    return pl.pallas_call(
        functools.partial(down_product_kernel, added=len(added)),
        out_shape=out + [MARK],
        grid_spec=pltpu.PrefetchScalarGridSpec(
            num_scalar_prefetch=1,
            grid=(width // tile,),
            in_specs=[
                pl.BlockSpec(hidden.shape, lambda n, *_: (0, 0, 0, 0)),
                pl.BlockSpec((1, total, tile), lambda n, *_: (chunk, 0, n)),
            ]
            + [tiles] * len(added),
            out_specs=out_tiles + [MARK_SPEC],
            scratch_shapes=[pltpu.VMEM((parts * count, total), hidden.dtype)],
        ),
        compiler_params=pltpu.CompilerParams(vmem_limit_bytes=42 * MIB),
        cost_estimate=pl.CostEstimate(
            flops=2 * parts * count * total * width,
            bytes_accessed=2 * total * (width + parts * count) + 8 * parts * count * width,
            transcendentals=0,
        ),
        name=f"down_{chunk}",
    )(place, hidden, dense, *added)


def down_steps_kernel(place, own, other, *refs):
    pieces = 2 * own.shape[0]
    weights, before, outs, mark = refs[:pieces], refs[pieces], refs[pieces + 1:-1], refs[-1]
    leave(mark)
    count = before.shape[0] // len(outs)
    for step, out in enumerate(outs):
        at = 0 if len(outs) == 1 else (place[1] ^ step) * count
        rows = pl.ds(pl.multiple_of(at, count), count)
        total = before[rows]
        for i in range(pieces // 2):
            for j, side in enumerate((own, other)):
                total += jnp.dot(
                    side[i, rows], weights[2 * i + j][0, 0], preferred_element_type=jnp.float32
                )
        out[...] = total.astype(out.dtype)


def down_steps(place, own, other, steps, dense, before, chunk, last):
    _, count, depth = own.shape
    width = dense.shape[-1]
    dense = dense.reshape(dense.shape[0], -1, depth, width)
    tile = width // 2
    tiles = pl.BlockSpec((count, tile), lambda n, *_: (0, n))
    whole = pl.BlockSpec(own.shape, lambda n, *_: (0, 0, 0))
    weights = []
    for step in steps:
        for flip in range(2):

            def at(n, place, step=step, flip=flip):
                return chunk, 2 * (place[0] ^ step) + (place[2] ^ flip), 0, n

            weights.append(pl.BlockSpec((1, 1, depth, tile), at))
    out, out_tiles = [jax.ShapeDtypeStruct((count, width), jnp.float32)], [tiles]
    if last:
        out = [jax.ShapeDtypeStruct((count // 4, width), own.dtype)] * 4
        out_tiles = [pl.BlockSpec((count // 4, tile), lambda n, *_: (0, n))] * 4
    return pl.pallas_call(
        down_steps_kernel,
        out_shape=out + [MARK],
        grid_spec=pltpu.PrefetchScalarGridSpec(
            num_scalar_prefetch=1,
            grid=(width // tile,),
            in_specs=[whole, whole] + weights + [tiles],
            out_specs=out_tiles + [MARK_SPEC],
        ),
        compiler_params=pltpu.CompilerParams(vmem_limit_bytes=42 * MIB),
        cost_estimate=pl.CostEstimate(
            flops=4 * len(steps) * count * depth * width,
            bytes_accessed=4 * len(steps) * depth * (width + count) + 8 * count * width,
            transcendentals=0,
        ),
        name=f"down_{chunk}_{steps[0]}",
    )(place, own, other, *[dense] * len(weights), before)


def by_columns(
    tokens,
    norm_gain,
    gate_block_entries,
    gate_block_places,
    up_block_entries,
    up_block_places,
    down_values,
    down_slots,
):
    edge = gate_block_entries.shape[-1]
    tok_size = lax.axis_size("tok")
    col_size = lax.axis_size("col")
    rows_per = MODEL_WIDTH // edge // tok_size
    cols_per = HIDDEN_UNITS // edge // col_size
    width_blocks = MODEL_WIDTH // edge // col_size
    share = cols_per // tok_size
    chunks = 2
    cols = share // chunks
    count, half = tokens.shape
    tok, col = lax.axis_index("tok"), lax.axis_index("col")
    chip, side = col // 2, col % 2
    parts = range(tok_size)

    def swap_tok(array, step):
        return lax.ppermute(array, "tok", [(i, i ^ step) for i in parts])

    def swap_chip(array, step):
        return lax.ppermute(array, "col", [(i, i ^ (2 * step)) for i in range(col_size)])

    def swap_core(array):
        return lax.ppermute(array, "col", [(i, i ^ 1) for i in range(col_size)])

    def to_users(array, part):
        pairs = []
        for i in parts:
            for j in range(col_size):
                user = (j // 2) * col_size + 2 * (i ^ part) + j % 2
                pairs.append((i * col_size + j, user))
        return lax.ppermute(array, ("tok", "col"), pairs)

    squares = sum_squares(tokens)
    squares += swap_core(squares)
    squares += functools.reduce(jnp.add, [swap_chip(squares, step) for step in parts[1:]])
    scale = lax.rsqrt(squares.reshape(-1, 1) / MODEL_WIDTH + EPSILON)
    gain = lax.dynamic_slice_in_dim(norm_gain, col * half, half, 0)
    normed = (tokens.astype(jnp.float32) * scale * gain).astype(jnp.bfloat16)
    pieces = [to_users(normed, part) for part in parts]

    k, r, p, q = jnp.meshgrid(
        jnp.arange(chunks), jnp.arange(rows_per), jnp.arange(tok_size), jnp.arange(cols),
        indexing="ij",
    )
    row = (r + side * (rows_per // 2)) % rows_per
    slots = (row * cols_per + (p ^ tok) * share + k * cols + q).reshape(-1).astype(jnp.int32)
    gate_at = lookup(gate_block_places[0], slots)
    up_at = lookup(up_block_places[0], slots)
    slots = tok * share * width_blocks + jnp.arange(share * width_blocks, dtype=jnp.int32)
    down_at = lookup(down_slots, slots).reshape(-1)
    gate_at, up_at = gate_at.reshape(chunks, -1), up_at.reshape(chunks, -1)

    def spread(chunk, after):
        return spread_shares(
            gate_at[chunk], up_at[chunk], gate_block_entries, up_block_entries,
            rows_per, tok_size, cols, after, chunk,
        )

    dense, mark = spread(0, [])
    own = pack(pieces, [mark])
    other = swap_core(own)

    place = jnp.stack([chip, chip ^ tok, side])
    mixed = [None]
    gathered = []
    *sums, mark = panel_product(own, other, dense, [], 0)
    if chunks > 1:
        dense, mark = spread(1, [mark])
    for chunk in range(chunks):
        kept_a, sent_a, kept_b, sent_b = sums
        came_a, came_b = swap_tok(sent_a, 1), swap_tok(sent_b, 2)
        last_a, last_b, mark = halfway(kept_a, came_a, kept_b, came_b, [mark], chunk)
        last_a, last_b = swap_tok(last_a, 2), swap_tok(last_b, 1)
        if chunk + 1 < chunks:
            *sums, mark = panel_product(own, other, dense, [mark], chunk + 1)
        hidden, mark = combine(kept_a, came_a, last_a, kept_b, came_b, last_b, [mark], chunk)
        if chunk + 2 < chunks:
            dense, mark = spread(chunk + 2, [mark])
        elif chunk == max(chunks - 2, 0):
            down_dense, mark = spread_panels(
                down_at, down_values, chunks, cols, width_blocks, [mark]
            )
        if chunk + 1 < chunks:
            gathered.append(lax.all_gather(hidden.reshape(tok_size, count, -1), "col"))

    far = swap_chip(hidden, 2)
    near = swap_chip(hidden, 1)
    inner = lax.ppermute(hidden, "col", [(i, i ^ 6) for i in range(2, 6)])
    ends = lax.ppermute(far, "col", [(i, i ^ 2) for i in range(2, 6)])
    for chunk in range(chunks - 1):
        *mixed, mark = down_product(place, gathered[chunk], down_dense, mixed[0], chunk, False)
    for steps, pieces in (((0, 1, 2), [hidden, near, far]), ((3,), [inner, ends])):
        held = stack(pieces, steps, mark)
        *mixed, mark = down_steps(
            place, held, swap_core(held), steps, down_dense, mixed[0], chunks - 1, steps == (3,)
        )

    total = mixed[0].astype(jnp.float32)
    for step in parts[1:]:
        total += swap_tok(mixed[step], step).astype(jnp.float32)
    return total.astype(jnp.bfloat16)


def shards(*arrays):
    tok_size = lax.axis_size("tok")
    col_size = lax.axis_size("col")
    blocks = HIDDEN_UNITS // arrays[2].shape[-1]
    even = blocks % (2 * col_size * tok_size) == 0 and col_size == 2 * tok_size == 8
    return (by_columns if even else by_tokens)(*arrays)


def solution(mesh):
    return jax.shard_map(
        shards,
        mesh=mesh,
        in_specs=(
            P("tok", "col"),
            P(),
            P("tok", "col", None, None),
            P("tok", "col"),
            P("tok", "col", None, None),
            P("tok", "col"),
            P(None, "col", None, None),
            P(None, "col"),
        ),
        out_specs=P("tok", "col"),
        check_vma=False,
    )
```

```python
import functools

import jax
import jax.numpy as jnp
from jax import lax
from jax.experimental import pallas as pl
from jax.experimental.pallas import tpu as pltpu
from jax.sharding import PartitionSpec as P

MODEL_WIDTH = 8192
HIDDEN_UNITS = 24576

EPSILON = 1e-05
MIB = 1 << 20
MARK = jax.ShapeDtypeStruct((8, 128), jnp.float32)
MARK_SPEC = pl.BlockSpec(MARK.shape, lambda *_: (0, 0))
ANY_SPEC = pl.BlockSpec(memory_space=pl.ANY)
LITTLE = pl.CostEstimate(flops=1, bytes_accessed=1, transcendentals=0)


def leave(mark):
    mark[...] = jnp.zeros_like(mark)


def lookup(places, slots):
    hit = places[..., None, :] == slots[:, None]
    entry = jnp.arange(places.shape[-1], dtype=jnp.int32)
    return jnp.max(jnp.where(hit, entry, -1), axis=-1)


def put(out_ref, row, col, source_ref, entry):
    edge = source_ref.shape[-1]
    block = source_ref[0, jnp.maximum(entry, 0)]
    block = jnp.where(entry >= 0, block, jnp.zeros_like(block))
    out_ref[0, pl.ds(pl.multiple_of(row * edge, edge), edge), col * edge:(col + 1) * edge] = block


def spread_gate_up_kernel(gate_at, up_at, gate_ref, up_ref, out_ref, *, rows, cols):
    chunk = pl.program_id(0)

    @pl.loop(0, rows)
    def _(row):
        for col in range(cols):
            at = (chunk * rows + row) * cols + col
            put(out_ref, row, col, gate_ref, gate_at[at])
            put(out_ref, row, cols + col, up_ref, up_at[at])


def spread_gate_up(gate_at, up_at, gate, up, chunks, rows, cols):
    edge = gate.shape[-1]
    whole = pl.BlockSpec(gate.shape, lambda k, *_: (0, 0, 0, 0), pipeline_mode=pl.Buffered(1))
    out = jax.ShapeDtypeStruct((chunks, rows * edge, 2 * cols * edge), gate.dtype)
    return pl.pallas_call(
        functools.partial(spread_gate_up_kernel, rows=rows, cols=cols),
        out_shape=out,
        grid_spec=pltpu.PrefetchScalarGridSpec(
            num_scalar_prefetch=2,
            grid=(chunks,),
            in_specs=[whole, whole],
            out_specs=pl.BlockSpec((1,) + out.shape[1:], lambda k, *_: (k, 0, 0)),
        ),
        compiler_params=pltpu.CompilerParams(vmem_limit_bytes=48 * MIB),
        cost_estimate=pl.CostEstimate(
            flops=0, bytes_accessed=2 * (2 * gate.size + out.size), transcendentals=0
        ),
        name="spread_gate_up",
    )(gate_at, up_at, gate, up)


def spread_down_kernel(at_ref, values_ref, out_ref, *, rows, cols):
    panel, chunk = pl.program_id(0), pl.program_id(1)
    base = (panel * pl.num_programs(1) + chunk) * rows * cols

    @pl.loop(0, rows)
    def _(row):
        for col in range(cols):
            put(out_ref.at[0], row, col, values_ref, at_ref[base + row * cols + col])


def spread_down(at, values, chunks, rows, cols):
    panels, _, edge, _ = values.shape
    out = jax.ShapeDtypeStruct((chunks, panels, rows * edge, cols * edge), values.dtype)
    return pl.pallas_call(
        functools.partial(spread_down_kernel, rows=rows, cols=cols),
        out_shape=out,
        grid_spec=pltpu.PrefetchScalarGridSpec(
            num_scalar_prefetch=1,
            grid=(panels, chunks),
            in_specs=[pl.BlockSpec((1,) + values.shape[1:], lambda g, k, *_: (g, 0, 0, 0))],
            out_specs=pl.BlockSpec((1, 1) + out.shape[2:], lambda g, k, *_: (k, g, 0, 0)),
        ),
        compiler_params=pltpu.CompilerParams(vmem_limit_bytes=48 * MIB),
        cost_estimate=pl.CostEstimate(
            flops=0, bytes_accessed=2 * (values.size + out.size), transcendentals=0
        ),
        name="spread_down",
    )(at, values)


def gate_up_kernel(*refs, parts):
    own, other = refs[:parts], refs[parts:2 * parts]
    weight = refs[2 * parts]
    outs, held = refs[2 * parts + 1:3 * parts + 1], refs[-1]
    count, half = own[0].shape

    @pl.when(pl.program_id(0) == 0)
    def _():
        for part in range(parts):
            rows = slice(part * count, (part + 1) * count)
            held[rows, :half] = own[part][...]
            held[rows, half:] = other[part][...]

    product = jnp.dot(held[...], weight[0], preferred_element_type=jnp.float32)
    for part in range(parts):
        outs[part][...] = product[part * count:(part + 1) * count].astype(outs[part].dtype)


def gate_up(own, other, dense, chunk):
    parts = len(own)
    count, half = own[0].shape
    _, depth, width = dense.shape
    tile = 256
    out = jax.ShapeDtypeStruct((count, width), own[0].dtype)
    return pl.pallas_call(
        functools.partial(gate_up_kernel, parts=parts),
        out_shape=[out] * parts,
        grid=(width // tile,),
        in_specs=[pl.BlockSpec((count, half), lambda n: (0, 0))] * (2 * parts)
        + [pl.BlockSpec((1, depth, tile), lambda n: (chunk, 0, n))],
        out_specs=[pl.BlockSpec((count, tile), lambda n: (0, n))] * parts,
        scratch_shapes=[pltpu.VMEM((parts * count, 2 * half), own[0].dtype)],
        compiler_params=pltpu.CompilerParams(vmem_limit_bytes=32 * MIB),
        cost_estimate=pl.CostEstimate(
            flops=2 * parts * count * depth * width,
            bytes_accessed=2 * (depth * width + parts * count * (depth + width)),
            transcendentals=0,
        ),
        name=f"gate_up_{chunk}",
    )(*own, *other, dense)


def down_kernel(hidden_ref, weight_ref, before_ref, out_ref, total):
    panel = pl.program_id(0)

    @pl.when(panel == 0)
    def _():
        total[...] = before_ref[...]

    total[...] += jnp.dot(hidden_ref[0], weight_ref[0, 0], preferred_element_type=jnp.float32)

    @pl.when(panel == pl.num_programs(0) - 1)
    def _():
        out_ref[...] = total[...].astype(out_ref.dtype)


def down(hidden, dense, before, chunk, dtype):
    panels, count, depth = hidden.shape
    width = dense.shape[-1]
    return pl.pallas_call(
        down_kernel,
        out_shape=jax.ShapeDtypeStruct((count, width), dtype),
        grid=(panels,),
        in_specs=[
            pl.BlockSpec((1, count, depth), lambda g: (g, 0, 0)),
            pl.BlockSpec((1, 1, depth, width), lambda g: (chunk, g, 0, 0)),
            pl.BlockSpec((count, width), lambda g: (0, 0)),
        ],
        out_specs=pl.BlockSpec((count, width), lambda g: (0, 0)),
        scratch_shapes=[pltpu.VMEM((count, width), jnp.float32)],
        compiler_params=pltpu.CompilerParams(vmem_limit_bytes=32 * MIB),
        cost_estimate=pl.CostEstimate(
            flops=2 * panels * count * depth * width,
            bytes_accessed=2 * panels * depth * (width + count) + 6 * count * width,
            transcendentals=0,
        ),
        name=f"down_{chunk}",
    )(hidden, dense, before)


def by_tokens(
    tokens,
    norm_gain,
    gate_block_entries,
    gate_block_places,
    up_block_entries,
    up_block_places,
    down_values,
    down_slots,
):
    edge = gate_block_entries.shape[-1]
    tok_size = lax.axis_size("tok")
    col_size = lax.axis_size("col")
    rows_per = MODEL_WIDTH // edge // tok_size
    cols_per = HIDDEN_UNITS // edge // col_size
    width_blocks = MODEL_WIDTH // edge // col_size
    chunks = 4 if cols_per % 4 == 0 else 1
    chunk_cols = cols_per // chunks
    count, features = tokens.shape
    half = MODEL_WIDTH // tok_size // 2
    tok, col = lax.axis_index("tok"), lax.axis_index("col")
    side = col % 2

    def swap_tok(array, step):
        return lax.ppermute(array, "tok", [(i, i ^ step) for i in range(tok_size)])

    def swap_core(array):
        return lax.ppermute(array, "col", [(i, i ^ 1) for i in range(col_size)])

    k, r, q = jnp.meshgrid(
        jnp.arange(chunks), jnp.arange(rows_per), jnp.arange(chunk_cols), indexing="ij"
    )
    row = (r + side * (rows_per // 2)) % rows_per
    slots = (row * cols_per + k * chunk_cols + q).reshape(-1).astype(jnp.int32)
    gate_at = lookup(gate_block_places[0], slots)
    up_at = lookup(up_block_places[0], slots)
    down_at = lookup(down_slots, jnp.arange(cols_per * width_blocks, dtype=jnp.int32)).reshape(-1)

    gathered = lax.all_gather(tokens, "col")
    dense = spread_gate_up(
        gate_at, up_at, gate_block_entries, up_block_entries, chunks, rows_per, chunk_cols
    )
    down_dense = spread_down(down_at, down_values, chunks, chunk_cols, width_blocks)

    widened = gathered.astype(jnp.float32)
    mean_square = jnp.mean(widened * widened, axis=(0, 2))[:, None]
    scale = lax.rsqrt(mean_square + EPSILON)
    subs = half // features

    def normed(panel):
        at = panel * 2 + side
        piece = lax.dynamic_slice_in_dim(gathered, at * subs, subs, 0)
        piece = piece.transpose(1, 0, 2).reshape(count, half).astype(jnp.float32)
        gain = lax.dynamic_slice_in_dim(norm_gain, at * half, half, 0)
        return (piece * scale * gain).astype(jnp.bfloat16)

    own = [normed(tok ^ part) for part in range(tok_size)]
    own = [own[0]] + [swap_tok(own[part], part) for part in range(1, tok_size)]
    other = [swap_core(part) for part in own]

    hiddens, halves = [], []
    for chunk in range(chunks):
        sums = gate_up(own, other, dense, chunk)
        terms = [sums[0]] + [swap_tok(sums[part], part) for part in range(1, tok_size)]
        total = functools.reduce(jnp.add, [term.astype(jnp.float32) for term in terms])
        gate_sum, up_sum = jnp.split(total, 2, axis=1)
        hiddens.append((jax.nn.silu(gate_sum) * up_sum).astype(jnp.bfloat16))

    mixed = jnp.zeros((count, width_blocks * edge), jnp.float32)
    for chunk in range(chunks):
        hidden = lax.all_gather(hiddens[chunk], "col")
        last = chunk == chunks - 1
        mixed = down(hidden, down_dense, mixed, chunk, jnp.bfloat16 if last else jnp.float32)
    return mixed

def spread_shares_kernel(gate_at, up_at, *refs, rows, shares, cols):
    (gate_ref, up_ref), (out_ref, mark) = refs[:2], refs[-2:]
    step = pl.program_id(0)
    leave(mark)

    @pl.loop(0, rows)
    def _(row):
        for share in range(shares):
            for col in range(cols):
                at = ((step * rows + row) * shares + share) * cols + col
                put(out_ref, row, 2 * share * cols + col, gate_ref, gate_at[at])
                put(out_ref, row, (2 * share + 1) * cols + col, up_ref, up_at[at])


def spread_shares(gate_at, up_at, gate, up, rows, shares, cols, after, chunk):
    edge = gate.shape[-1]
    steps = 4
    whole = pl.BlockSpec(gate.shape, lambda k, *_: (0, 0, 0, 0), pipeline_mode=pl.Buffered(1))
    out = jax.ShapeDtypeStruct((1, rows * edge, 2 * shares * cols * edge), gate.dtype)
    block = (1, out.shape[1] // steps, out.shape[2])
    return pl.pallas_call(
        functools.partial(spread_shares_kernel, rows=rows // steps, shares=shares, cols=cols),
        out_shape=[out, MARK],
        grid_spec=pltpu.PrefetchScalarGridSpec(
            num_scalar_prefetch=2,
            grid=(steps,),
            in_specs=[whole, whole] + [ANY_SPEC] * len(after),
            out_specs=[pl.BlockSpec(block, lambda k, *_: (0, k, 0)), MARK_SPEC],
        ),
        compiler_params=pltpu.CompilerParams(vmem_limit_bytes=54 * MIB),
        cost_estimate=LITTLE,
        name=f"spread_gate_up_{chunk}",
    )(gate_at, up_at, gate, up, *after)


def spread_panels_kernel(at_ref, values_ref, *refs, chunks, rows, cols):
    out_ref, mark = refs[-2:]
    panel = pl.program_id(0)
    leave(mark)
    for chunk in range(chunks):
        for row in range(rows):
            for col in range(cols):
                at = ((panel * chunks + chunk) * rows + row) * cols + col
                put(out_ref.at[pl.ds(chunk, 1)], row, col, values_ref, at_ref[at])


def spread_panels(at, values, chunks, rows, cols, after):
    count, _, edge, _ = values.shape
    out = jax.ShapeDtypeStruct((chunks, count * rows * edge, cols * edge), values.dtype)
    return pl.pallas_call(
        functools.partial(spread_panels_kernel, chunks=chunks, rows=rows, cols=cols),
        out_shape=[out, MARK],
        grid_spec=pltpu.PrefetchScalarGridSpec(
            num_scalar_prefetch=1,
            grid=(count,),
            in_specs=[
                pl.BlockSpec((1,) + values.shape[1:], lambda m, *_: (m, 0, 0, 0))
            ]
            + [ANY_SPEC] * len(after),
            out_specs=[
                pl.BlockSpec((chunks, rows * edge, cols * edge), lambda m, *_: (0, m, 0)),
                MARK_SPEC,
            ],
        ),
        compiler_params=pltpu.CompilerParams(vmem_limit_bytes=50 * MIB),
        cost_estimate=LITTLE,
        name="spread_down",
    )(at, values, *after)

def sum_squares_kernel(tokens, out):
    widened = tokens[...].astype(jnp.float32)
    out[...] = jnp.sum(widened * widened, axis=1)[None]


def sum_squares(tokens):
    return pl.pallas_call(
        sum_squares_kernel,
        out_shape=jax.ShapeDtypeStruct((1, tokens.shape[0]), jnp.float32),
        in_specs=[pl.BlockSpec(memory_space=pltpu.VMEM)],
        out_specs=pl.BlockSpec(memory_space=pltpu.VMEM),
        compiler_params=pltpu.CompilerParams(vmem_limit_bytes=4 * MIB),
        name="sum_squares",
    )(tokens)


def pack_kernel(*refs, parts):
    count = refs[0].shape[0]
    for part in range(parts):
        refs[-1][part * count:(part + 1) * count] = refs[part][...]


def pack(pieces, after):
    parts = len(pieces)
    count, width = pieces[0].shape
    return pl.pallas_call(
        functools.partial(pack_kernel, parts=parts),
        out_shape=jax.ShapeDtypeStruct((parts * count, width), pieces[0].dtype),
        in_specs=[pl.BlockSpec(memory_space=pltpu.VMEM)] * parts + [ANY_SPEC] * len(after),
        out_specs=pl.BlockSpec(memory_space=pltpu.VMEM),
        compiler_params=pltpu.CompilerParams(vmem_limit_bytes=16 * MIB),
        cost_estimate=LITTLE,
        name="pack",
    )(*pieces, *after)


def stack_kernel(*refs, steps):
    pieces, out = refs[:-2], refs[-1]
    count = out.shape[1] // 4
    for i, step in enumerate(steps):
        for part in range(4):
            there = slice((part ^ step) * count, ((part ^ step) + 1) * count)
            rows = pieces[i][there]
            if i + 1 == len(steps) < len(pieces):
                rows += pieces[i + 1][there]
            out[i, part * count:(part + 1) * count] = rows


def stack(pieces, steps, after):
    return pl.pallas_call(
        functools.partial(stack_kernel, steps=steps),
        out_shape=jax.ShapeDtypeStruct((len(steps),) + pieces[0].shape, pieces[0].dtype),
        in_specs=[pl.BlockSpec(memory_space=pltpu.VMEM)] * len(pieces) + [ANY_SPEC],
        out_specs=pl.BlockSpec(memory_space=pltpu.VMEM),
        compiler_params=pltpu.CompilerParams(vmem_limit_bytes=16 * MIB),
        cost_estimate=LITTLE,
        name="stack",
    )(*pieces, after)


def halfway_kernel(kept_a, came_a, kept_b, came_b, *refs):
    out_a, out_b, mark = refs[-3:]
    leave(mark)
    for kept, came, out in ((kept_a, came_a, out_a), (kept_b, came_b, out_b)):
        out[...] = (kept[0].astype(jnp.float32) + came[0].astype(jnp.float32)).astype(out.dtype)


def halfway(kept_a, came_a, kept_b, came_b, after, chunk):
    _, count, width = kept_a.shape
    second = pl.BlockSpec((1, count, width), lambda i: (1, 0, 0))
    whole = pl.BlockSpec((count, width), lambda i: (0, 0))
    out = jax.ShapeDtypeStruct((count, width), kept_a.dtype)
    return pl.pallas_call(
        halfway_kernel,
        out_shape=[out, out, MARK],
        grid=(1,),
        in_specs=[second] * 4 + [ANY_SPEC] * len(after),
        out_specs=[whole, whole, MARK_SPEC],
        compiler_params=pltpu.CompilerParams(vmem_limit_bytes=8 * MIB),
        cost_estimate=LITTLE,
        name=f"halfway_{chunk}",
    )(kept_a, came_a, kept_b, came_b, *after)


def combine_kernel(*refs):
    terms, out, mark = refs[:6], refs[-2], refs[-1]
    leave(mark)
    count = out.shape[0] // 2
    width = out.shape[1]
    for i in range(2):
        kept, came, last = terms[3 * i:3 * i + 3]
        total = kept[0].astype(jnp.float32) + came[0].astype(jnp.float32)
        total += last[...].astype(jnp.float32)
        gate_sum, up_sum = total[:, :width], total[:, width:]
        hidden = gate_sum / (1.0 + jnp.exp(-gate_sum)) * up_sum
        out[i * count:(i + 1) * count] = hidden.astype(out.dtype)


def combine(kept_a, came_a, last_a, kept_b, came_b, last_b, after, chunk):
    count, width = last_a.shape
    first = pl.BlockSpec((1, count, width), lambda i: (0, 0, 0))
    whole = pl.BlockSpec((count, width), lambda i: (0, 0))
    return pl.pallas_call(
        combine_kernel,
        out_shape=[jax.ShapeDtypeStruct((2 * count, width // 2), last_a.dtype), MARK],
        grid=(1,),
        in_specs=[first, first, whole] * 2 + [ANY_SPEC] * len(after),
        out_specs=[pl.BlockSpec((2 * count, width // 2), lambda i: (0, 0)), MARK_SPEC],
        compiler_params=pltpu.CompilerParams(vmem_limit_bytes=10 * MIB),
        cost_estimate=LITTLE,
        name=f"combine_{chunk}",
    )(kept_a, came_a, last_a, kept_b, came_b, last_b, *after)


def panel_product_kernel(own, other, weight, *refs):
    kept_a, sent_a, kept_b, sent_b, mark = refs[-5:]
    leave(mark)
    half = own.shape[1]
    product = jnp.dot(own[...], weight[0, :half], preferred_element_type=jnp.float32)
    product += jnp.dot(other[...], weight[0, half:], preferred_element_type=jnp.float32)
    product = product.astype(kept_a.dtype)
    count = product.shape[0] // 2
    part = pl.program_id(0)
    for flip in range(2):

        @pl.when(part % 2 == flip)
        def _():
            (sent_a if flip else kept_a)[0] = product[:count]

        @pl.when(part // 2 == flip)
        def _():
            (sent_b if flip else kept_b)[0] = product[count:]


def panel_product(own, other, dense, after, chunk):
    count, half = own.shape
    _, depth, width = dense.shape
    tile = width // 4
    out = jax.ShapeDtypeStruct((2, count // 2, tile), own.dtype)
    return pl.pallas_call(
        panel_product_kernel,
        out_shape=[out] * 4 + [MARK],
        grid=(4,),
        in_specs=[pl.BlockSpec((count, half), lambda n: (0, 0))] * 2
        + [pl.BlockSpec((1, depth, tile), lambda n: (0, 0, n))]
        + [ANY_SPEC] * len(after),
        out_specs=[
            pl.BlockSpec((1,) + out.shape[1:], lambda n: (n // 2, 0, 0)),
            pl.BlockSpec((1,) + out.shape[1:], lambda n: (n // 2, 0, 0)),
            pl.BlockSpec((1,) + out.shape[1:], lambda n: (jnp.minimum(n, 1), 0, 0)),
            pl.BlockSpec((1,) + out.shape[1:], lambda n: (jnp.maximum(n - 2, 0), 0, 0)),
            MARK_SPEC,
        ],
        compiler_params=pltpu.CompilerParams(vmem_limit_bytes=54 * MIB),
        cost_estimate=LITTLE,
        name=f"gate_up_{chunk}",
    )(own, other, dense, *after)


def panel_half_kernel(own, other, weight, *refs, first):
    out_a, out_b, mark = refs[-3:]
    leave(mark)
    half = own.shape[1]
    count = own.shape[0] // 2
    part = pl.program_id(0) + first

    def product(rows):
        total = jnp.dot(own[rows], weight[0, :half], preferred_element_type=jnp.float32)
        total += jnp.dot(other[rows], weight[0, half:], preferred_element_type=jnp.float32)
        return total.astype(out_a.dtype)

    @pl.when(part % 2 == first)
    def _():
        out_a[0] = product(slice(0, count))

    @pl.when(part // 2 == first)
    def _():
        out_b[0] = product(slice(count, 2 * count))


def panel_half(own, other, dense, first, after, chunk):
    count, half = own.shape
    _, depth, width = dense.shape
    tile = width // 4
    out = jax.ShapeDtypeStruct((2, count // 2, tile), own.dtype)
    at = pl.BlockSpec((1,) + out.shape[1:], lambda n: ((n // 2 if first else (n + 1) // 2), 0, 0))
    return pl.pallas_call(
        functools.partial(panel_half_kernel, first=first),
        out_shape=[out, out, MARK],
        grid=(3,),
        in_specs=[pl.BlockSpec((count, half), lambda n: (0, 0))] * 2
        + [pl.BlockSpec((1, depth, tile), lambda n: (0, 0, n + first))]
        + [ANY_SPEC] * len(after),
        out_specs=[at, at, MARK_SPEC],
        compiler_params=pltpu.CompilerParams(vmem_limit_bytes=54 * MIB),
        cost_estimate=LITTLE,
        name=f"{'sent' if first else 'kept'}_{chunk}",
    )(own, other, dense, *after)


def down_product_kernel(place, hidden, weight, *refs, added):
    before, outs, mark, held = refs[:added], refs[added:-2], refs[-2], refs[-1]
    leave(mark)
    panels, parts, count, depth = hidden.shape
    chip, flips = place[0], place[1]

    @pl.when(pl.program_id(0) == 0)
    def _():
        for panel in range(panels):
            columns = slice(panel * depth, (panel + 1) * depth)
            for part in range(parts):
                there = part ^ chip ^ (panel // 2)
                held[part * count:(part + 1) * count, columns] = hidden[panel, there]

    if len(outs) == 1:
        product = jnp.dot(held[...], weight[0], preferred_element_type=jnp.float32)
        for term in before:
            product += term[...]
        outs[0][...] = product
        return
    for step, out in enumerate(outs):
        rows = pl.ds(pl.multiple_of((flips ^ step) * count, count), count)
        product = jnp.dot(held[rows], weight[0], preferred_element_type=jnp.float32)
        for term in before:
            product += term[rows]
        out[...] = product.astype(out.dtype)


def down_product(place, hidden, dense, before, chunk, last):
    panels, parts, count, depth = hidden.shape
    _, total, width = dense.shape
    tile = width // 2
    tiles = pl.BlockSpec((parts * count, tile), lambda n, *_: (0, n))
    added = [] if before is None else [before]
    if last:
        out = [jax.ShapeDtypeStruct((count, width), hidden.dtype)] * parts
        out_tiles = [pl.BlockSpec((count, tile), lambda n, *_: (0, n))] * parts
    else:
        out, out_tiles = [jax.ShapeDtypeStruct((parts * count, width), jnp.float32)], [tiles]
    return pl.pallas_call(
        functools.partial(down_product_kernel, added=len(added)),
        out_shape=out + [MARK],
        grid_spec=pltpu.PrefetchScalarGridSpec(
            num_scalar_prefetch=1,
            grid=(width // tile,),
            in_specs=[
                pl.BlockSpec(hidden.shape, lambda n, *_: (0, 0, 0, 0)),
                pl.BlockSpec((1, total, tile), lambda n, *_: (chunk, 0, n)),
            ]
            + [tiles] * len(added),
            out_specs=out_tiles + [MARK_SPEC],
            scratch_shapes=[pltpu.VMEM((parts * count, total), hidden.dtype)],
        ),
        compiler_params=pltpu.CompilerParams(vmem_limit_bytes=42 * MIB),
        cost_estimate=LITTLE,
        name=f"down_{chunk}",
    )(place, hidden, dense, *added)


def down_steps_kernel(place, own, other, *refs):
    pieces = 2 * own.shape[0]
    weights, before, outs, mark = refs[:pieces], refs[pieces], refs[pieces + 1:-1], refs[-1]
    leave(mark)
    count = before.shape[0] // len(outs)
    for step, out in enumerate(outs):
        at = 0 if len(outs) == 1 else (place[1] ^ step) * count
        rows = pl.ds(pl.multiple_of(at, count), count)
        total = before[rows]
        for i in range(pieces // 2):
            for j, side in enumerate((own, other)):
                total += jnp.dot(
                    side[i, rows], weights[2 * i + j][0, 0], preferred_element_type=jnp.float32
                )
        out[...] = total.astype(out.dtype)


def down_steps(place, own, other, steps, dense, before, chunk, last):
    _, count, depth = own.shape
    width = dense.shape[-1]
    dense = dense.reshape(dense.shape[0], -1, depth, width)
    tile = width // 2
    tiles = pl.BlockSpec((count, tile), lambda n, *_: (0, n))
    whole = pl.BlockSpec(own.shape, lambda n, *_: (0, 0, 0))
    weights = []
    for step in steps:
        for flip in range(2):

            def at(n, place, step=step, flip=flip):
                return chunk, 2 * (place[0] ^ step) + (place[2] ^ flip), 0, n

            weights.append(pl.BlockSpec((1, 1, depth, tile), at))
    out, out_tiles = [jax.ShapeDtypeStruct((count, width), jnp.float32)], [tiles]
    if last:
        out = [jax.ShapeDtypeStruct((count // 4, width), own.dtype)] * 4
        out_tiles = [pl.BlockSpec((count // 4, tile), lambda n, *_: (0, n))] * 4
    return pl.pallas_call(
        down_steps_kernel,
        out_shape=out + [MARK],
        grid_spec=pltpu.PrefetchScalarGridSpec(
            num_scalar_prefetch=1,
            grid=(width // tile,),
            in_specs=[whole, whole] + weights + [tiles],
            out_specs=out_tiles + [MARK_SPEC],
        ),
        compiler_params=pltpu.CompilerParams(vmem_limit_bytes=42 * MIB),
        cost_estimate=LITTLE,
        name=f"down_{chunk}_{steps[0]}",
    )(place, own, other, *[dense] * len(weights), before)


def by_columns(
    tokens,
    norm_gain,
    gate_block_entries,
    gate_block_places,
    up_block_entries,
    up_block_places,
    down_values,
    down_slots,
):
    edge = gate_block_entries.shape[-1]
    tok_size = lax.axis_size("tok")
    col_size = lax.axis_size("col")
    rows_per = MODEL_WIDTH // edge // tok_size
    cols_per = HIDDEN_UNITS // edge // col_size
    width_blocks = MODEL_WIDTH // edge // col_size
    share = cols_per // tok_size
    chunks = 2
    cols = share // chunks
    count, half = tokens.shape
    tok, col = lax.axis_index("tok"), lax.axis_index("col")
    chip, side = col // 2, col % 2
    parts = range(tok_size)

    def swap_tok(array, step):
        return lax.ppermute(array, "tok", [(i, i ^ step) for i in parts])

    def swap_chip(array, step):
        return lax.ppermute(array, "col", [(i, i ^ (2 * step)) for i in range(col_size)])

    def swap_core(array):
        return lax.ppermute(array, "col", [(i, i ^ 1) for i in range(col_size)])

    def to_users(array, part):
        pairs = []
        for i in parts:
            for j in range(col_size):
                user = (j // 2) * col_size + 2 * (i ^ part) + j % 2
                pairs.append((i * col_size + j, user))
        return lax.ppermute(array, ("tok", "col"), pairs)

    squares = sum_squares(tokens)
    squares += swap_core(squares)
    squares += functools.reduce(jnp.add, [swap_chip(squares, step) for step in parts[1:]])
    scale = lax.rsqrt(squares.reshape(-1, 1) / MODEL_WIDTH + EPSILON)
    gain = lax.dynamic_slice_in_dim(norm_gain, col * half, half, 0)
    normed = (tokens.astype(jnp.float32) * scale * gain).astype(jnp.bfloat16)
    pieces = [to_users(normed, part) for part in parts]

    k, r, p, q = jnp.meshgrid(
        jnp.arange(chunks), jnp.arange(rows_per), jnp.arange(tok_size), jnp.arange(cols),
        indexing="ij",
    )
    row = (r + side * (rows_per // 2)) % rows_per
    slots = (row * cols_per + (p ^ tok) * share + k * cols + q).reshape(-1).astype(jnp.int32)
    gate_at = lookup(gate_block_places[0], slots)
    up_at = lookup(up_block_places[0], slots)
    slots = tok * share * width_blocks + jnp.arange(share * width_blocks, dtype=jnp.int32)
    down_at = lookup(down_slots, slots).reshape(-1)
    gate_at, up_at = gate_at.reshape(chunks, -1), up_at.reshape(chunks, -1)

    def spread(chunk, after):
        return spread_shares(
            gate_at[chunk], up_at[chunk], gate_block_entries, up_block_entries,
            rows_per, tok_size, cols, after, chunk,
        )

    dense, mark = spread(0, [])
    own = pack(pieces, [mark])
    other = swap_core(own)

    place = jnp.stack([chip, chip ^ tok, side])
    mixed = [None]
    gathered = []
    sent_a, sent_b, mark = panel_half(own, other, dense, 1, [], 0)
    kept_a, kept_b, mark = panel_half(own, other, dense, 0, [mark], 0)
    sums = kept_a, sent_a, kept_b, sent_b
    if chunks > 1:
        dense, mark = spread(1, [mark])
    for chunk in range(chunks):
        kept_a, sent_a, kept_b, sent_b = sums
        came_a, came_b = swap_tok(sent_a, 1), swap_tok(sent_b, 2)
        last_a, last_b, mark = halfway(kept_a, came_a, kept_b, came_b, [mark], chunk)
        last_a, last_b = swap_tok(last_a, 2), swap_tok(last_b, 1)
        if chunk + 1 < chunks:
            *sums, mark = panel_product(own, other, dense, [mark], chunk + 1)
        hidden, mark = combine(kept_a, came_a, last_a, kept_b, came_b, last_b, [mark], chunk)
        if chunk + 2 < chunks:
            dense, mark = spread(chunk + 2, [mark])
        elif chunk == max(chunks - 2, 0):
            down_dense, mark = spread_panels(
                down_at, down_values, chunks, cols, width_blocks, [mark]
            )
        if chunk + 1 < chunks:
            gathered.append(lax.all_gather(hidden.reshape(tok_size, count, -1), "col"))

    far = swap_chip(hidden, 2)
    near = swap_chip(hidden, 1)
    inner = lax.ppermute(hidden, "col", [(i, i ^ 6) for i in range(2, 6)])
    ends = lax.ppermute(far, "col", [(i, i ^ 2) for i in range(2, 6)])
    for chunk in range(chunks - 1):
        *mixed, mark = down_product(place, gathered[chunk], down_dense, mixed[0], chunk, False)
    for steps, pieces in (((0, 1, 2), [hidden, near, far]), ((3,), [inner, ends])):
        held = stack(pieces, steps, mark)
        *mixed, mark = down_steps(
            place, held, swap_core(held), steps, down_dense, mixed[0], chunks - 1, steps == (3,)
        )

    total = mixed[0].astype(jnp.float32)
    for step in parts[1:]:
        total += swap_tok(mixed[step], step).astype(jnp.float32)
    return total.astype(jnp.bfloat16)


def shards(*arrays):
    tok_size = lax.axis_size("tok")
    col_size = lax.axis_size("col")
    blocks = HIDDEN_UNITS // arrays[2].shape[-1]
    even = blocks % (2 * col_size * tok_size) == 0 and col_size == 2 * tok_size == 8
    return (by_columns if even else by_tokens)(*arrays)


def solution(mesh):
    return jax.shard_map(
        shards,
        mesh=mesh,
        in_specs=(
            P("tok", "col"),
            P(),
            P("tok", "col", None, None),
            P("tok", "col"),
            P("tok", "col", None, None),
            P("tok", "col"),
            P(None, "col", None, None),
            P(None, "col"),
        ),
        out_specs=P("tok", "col"),
        check_vma=False,
    )
```

```python
import functools

import jax
import jax.numpy as jnp
from jax import lax
from jax.experimental import pallas as pl
from jax.experimental.pallas import tpu as pltpu
from jax.sharding import PartitionSpec as P

MODEL_WIDTH = 8192
HIDDEN_UNITS = 24576

EPSILON = 1e-05
MIB = 1 << 20
MARK = jax.ShapeDtypeStruct((8, 128), jnp.float32)
MARK_SPEC = pl.BlockSpec(MARK.shape, lambda *_: (0, 0))
ANY_SPEC = pl.BlockSpec(memory_space=pl.ANY)
LITTLE = pl.CostEstimate(flops=1, bytes_accessed=1, transcendentals=0)


def leave(mark):
    mark[...] = jnp.zeros_like(mark)


def lookup(places, slots):
    hit = places[..., None, :] == slots[:, None]
    entry = jnp.arange(places.shape[-1], dtype=jnp.int32)
    return jnp.max(jnp.where(hit, entry, -1), axis=-1)


def put(out_ref, row, col, source_ref, entry):
    edge = source_ref.shape[-1]
    block = source_ref[0, jnp.maximum(entry, 0)]
    block = jnp.where(entry >= 0, block, jnp.zeros_like(block))
    out_ref[0, pl.ds(pl.multiple_of(row * edge, edge), edge), col * edge:(col + 1) * edge] = block


def spread_gate_up_kernel(gate_at, up_at, gate_ref, up_ref, out_ref, *, rows, cols):
    chunk = pl.program_id(0)

    @pl.loop(0, rows)
    def _(row):
        for col in range(cols):
            at = (chunk * rows + row) * cols + col
            put(out_ref, row, col, gate_ref, gate_at[at])
            put(out_ref, row, cols + col, up_ref, up_at[at])


def spread_gate_up(gate_at, up_at, gate, up, chunks, rows, cols):
    edge = gate.shape[-1]
    whole = pl.BlockSpec(gate.shape, lambda k, *_: (0, 0, 0, 0), pipeline_mode=pl.Buffered(1))
    out = jax.ShapeDtypeStruct((chunks, rows * edge, 2 * cols * edge), gate.dtype)
    return pl.pallas_call(
        functools.partial(spread_gate_up_kernel, rows=rows, cols=cols),
        out_shape=out,
        grid_spec=pltpu.PrefetchScalarGridSpec(
            num_scalar_prefetch=2,
            grid=(chunks,),
            in_specs=[whole, whole],
            out_specs=pl.BlockSpec((1,) + out.shape[1:], lambda k, *_: (k, 0, 0)),
        ),
        compiler_params=pltpu.CompilerParams(vmem_limit_bytes=48 * MIB),
        cost_estimate=pl.CostEstimate(
            flops=0, bytes_accessed=2 * (2 * gate.size + out.size), transcendentals=0
        ),
        name="spread_gate_up",
    )(gate_at, up_at, gate, up)


def spread_down_kernel(at_ref, values_ref, out_ref, *, rows, cols):
    panel, chunk = pl.program_id(0), pl.program_id(1)
    base = (panel * pl.num_programs(1) + chunk) * rows * cols

    @pl.loop(0, rows)
    def _(row):
        for col in range(cols):
            put(out_ref.at[0], row, col, values_ref, at_ref[base + row * cols + col])


def spread_down(at, values, chunks, rows, cols):
    panels, _, edge, _ = values.shape
    out = jax.ShapeDtypeStruct((chunks, panels, rows * edge, cols * edge), values.dtype)
    return pl.pallas_call(
        functools.partial(spread_down_kernel, rows=rows, cols=cols),
        out_shape=out,
        grid_spec=pltpu.PrefetchScalarGridSpec(
            num_scalar_prefetch=1,
            grid=(panels, chunks),
            in_specs=[pl.BlockSpec((1,) + values.shape[1:], lambda g, k, *_: (g, 0, 0, 0))],
            out_specs=pl.BlockSpec((1, 1) + out.shape[2:], lambda g, k, *_: (k, g, 0, 0)),
        ),
        compiler_params=pltpu.CompilerParams(vmem_limit_bytes=48 * MIB),
        cost_estimate=pl.CostEstimate(
            flops=0, bytes_accessed=2 * (values.size + out.size), transcendentals=0
        ),
        name="spread_down",
    )(at, values)


def gate_up_kernel(*refs, parts):
    own, other = refs[:parts], refs[parts:2 * parts]
    weight = refs[2 * parts]
    outs, held = refs[2 * parts + 1:3 * parts + 1], refs[-1]
    count, half = own[0].shape

    @pl.when(pl.program_id(0) == 0)
    def _():
        for part in range(parts):
            rows = slice(part * count, (part + 1) * count)
            held[rows, :half] = own[part][...]
            held[rows, half:] = other[part][...]

    product = jnp.dot(held[...], weight[0], preferred_element_type=jnp.float32)
    for part in range(parts):
        outs[part][...] = product[part * count:(part + 1) * count].astype(outs[part].dtype)


def gate_up(own, other, dense, chunk):
    parts = len(own)
    count, half = own[0].shape
    _, depth, width = dense.shape
    tile = 256
    out = jax.ShapeDtypeStruct((count, width), own[0].dtype)
    return pl.pallas_call(
        functools.partial(gate_up_kernel, parts=parts),
        out_shape=[out] * parts,
        grid=(width // tile,),
        in_specs=[pl.BlockSpec((count, half), lambda n: (0, 0))] * (2 * parts)
        + [pl.BlockSpec((1, depth, tile), lambda n: (chunk, 0, n))],
        out_specs=[pl.BlockSpec((count, tile), lambda n: (0, n))] * parts,
        scratch_shapes=[pltpu.VMEM((parts * count, 2 * half), own[0].dtype)],
        compiler_params=pltpu.CompilerParams(vmem_limit_bytes=32 * MIB),
        cost_estimate=pl.CostEstimate(
            flops=2 * parts * count * depth * width,
            bytes_accessed=2 * (depth * width + parts * count * (depth + width)),
            transcendentals=0,
        ),
        name=f"gate_up_{chunk}",
    )(*own, *other, dense)


def down_kernel(hidden_ref, weight_ref, before_ref, out_ref, total):
    panel = pl.program_id(0)

    @pl.when(panel == 0)
    def _():
        total[...] = before_ref[...]

    total[...] += jnp.dot(hidden_ref[0], weight_ref[0, 0], preferred_element_type=jnp.float32)

    @pl.when(panel == pl.num_programs(0) - 1)
    def _():
        out_ref[...] = total[...].astype(out_ref.dtype)


def down(hidden, dense, before, chunk, dtype):
    panels, count, depth = hidden.shape
    width = dense.shape[-1]
    return pl.pallas_call(
        down_kernel,
        out_shape=jax.ShapeDtypeStruct((count, width), dtype),
        grid=(panels,),
        in_specs=[
            pl.BlockSpec((1, count, depth), lambda g: (g, 0, 0)),
            pl.BlockSpec((1, 1, depth, width), lambda g: (chunk, g, 0, 0)),
            pl.BlockSpec((count, width), lambda g: (0, 0)),
        ],
        out_specs=pl.BlockSpec((count, width), lambda g: (0, 0)),
        scratch_shapes=[pltpu.VMEM((count, width), jnp.float32)],
        compiler_params=pltpu.CompilerParams(vmem_limit_bytes=32 * MIB),
        cost_estimate=pl.CostEstimate(
            flops=2 * panels * count * depth * width,
            bytes_accessed=2 * panels * depth * (width + count) + 6 * count * width,
            transcendentals=0,
        ),
        name=f"down_{chunk}",
    )(hidden, dense, before)


def by_tokens(
    tokens,
    norm_gain,
    gate_block_entries,
    gate_block_places,
    up_block_entries,
    up_block_places,
    down_values,
    down_slots,
):
    edge = gate_block_entries.shape[-1]
    tok_size = lax.axis_size("tok")
    col_size = lax.axis_size("col")
    rows_per = MODEL_WIDTH // edge // tok_size
    cols_per = HIDDEN_UNITS // edge // col_size
    width_blocks = MODEL_WIDTH // edge // col_size
    chunks = 4 if cols_per % 4 == 0 else 1
    chunk_cols = cols_per // chunks
    count, features = tokens.shape
    half = MODEL_WIDTH // tok_size // 2
    tok, col = lax.axis_index("tok"), lax.axis_index("col")
    side = col % 2

    def swap_tok(array, step):
        return lax.ppermute(array, "tok", [(i, i ^ step) for i in range(tok_size)])

    def swap_core(array):
        return lax.ppermute(array, "col", [(i, i ^ 1) for i in range(col_size)])

    k, r, q = jnp.meshgrid(
        jnp.arange(chunks), jnp.arange(rows_per), jnp.arange(chunk_cols), indexing="ij"
    )
    row = (r + side * (rows_per // 2)) % rows_per
    slots = (row * cols_per + k * chunk_cols + q).reshape(-1).astype(jnp.int32)
    gate_at = lookup(gate_block_places[0], slots)
    up_at = lookup(up_block_places[0], slots)
    down_at = lookup(down_slots, jnp.arange(cols_per * width_blocks, dtype=jnp.int32)).reshape(-1)

    gathered = lax.all_gather(tokens, "col")
    dense = spread_gate_up(
        gate_at, up_at, gate_block_entries, up_block_entries, chunks, rows_per, chunk_cols
    )
    down_dense = spread_down(down_at, down_values, chunks, chunk_cols, width_blocks)

    widened = gathered.astype(jnp.float32)
    mean_square = jnp.mean(widened * widened, axis=(0, 2))[:, None]
    scale = lax.rsqrt(mean_square + EPSILON)
    subs = half // features

    def normed(panel):
        at = panel * 2 + side
        piece = lax.dynamic_slice_in_dim(gathered, at * subs, subs, 0)
        piece = piece.transpose(1, 0, 2).reshape(count, half).astype(jnp.float32)
        gain = lax.dynamic_slice_in_dim(norm_gain, at * half, half, 0)
        return (piece * scale * gain).astype(jnp.bfloat16)

    own = [normed(tok ^ part) for part in range(tok_size)]
    own = [own[0]] + [swap_tok(own[part], part) for part in range(1, tok_size)]
    other = [swap_core(part) for part in own]

    hiddens, halves = [], []
    for chunk in range(chunks):
        sums = gate_up(own, other, dense, chunk)
        terms = [sums[0]] + [swap_tok(sums[part], part) for part in range(1, tok_size)]
        total = functools.reduce(jnp.add, [term.astype(jnp.float32) for term in terms])
        gate_sum, up_sum = jnp.split(total, 2, axis=1)
        hiddens.append((jax.nn.silu(gate_sum) * up_sum).astype(jnp.bfloat16))

    mixed = jnp.zeros((count, width_blocks * edge), jnp.float32)
    for chunk in range(chunks):
        hidden = lax.all_gather(hiddens[chunk], "col")
        last = chunk == chunks - 1
        mixed = down(hidden, down_dense, mixed, chunk, jnp.bfloat16 if last else jnp.float32)
    return mixed

def spread_shares_kernel(gate_at, up_at, *refs, rows, shares, cols):
    (gate_ref, up_ref), (out_ref, mark) = refs[:2], refs[-2:]
    step = pl.program_id(0)
    leave(mark)

    @pl.loop(0, rows)
    def _(row):
        for share in range(shares):
            for col in range(cols):
                at = ((step * rows + row) * shares + share) * cols + col
                put(out_ref, row, 2 * share * cols + col, gate_ref, gate_at[at])
                put(out_ref, row, (2 * share + 1) * cols + col, up_ref, up_at[at])


def spread_shares(gate_at, up_at, gate, up, rows, shares, cols, after, chunk):
    edge = gate.shape[-1]
    steps = 4
    whole = pl.BlockSpec(gate.shape, lambda k, *_: (0, 0, 0, 0), pipeline_mode=pl.Buffered(1))
    out = jax.ShapeDtypeStruct((1, rows * edge, 2 * shares * cols * edge), gate.dtype)
    block = (1, out.shape[1] // steps, out.shape[2])
    return pl.pallas_call(
        functools.partial(spread_shares_kernel, rows=rows // steps, shares=shares, cols=cols),
        out_shape=[out, MARK],
        grid_spec=pltpu.PrefetchScalarGridSpec(
            num_scalar_prefetch=2,
            grid=(steps,),
            in_specs=[whole, whole] + [ANY_SPEC] * len(after),
            out_specs=[pl.BlockSpec(block, lambda k, *_: (0, k, 0)), MARK_SPEC],
        ),
        compiler_params=pltpu.CompilerParams(vmem_limit_bytes=54 * MIB),
        cost_estimate=LITTLE,
        name=f"spread_gate_up_{chunk}",
    )(gate_at, up_at, gate, up, *after)


def spread_panels_kernel(at_ref, values_ref, *refs, chunks, rows, cols):
    out_ref, mark = refs[-2:]
    panel = pl.program_id(0)
    leave(mark)
    for chunk in range(chunks):
        for row in range(rows):
            for col in range(cols):
                at = ((panel * chunks + chunk) * rows + row) * cols + col
                put(out_ref.at[pl.ds(chunk, 1)], row, col, values_ref, at_ref[at])


def spread_panels(at, values, chunks, rows, cols, after):
    count, _, edge, _ = values.shape
    out = jax.ShapeDtypeStruct((chunks, count * rows * edge, cols * edge), values.dtype)
    return pl.pallas_call(
        functools.partial(spread_panels_kernel, chunks=chunks, rows=rows, cols=cols),
        out_shape=[out, MARK],
        grid_spec=pltpu.PrefetchScalarGridSpec(
            num_scalar_prefetch=1,
            grid=(count,),
            in_specs=[
                pl.BlockSpec((1,) + values.shape[1:], lambda m, *_: (m, 0, 0, 0))
            ]
            + [ANY_SPEC] * len(after),
            out_specs=[
                pl.BlockSpec((chunks, rows * edge, cols * edge), lambda m, *_: (0, m, 0)),
                MARK_SPEC,
            ],
        ),
        compiler_params=pltpu.CompilerParams(vmem_limit_bytes=50 * MIB),
        cost_estimate=LITTLE,
        name="spread_down",
    )(at, values, *after)

def sum_squares_kernel(tokens, out):
    widened = tokens[...].astype(jnp.float32)
    out[...] = jnp.sum(widened * widened, axis=1)[None]


def sum_squares(tokens):
    return pl.pallas_call(
        sum_squares_kernel,
        out_shape=jax.ShapeDtypeStruct((1, tokens.shape[0]), jnp.float32),
        in_specs=[pl.BlockSpec(memory_space=pltpu.VMEM)],
        out_specs=pl.BlockSpec(memory_space=pltpu.VMEM),
        compiler_params=pltpu.CompilerParams(vmem_limit_bytes=4 * MIB),
        name="sum_squares",
    )(tokens)


def pack_kernel(*refs, parts):
    count = refs[0].shape[0]
    for part in range(parts):
        refs[-1][part * count:(part + 1) * count] = refs[part][...]


def pack(pieces, after):
    parts = len(pieces)
    count, width = pieces[0].shape
    return pl.pallas_call(
        functools.partial(pack_kernel, parts=parts),
        out_shape=jax.ShapeDtypeStruct((parts * count, width), pieces[0].dtype),
        in_specs=[pl.BlockSpec(memory_space=pltpu.VMEM)] * parts + [ANY_SPEC] * len(after),
        out_specs=pl.BlockSpec(memory_space=pltpu.VMEM),
        compiler_params=pltpu.CompilerParams(vmem_limit_bytes=16 * MIB),
        cost_estimate=LITTLE,
        name="pack",
    )(*pieces, *after)


def stack_kernel(*refs, steps):
    pieces, out, mark = refs[:-3], refs[-2], refs[-1]
    leave(mark)
    count = out.shape[1] // 4
    for i, step in enumerate(steps):
        for part in range(4):
            there = slice((part ^ step) * count, ((part ^ step) + 1) * count)
            rows = pieces[i][there]
            if i + 1 == len(steps) < len(pieces):
                rows += pieces[i + 1][there]
            out[i, part * count:(part + 1) * count] = rows


def stack(pieces, steps, after):
    return pl.pallas_call(
        functools.partial(stack_kernel, steps=steps),
        out_shape=[jax.ShapeDtypeStruct((len(steps),) + pieces[0].shape, pieces[0].dtype), MARK],
        in_specs=[pl.BlockSpec(memory_space=pltpu.VMEM)] * len(pieces) + [ANY_SPEC],
        out_specs=[pl.BlockSpec(memory_space=pltpu.VMEM)] * 2,
        compiler_params=pltpu.CompilerParams(vmem_limit_bytes=16 * MIB),
        cost_estimate=LITTLE,
        name="stack",
    )(*pieces, after)


def halfway_kernel(kept_a, came_a, kept_b, came_b, *refs):
    out_a, out_b, mark = refs[-3:]
    leave(mark)
    for kept, came, out in ((kept_a, came_a, out_a), (kept_b, came_b, out_b)):
        out[...] = (kept[0].astype(jnp.float32) + came[0].astype(jnp.float32)).astype(out.dtype)


def halfway(kept_a, came_a, kept_b, came_b, after, chunk):
    _, count, width = kept_a.shape
    second = pl.BlockSpec((1, count, width), lambda i: (1, 0, 0))
    whole = pl.BlockSpec((count, width), lambda i: (0, 0))
    out = jax.ShapeDtypeStruct((count, width), kept_a.dtype)
    return pl.pallas_call(
        halfway_kernel,
        out_shape=[out, out, MARK],
        grid=(1,),
        in_specs=[second] * 4 + [ANY_SPEC] * len(after),
        out_specs=[whole, whole, MARK_SPEC],
        compiler_params=pltpu.CompilerParams(vmem_limit_bytes=8 * MIB),
        cost_estimate=LITTLE,
        name=f"halfway_{chunk}",
    )(kept_a, came_a, kept_b, came_b, *after)


def combine_kernel(*refs):
    terms, out, mark = refs[:6], refs[-2], refs[-1]
    leave(mark)
    count = out.shape[0] // 2
    width = out.shape[1]
    for i in range(2):
        kept, came, last = terms[3 * i:3 * i + 3]
        total = kept[0].astype(jnp.float32) + came[0].astype(jnp.float32)
        total += last[...].astype(jnp.float32)
        gate_sum, up_sum = total[:, :width], total[:, width:]
        hidden = gate_sum / (1.0 + jnp.exp(-gate_sum)) * up_sum
        out[i * count:(i + 1) * count] = hidden.astype(out.dtype)


def combine(kept_a, came_a, last_a, kept_b, came_b, last_b, after, chunk):
    count, width = last_a.shape
    first = pl.BlockSpec((1, count, width), lambda i: (0, 0, 0))
    whole = pl.BlockSpec((count, width), lambda i: (0, 0))
    return pl.pallas_call(
        combine_kernel,
        out_shape=[jax.ShapeDtypeStruct((2 * count, width // 2), last_a.dtype), MARK],
        grid=(1,),
        in_specs=[first, first, whole] * 2 + [ANY_SPEC] * len(after),
        out_specs=[pl.BlockSpec((2 * count, width // 2), lambda i: (0, 0)), MARK_SPEC],
        compiler_params=pltpu.CompilerParams(vmem_limit_bytes=10 * MIB),
        cost_estimate=LITTLE,
        name=f"combine_{chunk}",
    )(kept_a, came_a, last_a, kept_b, came_b, last_b, *after)


def panel_product_kernel(own, other, weight, *refs):
    kept_a, sent_a, kept_b, sent_b, mark = refs[-5:]
    leave(mark)
    half = own.shape[1]
    product = jnp.dot(own[...], weight[0, :half], preferred_element_type=jnp.float32)
    product += jnp.dot(other[...], weight[0, half:], preferred_element_type=jnp.float32)
    product = product.astype(kept_a.dtype)
    count = product.shape[0] // 2
    part = pl.program_id(0)
    for flip in range(2):

        @pl.when(part % 2 == flip)
        def _():
            (sent_a if flip else kept_a)[0] = product[:count]

        @pl.when(part // 2 == flip)
        def _():
            (sent_b if flip else kept_b)[0] = product[count:]


def panel_product(own, other, dense, after, chunk):
    count, half = own.shape
    _, depth, width = dense.shape
    tile = width // 4
    out = jax.ShapeDtypeStruct((2, count // 2, tile), own.dtype)
    return pl.pallas_call(
        panel_product_kernel,
        out_shape=[out] * 4 + [MARK],
        grid=(4,),
        in_specs=[pl.BlockSpec((count, half), lambda n: (0, 0))] * 2
        + [pl.BlockSpec((1, depth, tile), lambda n: (0, 0, n))]
        + [ANY_SPEC] * len(after),
        out_specs=[
            pl.BlockSpec((1,) + out.shape[1:], lambda n: (n // 2, 0, 0)),
            pl.BlockSpec((1,) + out.shape[1:], lambda n: (n // 2, 0, 0)),
            pl.BlockSpec((1,) + out.shape[1:], lambda n: (jnp.minimum(n, 1), 0, 0)),
            pl.BlockSpec((1,) + out.shape[1:], lambda n: (jnp.maximum(n - 2, 0), 0, 0)),
            MARK_SPEC,
        ],
        compiler_params=pltpu.CompilerParams(vmem_limit_bytes=54 * MIB),
        cost_estimate=LITTLE,
        name=f"gate_up_{chunk}",
    )(own, other, dense, *after)


def down_steps_kernel(place, own, other, *refs, added, outputs):
    pieces = 2 * own.shape[0]
    weights, before = refs[:pieces], refs[pieces:pieces + added]
    outs, mark = refs[-1 - outputs:-1], refs[-1]
    leave(mark)
    count = own.shape[1] // len(outs)
    for step, out in enumerate(outs):
        at = 0 if len(outs) == 1 else (place[1] ^ step) * count
        rows = pl.ds(pl.multiple_of(at, count), count)
        total = 0.0
        for term in before:
            total += term[rows]
        for i in range(pieces // 2):
            for j, side in enumerate((own, other)):
                total += jnp.dot(
                    side[i, rows], weights[2 * i + j][0, 0], preferred_element_type=jnp.float32
                )
        out[...] = total.astype(out.dtype)


def down_steps(place, own, other, steps, dense, before, chunk, last, after):
    _, count, depth = own.shape
    width = dense.shape[-1]
    dense = dense.reshape(dense.shape[0], -1, depth, width)
    tile = width // 2
    tiles = pl.BlockSpec((count, tile), lambda n, *_: (0, n))
    whole = pl.BlockSpec(own.shape, lambda n, *_: (0, 0, 0))
    weights = []
    for step in steps:
        for flip in range(2):

            def at(n, place, step=step, flip=flip):
                return chunk, 2 * (place[0] ^ step) + (place[2] ^ flip), 0, n

            weights.append(pl.BlockSpec((1, 1, depth, tile), at))
    added = [] if before is None else [before]
    out, out_tiles = [jax.ShapeDtypeStruct((count, width), jnp.float32)], [tiles]
    if last:
        out = [jax.ShapeDtypeStruct((count // 4, width), own.dtype)] * 4
        out_tiles = [pl.BlockSpec((count // 4, tile), lambda n, *_: (0, n))] * 4
    return pl.pallas_call(
        functools.partial(down_steps_kernel, added=len(added), outputs=len(out)),
        out_shape=out + [MARK],
        grid_spec=pltpu.PrefetchScalarGridSpec(
            num_scalar_prefetch=1,
            grid=(width // tile,),
            in_specs=[whole, whole] + weights + [tiles] * len(added) + [ANY_SPEC],
            out_specs=out_tiles + [MARK_SPEC],
        ),
        compiler_params=pltpu.CompilerParams(vmem_limit_bytes=42 * MIB),
        cost_estimate=LITTLE,
        name=f"down_{chunk}_{steps[0]}",
    )(place, own, other, *[dense] * len(weights), *added, after)


def by_columns(
    tokens,
    norm_gain,
    gate_block_entries,
    gate_block_places,
    up_block_entries,
    up_block_places,
    down_values,
    down_slots,
):
    edge = gate_block_entries.shape[-1]
    tok_size = lax.axis_size("tok")
    col_size = lax.axis_size("col")
    rows_per = MODEL_WIDTH // edge // tok_size
    cols_per = HIDDEN_UNITS // edge // col_size
    width_blocks = MODEL_WIDTH // edge // col_size
    share = cols_per // tok_size
    chunks = 2
    cols = share // chunks
    count, half = tokens.shape
    tok, col = lax.axis_index("tok"), lax.axis_index("col")
    chip, side = col // 2, col % 2
    parts = range(tok_size)

    def swap_tok(array, step):
        return lax.ppermute(array, "tok", [(i, i ^ step) for i in parts])

    def swap_chip(array, step):
        return lax.ppermute(array, "col", [(i, i ^ (2 * step)) for i in range(col_size)])

    def swap_core(array):
        return lax.ppermute(array, "col", [(i, i ^ 1) for i in range(col_size)])

    def to_users(array, part):
        pairs = []
        for i in parts:
            for j in range(col_size):
                user = (j // 2) * col_size + 2 * (i ^ part) + j % 2
                pairs.append((i * col_size + j, user))
        return lax.ppermute(array, ("tok", "col"), pairs)

    squares = sum_squares(tokens)
    squares += swap_core(squares)
    squares += functools.reduce(jnp.add, [swap_chip(squares, step) for step in parts[1:]])
    scale = lax.rsqrt(squares.reshape(-1, 1) / MODEL_WIDTH + EPSILON)
    gain = lax.dynamic_slice_in_dim(norm_gain, col * half, half, 0)
    normed = (tokens.astype(jnp.float32) * scale * gain).astype(jnp.bfloat16)
    pieces = [to_users(normed, part) for part in parts]

    k, r, p, q = jnp.meshgrid(
        jnp.arange(chunks), jnp.arange(rows_per), jnp.arange(tok_size), jnp.arange(cols),
        indexing="ij",
    )
    row = (r + side * (rows_per // 2)) % rows_per
    slots = (row * cols_per + (p ^ tok) * share + k * cols + q).reshape(-1).astype(jnp.int32)
    gate_at = lookup(gate_block_places[0], slots)
    up_at = lookup(up_block_places[0], slots)
    slots = tok * share * width_blocks + jnp.arange(share * width_blocks, dtype=jnp.int32)
    down_at = lookup(down_slots, slots).reshape(-1)
    gate_at, up_at = gate_at.reshape(chunks, -1), up_at.reshape(chunks, -1)

    def spread(chunk, after):
        return spread_shares(
            gate_at[chunk], up_at[chunk], gate_block_entries, up_block_entries,
            rows_per, tok_size, cols, after, chunk,
        )

    dense, mark = spread(0, [])
    own = pack(pieces, [mark])
    other = swap_core(own)

    place = jnp.stack([chip, chip ^ tok, side])

    def send(hidden):
        far = swap_chip(hidden, 2)
        near = swap_chip(hidden, 1)
        inner = lax.ppermute(hidden, "col", [(i, i ^ 6) for i in range(2, 6)])
        ends = lax.ppermute(far, "col", [(i, i ^ 2) for i in range(2, 6)])
        return [hidden, near, far], [inner, ends]

    *sums, mark = panel_product(own, other, dense, [], 0)
    dense, mark = spread(1, [mark])
    mixed = None
    for chunk in range(2):
        kept_a, sent_a, kept_b, sent_b = sums
        came_a, came_b = swap_tok(sent_a, 1), swap_tok(sent_b, 2)
        if not chunk:
            *sums, mark = panel_product(own, other, dense, [mark], 1)
        last_a, last_b, mark = halfway(kept_a, came_a, kept_b, came_b, [mark], chunk)
        last_a, last_b = swap_tok(last_a, 2), swap_tok(last_b, 1)
        if chunk:
            held, mark = stack(early, (0, 1, 2), mark)
            mixed, mark = down_steps(
                place, held, swap_core(held), (0, 1, 2), down_dense, None, 0, False, mark
            )
            held, mark = stack(late, (3,), mark)
        hidden, mark = combine(kept_a, came_a, last_a, kept_b, came_b, last_b, [mark], chunk)
        if chunk:
            mixed, mark = down_steps(
                place, held, swap_core(held), (3,), down_dense, mixed, 0, False, mark
            )
        else:
            down_dense, mark = spread_panels(
                down_at, down_values, chunks, cols, width_blocks, [mark]
            )
        early, late = send(hidden)
    held, mark = stack(early, (0, 1, 2), mark)
    mixed, mark = down_steps(
        place, held, swap_core(held), (0, 1, 2), down_dense, mixed, 1, False, mark
    )
    held, mark = stack(late, (3,), mark)
    *mixed, _ = down_steps(place, held, swap_core(held), (3,), down_dense, mixed, 1, True, mark)

    total = mixed[0].astype(jnp.float32)
    for step in parts[1:]:
        total += swap_tok(mixed[step], step).astype(jnp.float32)
    return total.astype(jnp.bfloat16)


def shards(*arrays):
    tok_size = lax.axis_size("tok")
    col_size = lax.axis_size("col")
    blocks = HIDDEN_UNITS // arrays[2].shape[-1]
    even = blocks % (2 * col_size * tok_size) == 0 and col_size == 2 * tok_size == 8
    return (by_columns if even else by_tokens)(*arrays)


def solution(mesh):
    return jax.shard_map(
        shards,
        mesh=mesh,
        in_specs=(
            P("tok", "col"),
            P(),
            P("tok", "col", None, None),
            P("tok", "col"),
            P("tok", "col", None, None),
            P("tok", "col"),
            P(None, "col", None, None),
            P(None, "col"),
        ),
        out_specs=P("tok", "col"),
        check_vma=False,
    )
```

```python
import functools

import jax
import jax.numpy as jnp
from jax import lax
from jax.experimental import pallas as pl
from jax.experimental.pallas import tpu as pltpu
from jax.sharding import PartitionSpec as P

MODEL_WIDTH = 8192
HIDDEN_UNITS = 24576

EPSILON = 1e-05
MIB = 1 << 20
MARK = jax.ShapeDtypeStruct((8, 128), jnp.float32)
MARK_SPEC = pl.BlockSpec(MARK.shape, lambda *_: (0, 0))
ANY_SPEC = pl.BlockSpec(memory_space=pl.ANY)
LITTLE = pl.CostEstimate(flops=1, bytes_accessed=1, transcendentals=0)


def leave(mark):
    mark[...] = jnp.zeros_like(mark)


def lookup(places, slots):
    hit = places[..., None, :] == slots[:, None]
    entry = jnp.arange(places.shape[-1], dtype=jnp.int32)
    return jnp.max(jnp.where(hit, entry, -1), axis=-1)


def put(out_ref, row, col, source_ref, entry):
    edge = source_ref.shape[-1]
    block = source_ref[0, jnp.maximum(entry, 0)]
    block = jnp.where(entry >= 0, block, jnp.zeros_like(block))
    out_ref[0, pl.ds(pl.multiple_of(row * edge, edge), edge), col * edge:(col + 1) * edge] = block


def spread_gate_up_kernel(gate_at, up_at, gate_ref, up_ref, out_ref, *, rows, cols):
    chunk = pl.program_id(0)

    @pl.loop(0, rows)
    def _(row):
        for col in range(cols):
            at = (chunk * rows + row) * cols + col
            put(out_ref, row, col, gate_ref, gate_at[at])
            put(out_ref, row, cols + col, up_ref, up_at[at])


def spread_gate_up(gate_at, up_at, gate, up, chunks, rows, cols):
    edge = gate.shape[-1]
    whole = pl.BlockSpec(gate.shape, lambda k, *_: (0, 0, 0, 0), pipeline_mode=pl.Buffered(1))
    out = jax.ShapeDtypeStruct((chunks, rows * edge, 2 * cols * edge), gate.dtype)
    return pl.pallas_call(
        functools.partial(spread_gate_up_kernel, rows=rows, cols=cols),
        out_shape=out,
        grid_spec=pltpu.PrefetchScalarGridSpec(
            num_scalar_prefetch=2,
            grid=(chunks,),
            in_specs=[whole, whole],
            out_specs=pl.BlockSpec((1,) + out.shape[1:], lambda k, *_: (k, 0, 0)),
        ),
        compiler_params=pltpu.CompilerParams(vmem_limit_bytes=48 * MIB),
        cost_estimate=pl.CostEstimate(
            flops=0, bytes_accessed=2 * (2 * gate.size + out.size), transcendentals=0
        ),
        name="spread_gate_up",
    )(gate_at, up_at, gate, up)


def spread_down_kernel(at_ref, values_ref, out_ref, *, rows, cols):
    panel, chunk = pl.program_id(0), pl.program_id(1)
    base = (panel * pl.num_programs(1) + chunk) * rows * cols

    @pl.loop(0, rows)
    def _(row):
        for col in range(cols):
            put(out_ref.at[0], row, col, values_ref, at_ref[base + row * cols + col])


def spread_down(at, values, chunks, rows, cols):
    panels, _, edge, _ = values.shape
    out = jax.ShapeDtypeStruct((chunks, panels, rows * edge, cols * edge), values.dtype)
    return pl.pallas_call(
        functools.partial(spread_down_kernel, rows=rows, cols=cols),
        out_shape=out,
        grid_spec=pltpu.PrefetchScalarGridSpec(
            num_scalar_prefetch=1,
            grid=(panels, chunks),
            in_specs=[pl.BlockSpec((1,) + values.shape[1:], lambda g, k, *_: (g, 0, 0, 0))],
            out_specs=pl.BlockSpec((1, 1) + out.shape[2:], lambda g, k, *_: (k, g, 0, 0)),
        ),
        compiler_params=pltpu.CompilerParams(vmem_limit_bytes=48 * MIB),
        cost_estimate=pl.CostEstimate(
            flops=0, bytes_accessed=2 * (values.size + out.size), transcendentals=0
        ),
        name="spread_down",
    )(at, values)


def gate_up_kernel(*refs, parts):
    own, other = refs[:parts], refs[parts:2 * parts]
    weight = refs[2 * parts]
    outs, held = refs[2 * parts + 1:3 * parts + 1], refs[-1]
    count, half = own[0].shape

    @pl.when(pl.program_id(0) == 0)
    def _():
        for part in range(parts):
            rows = slice(part * count, (part + 1) * count)
            held[rows, :half] = own[part][...]
            held[rows, half:] = other[part][...]

    product = jnp.dot(held[...], weight[0], preferred_element_type=jnp.float32)
    for part in range(parts):
        outs[part][...] = product[part * count:(part + 1) * count].astype(outs[part].dtype)


def gate_up(own, other, dense, chunk):
    parts = len(own)
    count, half = own[0].shape
    _, depth, width = dense.shape
    tile = 256
    out = jax.ShapeDtypeStruct((count, width), own[0].dtype)
    return pl.pallas_call(
        functools.partial(gate_up_kernel, parts=parts),
        out_shape=[out] * parts,
        grid=(width // tile,),
        in_specs=[pl.BlockSpec((count, half), lambda n: (0, 0))] * (2 * parts)
        + [pl.BlockSpec((1, depth, tile), lambda n: (chunk, 0, n))],
        out_specs=[pl.BlockSpec((count, tile), lambda n: (0, n))] * parts,
        scratch_shapes=[pltpu.VMEM((parts * count, 2 * half), own[0].dtype)],
        compiler_params=pltpu.CompilerParams(vmem_limit_bytes=32 * MIB),
        cost_estimate=pl.CostEstimate(
            flops=2 * parts * count * depth * width,
            bytes_accessed=2 * (depth * width + parts * count * (depth + width)),
            transcendentals=0,
        ),
        name=f"gate_up_{chunk}",
    )(*own, *other, dense)


def down_kernel(hidden_ref, weight_ref, before_ref, out_ref, total):
    panel = pl.program_id(0)

    @pl.when(panel == 0)
    def _():
        total[...] = before_ref[...]

    total[...] += jnp.dot(hidden_ref[0], weight_ref[0, 0], preferred_element_type=jnp.float32)

    @pl.when(panel == pl.num_programs(0) - 1)
    def _():
        out_ref[...] = total[...].astype(out_ref.dtype)


def down(hidden, dense, before, chunk, dtype):
    panels, count, depth = hidden.shape
    width = dense.shape[-1]
    return pl.pallas_call(
        down_kernel,
        out_shape=jax.ShapeDtypeStruct((count, width), dtype),
        grid=(panels,),
        in_specs=[
            pl.BlockSpec((1, count, depth), lambda g: (g, 0, 0)),
            pl.BlockSpec((1, 1, depth, width), lambda g: (chunk, g, 0, 0)),
            pl.BlockSpec((count, width), lambda g: (0, 0)),
        ],
        out_specs=pl.BlockSpec((count, width), lambda g: (0, 0)),
        scratch_shapes=[pltpu.VMEM((count, width), jnp.float32)],
        compiler_params=pltpu.CompilerParams(vmem_limit_bytes=32 * MIB),
        cost_estimate=pl.CostEstimate(
            flops=2 * panels * count * depth * width,
            bytes_accessed=2 * panels * depth * (width + count) + 6 * count * width,
            transcendentals=0,
        ),
        name=f"down_{chunk}",
    )(hidden, dense, before)


def by_tokens(
    tokens,
    norm_gain,
    gate_block_entries,
    gate_block_places,
    up_block_entries,
    up_block_places,
    down_values,
    down_slots,
):
    edge = gate_block_entries.shape[-1]
    tok_size = lax.axis_size("tok")
    col_size = lax.axis_size("col")
    rows_per = MODEL_WIDTH // edge // tok_size
    cols_per = HIDDEN_UNITS // edge // col_size
    width_blocks = MODEL_WIDTH // edge // col_size
    chunks = 4 if cols_per % 4 == 0 else 1
    chunk_cols = cols_per // chunks
    count, features = tokens.shape
    half = MODEL_WIDTH // tok_size // 2
    tok, col = lax.axis_index("tok"), lax.axis_index("col")
    side = col % 2

    def swap_tok(array, step):
        return lax.ppermute(array, "tok", [(i, i ^ step) for i in range(tok_size)])

    def swap_core(array):
        return lax.ppermute(array, "col", [(i, i ^ 1) for i in range(col_size)])

    k, r, q = jnp.meshgrid(
        jnp.arange(chunks), jnp.arange(rows_per), jnp.arange(chunk_cols), indexing="ij"
    )
    row = (r + side * (rows_per // 2)) % rows_per
    slots = (row * cols_per + k * chunk_cols + q).reshape(-1).astype(jnp.int32)
    gate_at = lookup(gate_block_places[0], slots)
    up_at = lookup(up_block_places[0], slots)
    down_at = lookup(down_slots, jnp.arange(cols_per * width_blocks, dtype=jnp.int32)).reshape(-1)

    gathered = lax.all_gather(tokens, "col")
    dense = spread_gate_up(
        gate_at, up_at, gate_block_entries, up_block_entries, chunks, rows_per, chunk_cols
    )
    down_dense = spread_down(down_at, down_values, chunks, chunk_cols, width_blocks)

    widened = gathered.astype(jnp.float32)
    mean_square = jnp.mean(widened * widened, axis=(0, 2))[:, None]
    scale = lax.rsqrt(mean_square + EPSILON)
    subs = half // features

    def normed(panel):
        at = panel * 2 + side
        piece = lax.dynamic_slice_in_dim(gathered, at * subs, subs, 0)
        piece = piece.transpose(1, 0, 2).reshape(count, half).astype(jnp.float32)
        gain = lax.dynamic_slice_in_dim(norm_gain, at * half, half, 0)
        return (piece * scale * gain).astype(jnp.bfloat16)

    own = [normed(tok ^ part) for part in range(tok_size)]
    own = [own[0]] + [swap_tok(own[part], part) for part in range(1, tok_size)]
    other = [swap_core(part) for part in own]

    hiddens, halves = [], []
    for chunk in range(chunks):
        sums = gate_up(own, other, dense, chunk)
        terms = [sums[0]] + [swap_tok(sums[part], part) for part in range(1, tok_size)]
        total = functools.reduce(jnp.add, [term.astype(jnp.float32) for term in terms])
        gate_sum, up_sum = jnp.split(total, 2, axis=1)
        hiddens.append((jax.nn.silu(gate_sum) * up_sum).astype(jnp.bfloat16))

    mixed = jnp.zeros((count, width_blocks * edge), jnp.float32)
    for chunk in range(chunks):
        hidden = lax.all_gather(hiddens[chunk], "col")
        last = chunk == chunks - 1
        mixed = down(hidden, down_dense, mixed, chunk, jnp.bfloat16 if last else jnp.float32)
    return mixed

def spread_shares_kernel(gate_at, up_at, *refs, rows, shares, cols):
    (gate_ref, up_ref), (out_ref, mark) = refs[:2], refs[-2:]
    step = pl.program_id(0)
    leave(mark)

    @pl.loop(0, rows)
    def _(row):
        for share in range(shares):
            for col in range(cols):
                at = ((step * rows + row) * shares + share) * cols + col
                put(out_ref, row, 2 * share * cols + col, gate_ref, gate_at[at])
                put(out_ref, row, (2 * share + 1) * cols + col, up_ref, up_at[at])


def spread_shares(gate_at, up_at, gate, up, rows, shares, cols, after, chunk):
    edge = gate.shape[-1]
    steps = 4
    whole = pl.BlockSpec(gate.shape, lambda k, *_: (0, 0, 0, 0), pipeline_mode=pl.Buffered(1))
    out = jax.ShapeDtypeStruct((1, rows * edge, 2 * shares * cols * edge), gate.dtype)
    block = (1, out.shape[1] // steps, out.shape[2])
    return pl.pallas_call(
        functools.partial(spread_shares_kernel, rows=rows // steps, shares=shares, cols=cols),
        out_shape=[out, MARK],
        grid_spec=pltpu.PrefetchScalarGridSpec(
            num_scalar_prefetch=2,
            grid=(steps,),
            in_specs=[whole, whole] + [ANY_SPEC] * len(after),
            out_specs=[pl.BlockSpec(block, lambda k, *_: (0, k, 0)), MARK_SPEC],
        ),
        compiler_params=pltpu.CompilerParams(vmem_limit_bytes=54 * MIB),
        cost_estimate=LITTLE,
        name=f"spread_gate_up_{chunk}",
    )(gate_at, up_at, gate, up, *after)


def spread_panels_kernel(at_ref, values_ref, *refs, chunks, rows, cols):
    out_ref, mark = refs[-2:]
    panel = pl.program_id(0)
    leave(mark)
    for chunk in range(chunks):
        for row in range(rows):
            for col in range(cols):
                at = ((panel * chunks + chunk) * rows + row) * cols + col
                put(out_ref.at[pl.ds(chunk, 1)], row, col, values_ref, at_ref[at])


def spread_panels(at, values, chunks, rows, cols, after):
    count, _, edge, _ = values.shape
    out = jax.ShapeDtypeStruct((chunks, count * rows * edge, cols * edge), values.dtype)
    return pl.pallas_call(
        functools.partial(spread_panels_kernel, chunks=chunks, rows=rows, cols=cols),
        out_shape=[out, MARK],
        grid_spec=pltpu.PrefetchScalarGridSpec(
            num_scalar_prefetch=1,
            grid=(count,),
            in_specs=[
                pl.BlockSpec((1,) + values.shape[1:], lambda m, *_: (m, 0, 0, 0))
            ]
            + [ANY_SPEC] * len(after),
            out_specs=[
                pl.BlockSpec((chunks, rows * edge, cols * edge), lambda m, *_: (0, m, 0)),
                MARK_SPEC,
            ],
        ),
        compiler_params=pltpu.CompilerParams(vmem_limit_bytes=50 * MIB),
        cost_estimate=LITTLE,
        name="spread_down",
    )(at, values, *after)

def sum_squares_kernel(tokens, out):
    widened = tokens[...].astype(jnp.float32)
    out[...] = jnp.sum(widened * widened, axis=1)[None]


def sum_squares(tokens):
    return pl.pallas_call(
        sum_squares_kernel,
        out_shape=jax.ShapeDtypeStruct((1, tokens.shape[0]), jnp.float32),
        in_specs=[pl.BlockSpec(memory_space=pltpu.VMEM)],
        out_specs=pl.BlockSpec(memory_space=pltpu.VMEM),
        compiler_params=pltpu.CompilerParams(vmem_limit_bytes=4 * MIB),
        name="sum_squares",
    )(tokens)


def pack_kernel(*refs, parts):
    count = refs[0].shape[0]
    for part in range(parts):
        refs[-1][part * count:(part + 1) * count] = refs[part][...]


def pack(pieces, after):
    parts = len(pieces)
    count, width = pieces[0].shape
    return pl.pallas_call(
        functools.partial(pack_kernel, parts=parts),
        out_shape=jax.ShapeDtypeStruct((parts * count, width), pieces[0].dtype),
        in_specs=[pl.BlockSpec(memory_space=pltpu.VMEM)] * parts + [ANY_SPEC] * len(after),
        out_specs=pl.BlockSpec(memory_space=pltpu.VMEM),
        compiler_params=pltpu.CompilerParams(vmem_limit_bytes=16 * MIB),
        cost_estimate=LITTLE,
        name="pack",
    )(*pieces, *after)


def hold_kernel(*refs):
    leave(refs[-1])


def hold(arrays, after):
    count = len(arrays)
    *arrays, _ = pl.pallas_call(
        hold_kernel,
        out_shape=[jax.ShapeDtypeStruct(array.shape, array.dtype) for array in arrays] + [MARK],
        in_specs=[ANY_SPEC] * (count + len(after)),
        out_specs=[ANY_SPEC] * count + [pl.BlockSpec(memory_space=pltpu.VMEM)],
        input_output_aliases={i: i for i in range(count)},
        cost_estimate=LITTLE,
        name="hold",
    )(*arrays, *after)
    return arrays


def stack_kernel(*refs, steps):
    pieces, out, mark = refs[:-3], refs[-2], refs[-1]
    leave(mark)
    count = out.shape[1] // 4
    for i, step in enumerate(steps):
        for part in range(4):
            there = slice((part ^ step) * count, ((part ^ step) + 1) * count)
            rows = pieces[i][there]
            if i + 1 == len(steps) < len(pieces):
                rows += pieces[i + 1][there]
            out[i, part * count:(part + 1) * count] = rows


def stack(pieces, steps, after):
    return pl.pallas_call(
        functools.partial(stack_kernel, steps=steps),
        out_shape=[jax.ShapeDtypeStruct((len(steps),) + pieces[0].shape, pieces[0].dtype), MARK],
        in_specs=[pl.BlockSpec(memory_space=pltpu.VMEM)] * len(pieces) + [ANY_SPEC],
        out_specs=[pl.BlockSpec(memory_space=pltpu.VMEM)] * 2,
        compiler_params=pltpu.CompilerParams(vmem_limit_bytes=16 * MIB),
        cost_estimate=LITTLE,
        name="stack",
    )(*pieces, after)


def halfway_kernel(kept_a, came_a, kept_b, came_b, *refs):
    out_a, out_b, mark = refs[-3:]
    leave(mark)
    for kept, came, out in ((kept_a, came_a, out_a), (kept_b, came_b, out_b)):
        out[...] = (kept[0].astype(jnp.float32) + came[0].astype(jnp.float32)).astype(out.dtype)


def halfway(kept_a, came_a, kept_b, came_b, after, chunk):
    _, count, width = kept_a.shape
    second = pl.BlockSpec((1, count, width), lambda i: (1, 0, 0))
    whole = pl.BlockSpec((count, width), lambda i: (0, 0))
    out = jax.ShapeDtypeStruct((count, width), kept_a.dtype)
    return pl.pallas_call(
        halfway_kernel,
        out_shape=[out, out, MARK],
        grid=(1,),
        in_specs=[second] * 4 + [ANY_SPEC] * len(after),
        out_specs=[whole, whole, MARK_SPEC],
        compiler_params=pltpu.CompilerParams(vmem_limit_bytes=8 * MIB),
        cost_estimate=LITTLE,
        name=f"halfway_{chunk}",
    )(kept_a, came_a, kept_b, came_b, *after)


def combine_kernel(*refs):
    terms, out, mark = refs[:6], refs[-2], refs[-1]
    leave(mark)
    count = out.shape[0] // 2
    width = out.shape[1]
    for i in range(2):
        kept, came, last = terms[3 * i:3 * i + 3]
        total = kept[0].astype(jnp.float32) + came[0].astype(jnp.float32)
        total += last[...].astype(jnp.float32)
        gate_sum, up_sum = total[:, :width], total[:, width:]
        hidden = gate_sum / (1.0 + jnp.exp(-gate_sum)) * up_sum
        out[i * count:(i + 1) * count] = hidden.astype(out.dtype)


def combine(kept_a, came_a, last_a, kept_b, came_b, last_b, after, chunk):
    count, width = last_a.shape
    first = pl.BlockSpec((1, count, width), lambda i: (0, 0, 0))
    whole = pl.BlockSpec((count, width), lambda i: (0, 0))
    return pl.pallas_call(
        combine_kernel,
        out_shape=[jax.ShapeDtypeStruct((2 * count, width // 2), last_a.dtype), MARK],
        grid=(1,),
        in_specs=[first, first, whole] * 2 + [ANY_SPEC] * len(after),
        out_specs=[pl.BlockSpec((2 * count, width // 2), lambda i: (0, 0)), MARK_SPEC],
        compiler_params=pltpu.CompilerParams(vmem_limit_bytes=10 * MIB),
        cost_estimate=LITTLE,
        name=f"combine_{chunk}",
    )(kept_a, came_a, last_a, kept_b, came_b, last_b, *after)


def panel_product_kernel(own, other, weight, *refs):
    kept_a, sent_a, kept_b, sent_b, mark = refs[-5:]
    leave(mark)
    half = own.shape[1]
    product = jnp.dot(own[...], weight[0, :half], preferred_element_type=jnp.float32)
    product += jnp.dot(other[...], weight[0, half:], preferred_element_type=jnp.float32)
    product = product.astype(kept_a.dtype)
    count = product.shape[0] // 2
    part = pl.program_id(0)
    for flip in range(2):

        @pl.when(part % 2 == flip)
        def _():
            (sent_a if flip else kept_a)[0] = product[:count]

        @pl.when(part // 2 == flip)
        def _():
            (sent_b if flip else kept_b)[0] = product[count:]


def panel_product(own, other, dense, after, chunk):
    count, half = own.shape
    _, depth, width = dense.shape
    tile = width // 4
    out = jax.ShapeDtypeStruct((2, count // 2, tile), own.dtype)
    return pl.pallas_call(
        panel_product_kernel,
        out_shape=[out] * 4 + [MARK],
        grid=(4,),
        in_specs=[pl.BlockSpec((count, half), lambda n: (0, 0))] * 2
        + [pl.BlockSpec((1, depth, tile), lambda n: (0, 0, n))]
        + [ANY_SPEC] * len(after),
        out_specs=[
            pl.BlockSpec((1,) + out.shape[1:], lambda n: (n // 2, 0, 0)),
            pl.BlockSpec((1,) + out.shape[1:], lambda n: (n // 2, 0, 0)),
            pl.BlockSpec((1,) + out.shape[1:], lambda n: (jnp.minimum(n, 1), 0, 0)),
            pl.BlockSpec((1,) + out.shape[1:], lambda n: (jnp.maximum(n - 2, 0), 0, 0)),
            MARK_SPEC,
        ],
        compiler_params=pltpu.CompilerParams(vmem_limit_bytes=54 * MIB),
        cost_estimate=LITTLE,
        name=f"gate_up_{chunk}",
    )(own, other, dense, *after)


def down_steps_kernel(place, own, other, *refs, added, outputs):
    pieces = 2 * own.shape[0]
    weights, before = refs[:pieces], refs[pieces:pieces + added]
    outs, mark = refs[-1 - outputs:-1], refs[-1]
    leave(mark)
    count = own.shape[1] // len(outs)
    for step, out in enumerate(outs):
        at = 0 if len(outs) == 1 else (place[1] ^ step) * count
        rows = pl.ds(pl.multiple_of(at, count), count)
        total = 0.0
        for term in before:
            total += term[rows]
        for i in range(pieces // 2):
            for j, side in enumerate((own, other)):
                total += jnp.dot(
                    side[i, rows], weights[2 * i + j][0, 0], preferred_element_type=jnp.float32
                )
        out[...] = total.astype(out.dtype)


def down_steps(place, own, other, steps, dense, before, chunk, last, after):
    _, count, depth = own.shape
    width = dense.shape[-1]
    dense = dense.reshape(dense.shape[0], -1, depth, width)
    tile = width // 2
    tiles = pl.BlockSpec((count, tile), lambda n, *_: (0, n))
    whole = pl.BlockSpec(own.shape, lambda n, *_: (0, 0, 0))
    weights = []
    for step in steps:
        for flip in range(2):

            def at(n, place, step=step, flip=flip):
                return chunk, 2 * (place[0] ^ step) + (place[2] ^ flip), 0, n

            weights.append(pl.BlockSpec((1, 1, depth, tile), at))
    added = [] if before is None else [before]
    out, out_tiles = [jax.ShapeDtypeStruct((count, width), jnp.float32)], [tiles]
    if last:
        out = [jax.ShapeDtypeStruct((count // 4, width), own.dtype)] * 4
        out_tiles = [pl.BlockSpec((count // 4, tile), lambda n, *_: (0, n))] * 4
    return pl.pallas_call(
        functools.partial(down_steps_kernel, added=len(added), outputs=len(out)),
        out_shape=out + [MARK],
        grid_spec=pltpu.PrefetchScalarGridSpec(
            num_scalar_prefetch=1,
            grid=(width // tile,),
            in_specs=[whole, whole] + weights + [tiles] * len(added) + [ANY_SPEC],
            out_specs=out_tiles + [MARK_SPEC],
        ),
        compiler_params=pltpu.CompilerParams(vmem_limit_bytes=42 * MIB),
        cost_estimate=LITTLE,
        name=f"down_{chunk}_{steps[0]}",
    )(place, own, other, *[dense] * len(weights), *added, after)


def by_columns(
    tokens,
    norm_gain,
    gate_block_entries,
    gate_block_places,
    up_block_entries,
    up_block_places,
    down_values,
    down_slots,
):
    edge = gate_block_entries.shape[-1]
    tok_size = lax.axis_size("tok")
    col_size = lax.axis_size("col")
    rows_per = MODEL_WIDTH // edge // tok_size
    cols_per = HIDDEN_UNITS // edge // col_size
    width_blocks = MODEL_WIDTH // edge // col_size
    share = cols_per // tok_size
    chunks = 2
    cols = share // chunks
    count, half = tokens.shape
    tok, col = lax.axis_index("tok"), lax.axis_index("col")
    chip, side = col // 2, col % 2
    parts = range(tok_size)

    def swap_tok(array, step):
        return lax.ppermute(array, "tok", [(i, i ^ step) for i in parts])

    def swap_chip(array, step):
        return lax.ppermute(array, "col", [(i, i ^ (2 * step)) for i in range(col_size)])

    def swap_core(array):
        return lax.ppermute(array, "col", [(i, i ^ 1) for i in range(col_size)])

    def to_users(array, part):
        pairs = []
        for i in parts:
            for j in range(col_size):
                user = (j // 2) * col_size + 2 * (i ^ part) + j % 2
                pairs.append((i * col_size + j, user))
        return lax.ppermute(array, ("tok", "col"), pairs)

    squares = sum_squares(tokens)
    squares += swap_core(squares)
    squares += functools.reduce(jnp.add, [swap_chip(squares, step) for step in parts[1:]])
    scale = lax.rsqrt(squares.reshape(-1, 1) / MODEL_WIDTH + EPSILON)
    gain = lax.dynamic_slice_in_dim(norm_gain, col * half, half, 0)
    normed = (tokens.astype(jnp.float32) * scale * gain).astype(jnp.bfloat16)
    pieces = [to_users(normed, part) for part in parts]

    k, r, p, q = jnp.meshgrid(
        jnp.arange(chunks), jnp.arange(rows_per), jnp.arange(tok_size), jnp.arange(cols),
        indexing="ij",
    )
    row = (r + side * (rows_per // 2)) % rows_per
    slots = (row * cols_per + (p ^ tok) * share + k * cols + q).reshape(-1).astype(jnp.int32)
    gate_at = lookup(gate_block_places[0], slots)
    up_at = lookup(up_block_places[0], slots)
    slots = tok * share * width_blocks + jnp.arange(share * width_blocks, dtype=jnp.int32)
    down_at = lookup(down_slots, slots).reshape(-1)
    gate_at, up_at = gate_at.reshape(chunks, -1), up_at.reshape(chunks, -1)

    def spread(chunk, after):
        return spread_shares(
            gate_at[chunk], up_at[chunk], gate_block_entries, up_block_entries,
            rows_per, tok_size, cols, after, chunk,
        )

    dense, mark = spread(0, [])
    own = pack(pieces, [mark])
    other = swap_core(own)

    place = jnp.stack([chip, chip ^ tok, side])

    def send(hidden):
        far = swap_chip(hidden, 2)
        near = swap_chip(hidden, 1)
        inner = lax.ppermute(hidden, "col", [(i, i ^ 6) for i in range(2, 6)])
        ends = lax.ppermute(far, "col", [(i, i ^ 2) for i in range(2, 6)])
        return [hidden, near, far], [inner, ends]

    *sums, mark = panel_product(own, other, dense, [], 0)
    dense, mark = spread(1, [mark])
    mixed = None
    for chunk in range(2):
        kept_a, sent_a, kept_b, sent_b = sums
        came_a, came_b = swap_tok(sent_a, 1), swap_tok(sent_b, 2)
        last_a, last_b, mark = halfway(kept_a, came_a, kept_b, came_b, [mark], chunk)
        last_a, last_b = swap_tok(last_a, 2), swap_tok(last_b, 1)
        if chunk:
            held, mark = stack(early, (0, 1, 2), mark)
            mixed, mark = down_steps(
                place, held, swap_core(held), (0, 1, 2), down_dense, None, 0, False, mark
            )
            held, mark = stack(late, (3,), mark)
        else:
            *sums, mark = panel_product(own, other, dense, [mark], 1)
        hidden, mark = combine(kept_a, came_a, last_a, kept_b, came_b, last_b, [mark], chunk)
        if chunk:
            mixed, mark = down_steps(
                place, held, swap_core(held), (3,), down_dense, mixed, 0, False, mark
            )
        else:
            kept_a, sent_a, kept_b, sent_b = sums
            sent_a, sent_b = hold([sent_a, sent_b], [mark])
            sums = kept_a, sent_a, kept_b, sent_b
            down_dense, mark = spread_panels(
                down_at, down_values, chunks, cols, width_blocks, [mark]
            )
        early, late = send(hidden)
    held, mark = stack(early, (0, 1, 2), mark)
    mixed, mark = down_steps(
        place, held, swap_core(held), (0, 1, 2), down_dense, mixed, 1, False, mark
    )
    held, mark = stack(late, (3,), mark)
    *mixed, _ = down_steps(place, held, swap_core(held), (3,), down_dense, mixed, 1, True, mark)

    total = mixed[0].astype(jnp.float32)
    for step in parts[1:]:
        total += swap_tok(mixed[step], step).astype(jnp.float32)
    return total.astype(jnp.bfloat16)


def shards(*arrays):
    tok_size = lax.axis_size("tok")
    col_size = lax.axis_size("col")
    blocks = HIDDEN_UNITS // arrays[2].shape[-1]
    even = blocks % (2 * col_size * tok_size) == 0 and col_size == 2 * tok_size == 8
    return (by_columns if even else by_tokens)(*arrays)


def solution(mesh):
    return jax.shard_map(
        shards,
        mesh=mesh,
        in_specs=(
            P("tok", "col"),
            P(),
            P("tok", "col", None, None),
            P("tok", "col"),
            P("tok", "col", None, None),
            P("tok", "col"),
            P(None, "col", None, None),
            P(None, "col"),
        ),
        out_specs=P("tok", "col"),
        check_vma=False,
    )
```

```python
import functools

import jax
import jax.numpy as jnp
from jax import lax
from jax.experimental import pallas as pl
from jax.experimental.pallas import tpu as pltpu
from jax.sharding import PartitionSpec as P

MODEL_WIDTH = 8192
HIDDEN_UNITS = 24576

EPSILON = 1e-05
MIB = 1 << 20
MARK = jax.ShapeDtypeStruct((8, 128), jnp.float32)
MARK_SPEC = pl.BlockSpec(MARK.shape, lambda *_: (0, 0))
ANY_SPEC = pl.BlockSpec(memory_space=pl.ANY)
LITTLE = pl.CostEstimate(flops=1, bytes_accessed=1, transcendentals=0)


def leave(mark):
    mark[...] = jnp.zeros_like(mark)


def lookup(places, slots):
    hit = places[..., None, :] == slots[:, None]
    entry = jnp.arange(places.shape[-1], dtype=jnp.int32)
    return jnp.max(jnp.where(hit, entry, -1), axis=-1)


def put(out_ref, row, col, source_ref, entry):
    edge = source_ref.shape[-1]
    block = source_ref[0, jnp.maximum(entry, 0)]
    block = jnp.where(entry >= 0, block, jnp.zeros_like(block))
    out_ref[0, pl.ds(pl.multiple_of(row * edge, edge), edge), col * edge:(col + 1) * edge] = block


def spread_gate_up_kernel(gate_at, up_at, gate_ref, up_ref, out_ref, *, rows, cols):
    chunk = pl.program_id(0)

    @pl.loop(0, rows)
    def _(row):
        for col in range(cols):
            at = (chunk * rows + row) * cols + col
            put(out_ref, row, col, gate_ref, gate_at[at])
            put(out_ref, row, cols + col, up_ref, up_at[at])


def spread_gate_up(gate_at, up_at, gate, up, chunks, rows, cols):
    edge = gate.shape[-1]
    whole = pl.BlockSpec(gate.shape, lambda k, *_: (0, 0, 0, 0), pipeline_mode=pl.Buffered(1))
    out = jax.ShapeDtypeStruct((chunks, rows * edge, 2 * cols * edge), gate.dtype)
    return pl.pallas_call(
        functools.partial(spread_gate_up_kernel, rows=rows, cols=cols),
        out_shape=out,
        grid_spec=pltpu.PrefetchScalarGridSpec(
            num_scalar_prefetch=2,
            grid=(chunks,),
            in_specs=[whole, whole],
            out_specs=pl.BlockSpec((1,) + out.shape[1:], lambda k, *_: (k, 0, 0)),
        ),
        compiler_params=pltpu.CompilerParams(vmem_limit_bytes=48 * MIB),
        cost_estimate=pl.CostEstimate(
            flops=0, bytes_accessed=2 * (2 * gate.size + out.size), transcendentals=0
        ),
        name="spread_gate_up",
    )(gate_at, up_at, gate, up)


def spread_down_kernel(at_ref, values_ref, out_ref, *, rows, cols):
    panel, chunk = pl.program_id(0), pl.program_id(1)
    base = (panel * pl.num_programs(1) + chunk) * rows * cols

    @pl.loop(0, rows)
    def _(row):
        for col in range(cols):
            put(out_ref.at[0], row, col, values_ref, at_ref[base + row * cols + col])


def spread_down(at, values, chunks, rows, cols):
    panels, _, edge, _ = values.shape
    out = jax.ShapeDtypeStruct((chunks, panels, rows * edge, cols * edge), values.dtype)
    return pl.pallas_call(
        functools.partial(spread_down_kernel, rows=rows, cols=cols),
        out_shape=out,
        grid_spec=pltpu.PrefetchScalarGridSpec(
            num_scalar_prefetch=1,
            grid=(panels, chunks),
            in_specs=[pl.BlockSpec((1,) + values.shape[1:], lambda g, k, *_: (g, 0, 0, 0))],
            out_specs=pl.BlockSpec((1, 1) + out.shape[2:], lambda g, k, *_: (k, g, 0, 0)),
        ),
        compiler_params=pltpu.CompilerParams(vmem_limit_bytes=48 * MIB),
        cost_estimate=pl.CostEstimate(
            flops=0, bytes_accessed=2 * (values.size + out.size), transcendentals=0
        ),
        name="spread_down",
    )(at, values)


def gate_up_kernel(*refs, parts):
    own, other = refs[:parts], refs[parts:2 * parts]
    weight = refs[2 * parts]
    outs, held = refs[2 * parts + 1:3 * parts + 1], refs[-1]
    count, half = own[0].shape

    @pl.when(pl.program_id(0) == 0)
    def _():
        for part in range(parts):
            rows = slice(part * count, (part + 1) * count)
            held[rows, :half] = own[part][...]
            held[rows, half:] = other[part][...]

    product = jnp.dot(held[...], weight[0], preferred_element_type=jnp.float32)
    for part in range(parts):
        outs[part][...] = product[part * count:(part + 1) * count].astype(outs[part].dtype)


def gate_up(own, other, dense, chunk):
    parts = len(own)
    count, half = own[0].shape
    _, depth, width = dense.shape
    tile = 256
    out = jax.ShapeDtypeStruct((count, width), own[0].dtype)
    return pl.pallas_call(
        functools.partial(gate_up_kernel, parts=parts),
        out_shape=[out] * parts,
        grid=(width // tile,),
        in_specs=[pl.BlockSpec((count, half), lambda n: (0, 0))] * (2 * parts)
        + [pl.BlockSpec((1, depth, tile), lambda n: (chunk, 0, n))],
        out_specs=[pl.BlockSpec((count, tile), lambda n: (0, n))] * parts,
        scratch_shapes=[pltpu.VMEM((parts * count, 2 * half), own[0].dtype)],
        compiler_params=pltpu.CompilerParams(vmem_limit_bytes=32 * MIB),
        cost_estimate=pl.CostEstimate(
            flops=2 * parts * count * depth * width,
            bytes_accessed=2 * (depth * width + parts * count * (depth + width)),
            transcendentals=0,
        ),
        name=f"gate_up_{chunk}",
    )(*own, *other, dense)


def down_kernel(hidden_ref, weight_ref, before_ref, out_ref, total):
    panel = pl.program_id(0)

    @pl.when(panel == 0)
    def _():
        total[...] = before_ref[...]

    total[...] += jnp.dot(hidden_ref[0], weight_ref[0, 0], preferred_element_type=jnp.float32)

    @pl.when(panel == pl.num_programs(0) - 1)
    def _():
        out_ref[...] = total[...].astype(out_ref.dtype)


def down(hidden, dense, before, chunk, dtype):
    panels, count, depth = hidden.shape
    width = dense.shape[-1]
    return pl.pallas_call(
        down_kernel,
        out_shape=jax.ShapeDtypeStruct((count, width), dtype),
        grid=(panels,),
        in_specs=[
            pl.BlockSpec((1, count, depth), lambda g: (g, 0, 0)),
            pl.BlockSpec((1, 1, depth, width), lambda g: (chunk, g, 0, 0)),
            pl.BlockSpec((count, width), lambda g: (0, 0)),
        ],
        out_specs=pl.BlockSpec((count, width), lambda g: (0, 0)),
        scratch_shapes=[pltpu.VMEM((count, width), jnp.float32)],
        compiler_params=pltpu.CompilerParams(vmem_limit_bytes=32 * MIB),
        cost_estimate=pl.CostEstimate(
            flops=2 * panels * count * depth * width,
            bytes_accessed=2 * panels * depth * (width + count) + 6 * count * width,
            transcendentals=0,
        ),
        name=f"down_{chunk}",
    )(hidden, dense, before)


def by_tokens(
    tokens,
    norm_gain,
    gate_block_entries,
    gate_block_places,
    up_block_entries,
    up_block_places,
    down_values,
    down_slots,
):
    edge = gate_block_entries.shape[-1]
    tok_size = lax.axis_size("tok")
    col_size = lax.axis_size("col")
    rows_per = MODEL_WIDTH // edge // tok_size
    cols_per = HIDDEN_UNITS // edge // col_size
    width_blocks = MODEL_WIDTH // edge // col_size
    chunks = 4 if cols_per % 4 == 0 else 1
    chunk_cols = cols_per // chunks
    count, features = tokens.shape
    half = MODEL_WIDTH // tok_size // 2
    tok, col = lax.axis_index("tok"), lax.axis_index("col")
    side = col % 2

    def swap_tok(array, step):
        return lax.ppermute(array, "tok", [(i, i ^ step) for i in range(tok_size)])

    def swap_core(array):
        return lax.ppermute(array, "col", [(i, i ^ 1) for i in range(col_size)])

    k, r, q = jnp.meshgrid(
        jnp.arange(chunks), jnp.arange(rows_per), jnp.arange(chunk_cols), indexing="ij"
    )
    row = (r + side * (rows_per // 2)) % rows_per
    slots = (row * cols_per + k * chunk_cols + q).reshape(-1).astype(jnp.int32)
    gate_at = lookup(gate_block_places[0], slots)
    up_at = lookup(up_block_places[0], slots)
    down_at = lookup(down_slots, jnp.arange(cols_per * width_blocks, dtype=jnp.int32)).reshape(-1)

    gathered = lax.all_gather(tokens, "col")
    dense = spread_gate_up(
        gate_at, up_at, gate_block_entries, up_block_entries, chunks, rows_per, chunk_cols
    )
    down_dense = spread_down(down_at, down_values, chunks, chunk_cols, width_blocks)

    widened = gathered.astype(jnp.float32)
    mean_square = jnp.mean(widened * widened, axis=(0, 2))[:, None]
    scale = lax.rsqrt(mean_square + EPSILON)
    subs = half // features

    def normed(panel):
        at = panel * 2 + side
        piece = lax.dynamic_slice_in_dim(gathered, at * subs, subs, 0)
        piece = piece.transpose(1, 0, 2).reshape(count, half).astype(jnp.float32)
        gain = lax.dynamic_slice_in_dim(norm_gain, at * half, half, 0)
        return (piece * scale * gain).astype(jnp.bfloat16)

    own = [normed(tok ^ part) for part in range(tok_size)]
    own = [own[0]] + [swap_tok(own[part], part) for part in range(1, tok_size)]
    other = [swap_core(part) for part in own]

    hiddens, halves = [], []
    for chunk in range(chunks):
        sums = gate_up(own, other, dense, chunk)
        terms = [sums[0]] + [swap_tok(sums[part], part) for part in range(1, tok_size)]
        total = functools.reduce(jnp.add, [term.astype(jnp.float32) for term in terms])
        gate_sum, up_sum = jnp.split(total, 2, axis=1)
        hiddens.append((jax.nn.silu(gate_sum) * up_sum).astype(jnp.bfloat16))

    mixed = jnp.zeros((count, width_blocks * edge), jnp.float32)
    for chunk in range(chunks):
        hidden = lax.all_gather(hiddens[chunk], "col")
        last = chunk == chunks - 1
        mixed = down(hidden, down_dense, mixed, chunk, jnp.bfloat16 if last else jnp.float32)
    return mixed

def spread_shares_kernel(gate_at, up_at, *refs, rows, shares, cols):
    (gate_ref, up_ref), (out_ref, mark) = refs[:2], refs[-2:]
    step = pl.program_id(0)
    leave(mark)

    @pl.loop(0, rows)
    def _(row):
        for share in range(shares):
            for col in range(cols):
                at = ((step * rows + row) * shares + share) * cols + col
                put(out_ref, row, 2 * share * cols + col, gate_ref, gate_at[at])
                put(out_ref, row, (2 * share + 1) * cols + col, up_ref, up_at[at])


def spread_shares(gate_at, up_at, gate, up, rows, shares, cols, after, chunk):
    edge = gate.shape[-1]
    steps = 4
    whole = pl.BlockSpec(gate.shape, lambda k, *_: (0, 0, 0, 0), pipeline_mode=pl.Buffered(1))
    out = jax.ShapeDtypeStruct((1, rows * edge, 2 * shares * cols * edge), gate.dtype)
    block = (1, out.shape[1] // steps, out.shape[2])
    return pl.pallas_call(
        functools.partial(spread_shares_kernel, rows=rows // steps, shares=shares, cols=cols),
        out_shape=[out, MARK],
        grid_spec=pltpu.PrefetchScalarGridSpec(
            num_scalar_prefetch=2,
            grid=(steps,),
            in_specs=[whole, whole] + [ANY_SPEC] * len(after),
            out_specs=[pl.BlockSpec(block, lambda k, *_: (0, k, 0)), MARK_SPEC],
        ),
        compiler_params=pltpu.CompilerParams(vmem_limit_bytes=54 * MIB),
        cost_estimate=LITTLE,
        name=f"spread_gate_up_{chunk}",
    )(gate_at, up_at, gate, up, *after)


def spread_panels_kernel(at_ref, values_ref, *refs, chunks, rows, cols):
    out_ref, mark = refs[-2:]
    panel = pl.program_id(0)
    leave(mark)
    for chunk in range(chunks):
        for row in range(rows):
            for col in range(cols):
                at = ((panel * chunks + chunk) * rows + row) * cols + col
                put(out_ref.at[pl.ds(chunk, 1)], row, col, values_ref, at_ref[at])


def spread_panels(at, values, chunks, rows, cols, after):
    count, _, edge, _ = values.shape
    out = jax.ShapeDtypeStruct((chunks, count * rows * edge, cols * edge), values.dtype)
    return pl.pallas_call(
        functools.partial(spread_panels_kernel, chunks=chunks, rows=rows, cols=cols),
        out_shape=[out, MARK],
        grid_spec=pltpu.PrefetchScalarGridSpec(
            num_scalar_prefetch=1,
            grid=(count,),
            in_specs=[
                pl.BlockSpec((1,) + values.shape[1:], lambda m, *_: (m, 0, 0, 0))
            ]
            + [ANY_SPEC] * len(after),
            out_specs=[
                pl.BlockSpec((chunks, rows * edge, cols * edge), lambda m, *_: (0, m, 0)),
                MARK_SPEC,
            ],
        ),
        compiler_params=pltpu.CompilerParams(vmem_limit_bytes=50 * MIB),
        cost_estimate=LITTLE,
        name="spread_down",
    )(at, values, *after)

def sum_squares_kernel(tokens, out):
    widened = tokens[...].astype(jnp.float32)
    out[...] = jnp.sum(widened * widened, axis=1)[None]


def sum_squares(tokens):
    return pl.pallas_call(
        sum_squares_kernel,
        out_shape=jax.ShapeDtypeStruct((1, tokens.shape[0]), jnp.float32),
        in_specs=[pl.BlockSpec(memory_space=pltpu.VMEM)],
        out_specs=pl.BlockSpec(memory_space=pltpu.VMEM),
        compiler_params=pltpu.CompilerParams(vmem_limit_bytes=4 * MIB),
        name="sum_squares",
    )(tokens)


def pack_kernel(*refs, parts):
    count = refs[0].shape[0]
    for part in range(parts):
        refs[-1][part * count:(part + 1) * count] = refs[part][...]


def pack(pieces, after):
    parts = len(pieces)
    count, width = pieces[0].shape
    return pl.pallas_call(
        functools.partial(pack_kernel, parts=parts),
        out_shape=jax.ShapeDtypeStruct((parts * count, width), pieces[0].dtype),
        in_specs=[pl.BlockSpec(memory_space=pltpu.VMEM)] * parts + [ANY_SPEC] * len(after),
        out_specs=pl.BlockSpec(memory_space=pltpu.VMEM),
        compiler_params=pltpu.CompilerParams(vmem_limit_bytes=16 * MIB),
        cost_estimate=LITTLE,
        name="pack",
    )(*pieces, *after)


def hold_kernel(*refs):
    leave(refs[-1])


def hold(arrays, after):
    count = len(arrays)
    *arrays, _ = pl.pallas_call(
        hold_kernel,
        out_shape=[jax.ShapeDtypeStruct(array.shape, array.dtype) for array in arrays] + [MARK],
        in_specs=[ANY_SPEC] * (count + len(after)),
        out_specs=[ANY_SPEC] * count + [pl.BlockSpec(memory_space=pltpu.VMEM)],
        input_output_aliases={i: i for i in range(count)},
        cost_estimate=LITTLE,
        name="hold",
    )(*arrays, *after)
    return arrays


def stack_kernel(*refs, steps):
    pieces, out, mark = refs[:-3], refs[-2], refs[-1]
    leave(mark)
    count = out.shape[1] // 4
    for i, step in enumerate(steps):
        for part in range(4):
            there = slice((part ^ step) * count, ((part ^ step) + 1) * count)
            rows = pieces[i][there]
            if i + 1 == len(steps) < len(pieces):
                rows += pieces[i + 1][there]
            out[i, part * count:(part + 1) * count] = rows


def stack(pieces, steps, after):
    return pl.pallas_call(
        functools.partial(stack_kernel, steps=steps),
        out_shape=[jax.ShapeDtypeStruct((len(steps),) + pieces[0].shape, pieces[0].dtype), MARK],
        in_specs=[pl.BlockSpec(memory_space=pltpu.VMEM)] * len(pieces) + [ANY_SPEC],
        out_specs=[pl.BlockSpec(memory_space=pltpu.VMEM)] * 2,
        compiler_params=pltpu.CompilerParams(vmem_limit_bytes=16 * MIB),
        cost_estimate=LITTLE,
        name="stack",
    )(*pieces, after)


def halfway_kernel(kept_a, came_a, kept_b, came_b, *refs):
    out_a, out_b, mark = refs[-3:]
    leave(mark)
    for kept, came, out in ((kept_a, came_a, out_a), (kept_b, came_b, out_b)):
        out[...] = (kept[0].astype(jnp.float32) + came[0].astype(jnp.float32)).astype(out.dtype)


def halfway(kept_a, came_a, kept_b, came_b, after, chunk):
    _, count, width = kept_a.shape
    second = pl.BlockSpec((1, count, width), lambda i: (1, 0, 0))
    whole = pl.BlockSpec((count, width), lambda i: (0, 0))
    out = jax.ShapeDtypeStruct((count, width), kept_a.dtype)
    return pl.pallas_call(
        halfway_kernel,
        out_shape=[out, out, MARK],
        grid=(1,),
        in_specs=[second] * 4 + [ANY_SPEC] * len(after),
        out_specs=[whole, whole, MARK_SPEC],
        compiler_params=pltpu.CompilerParams(vmem_limit_bytes=8 * MIB),
        cost_estimate=LITTLE,
        name=f"halfway_{chunk}",
    )(kept_a, came_a, kept_b, came_b, *after)


def combine_kernel(*refs):
    terms, out, mark = refs[:6], refs[-2], refs[-1]
    leave(mark)
    count = out.shape[0] // 2
    width = out.shape[1]
    for i in range(2):
        kept, came, last = terms[3 * i:3 * i + 3]
        total = kept[0].astype(jnp.float32) + came[0].astype(jnp.float32)
        total += last[...].astype(jnp.float32)
        gate_sum, up_sum = total[:, :width], total[:, width:]
        hidden = gate_sum / (1.0 + jnp.exp(-gate_sum)) * up_sum
        out[i * count:(i + 1) * count] = hidden.astype(out.dtype)


def combine(kept_a, came_a, last_a, kept_b, came_b, last_b, after, chunk):
    count, width = last_a.shape
    first = pl.BlockSpec((1, count, width), lambda i: (0, 0, 0))
    whole = pl.BlockSpec((count, width), lambda i: (0, 0))
    return pl.pallas_call(
        combine_kernel,
        out_shape=[jax.ShapeDtypeStruct((2 * count, width // 2), last_a.dtype), MARK],
        grid=(1,),
        in_specs=[first, first, whole] * 2 + [ANY_SPEC] * len(after),
        out_specs=[pl.BlockSpec((2 * count, width // 2), lambda i: (0, 0)), MARK_SPEC],
        compiler_params=pltpu.CompilerParams(vmem_limit_bytes=10 * MIB),
        cost_estimate=LITTLE,
        name=f"combine_{chunk}",
    )(kept_a, came_a, last_a, kept_b, came_b, last_b, *after)


def panel_product_kernel(own, other, weight, *refs):
    kept_a, sent_a, kept_b, sent_b, mark = refs[-5:]
    leave(mark)
    half = own.shape[1]
    product = jnp.dot(own[...], weight[0, :half], preferred_element_type=jnp.float32)
    product += jnp.dot(other[...], weight[0, half:], preferred_element_type=jnp.float32)
    product = product.astype(kept_a.dtype)
    count = product.shape[0] // 2
    part = pl.program_id(0)
    for flip in range(2):

        @pl.when(part % 2 == flip)
        def _():
            (sent_a if flip else kept_a)[0] = product[:count]

        @pl.when(part // 2 == flip)
        def _():
            (sent_b if flip else kept_b)[0] = product[count:]


def panel_product(own, other, dense, after, chunk):
    count, half = own.shape
    _, depth, width = dense.shape
    tile = width // 4
    out = jax.ShapeDtypeStruct((2, count // 2, tile), own.dtype)
    return pl.pallas_call(
        panel_product_kernel,
        out_shape=[out] * 4 + [MARK],
        grid=(4,),
        in_specs=[pl.BlockSpec((count, half), lambda n: (0, 0))] * 2
        + [pl.BlockSpec((1, depth, tile), lambda n: (0, 0, n))]
        + [ANY_SPEC] * len(after),
        out_specs=[
            pl.BlockSpec((1,) + out.shape[1:], lambda n: (n // 2, 0, 0)),
            pl.BlockSpec((1,) + out.shape[1:], lambda n: (n // 2, 0, 0)),
            pl.BlockSpec((1,) + out.shape[1:], lambda n: (jnp.minimum(n, 1), 0, 0)),
            pl.BlockSpec((1,) + out.shape[1:], lambda n: (jnp.maximum(n - 2, 0), 0, 0)),
            MARK_SPEC,
        ],
        compiler_params=pltpu.CompilerParams(vmem_limit_bytes=54 * MIB),
        cost_estimate=LITTLE,
        name=f"gate_up_{chunk}",
    )(own, other, dense, *after)


def down_steps_kernel(place, own, other, *refs, added, outputs):
    pieces = 2 * own.shape[0]
    weights, before = refs[:pieces], refs[pieces:pieces + added]
    outs, mark = refs[-1 - outputs:-1], refs[-1]
    leave(mark)
    count = own.shape[1] // len(outs)
    for step, out in enumerate(outs):
        at = 0 if len(outs) == 1 else (place[1] ^ step) * count
        rows = pl.ds(pl.multiple_of(at, count), count)
        total = 0.0
        for term in before:
            total += term[rows]
        for i in range(pieces // 2):
            for j, side in enumerate((own, other)):
                total += jnp.dot(
                    side[i, rows], weights[2 * i + j][0, 0], preferred_element_type=jnp.float32
                )
        out[...] = total.astype(out.dtype)


def down_steps(place, own, other, steps, dense, before, chunk, last, after):
    _, count, depth = own.shape
    width = dense.shape[-1]
    dense = dense.reshape(dense.shape[0], -1, depth, width)
    tile = width // 2
    tiles = pl.BlockSpec((count, tile), lambda n, *_: (0, n))
    whole = pl.BlockSpec(own.shape, lambda n, *_: (0, 0, 0))
    weights = []
    for step in steps:
        for flip in range(2):

            def at(n, place, step=step, flip=flip):
                return chunk, 2 * (place[0] ^ step) + (place[2] ^ flip), 0, n

            weights.append(pl.BlockSpec((1, 1, depth, tile), at))
    added = [] if before is None else [before]
    out, out_tiles = [jax.ShapeDtypeStruct((count, width), jnp.float32)], [tiles]
    if last:
        out = [jax.ShapeDtypeStruct((count // 4, width), own.dtype)] * 4
        out_tiles = [pl.BlockSpec((count // 4, tile), lambda n, *_: (0, n))] * 4
    return pl.pallas_call(
        functools.partial(down_steps_kernel, added=len(added), outputs=len(out)),
        out_shape=out + [MARK],
        grid_spec=pltpu.PrefetchScalarGridSpec(
            num_scalar_prefetch=1,
            grid=(width // tile,),
            in_specs=[whole, whole] + weights + [tiles] * len(added) + [ANY_SPEC],
            out_specs=out_tiles + [MARK_SPEC],
        ),
        compiler_params=pltpu.CompilerParams(vmem_limit_bytes=42 * MIB),
        cost_estimate=LITTLE,
        name=f"down_{chunk}_{steps[0]}",
    )(place, own, other, *[dense] * len(weights), *added, after)


def by_columns(
    tokens,
    norm_gain,
    gate_block_entries,
    gate_block_places,
    up_block_entries,
    up_block_places,
    down_values,
    down_slots,
):
    edge = gate_block_entries.shape[-1]
    tok_size = lax.axis_size("tok")
    col_size = lax.axis_size("col")
    rows_per = MODEL_WIDTH // edge // tok_size
    cols_per = HIDDEN_UNITS // edge // col_size
    width_blocks = MODEL_WIDTH // edge // col_size
    share = cols_per // tok_size
    chunks = 2
    cols = share // chunks
    count, half = tokens.shape
    tok, col = lax.axis_index("tok"), lax.axis_index("col")
    chip, side = col // 2, col % 2
    parts = range(tok_size)

    def swap_tok(array, step):
        return lax.ppermute(array, "tok", [(i, i ^ step) for i in parts])

    def swap_chip(array, step):
        return lax.ppermute(array, "col", [(i, i ^ (2 * step)) for i in range(col_size)])

    def swap_core(array):
        return lax.ppermute(array, "col", [(i, i ^ 1) for i in range(col_size)])

    def to_users(array, part):
        pairs = []
        for i in parts:
            for j in range(col_size):
                user = (j // 2) * col_size + 2 * (i ^ part) + j % 2
                pairs.append((i * col_size + j, user))
        return lax.ppermute(array, ("tok", "col"), pairs)

    squares = sum_squares(tokens)
    squares += swap_core(squares)
    squares += functools.reduce(jnp.add, [swap_chip(squares, step) for step in parts[1:]])
    scale = lax.rsqrt(squares.reshape(-1, 1) / MODEL_WIDTH + EPSILON)
    gain = lax.dynamic_slice_in_dim(norm_gain, col * half, half, 0)
    normed = (tokens.astype(jnp.float32) * scale * gain).astype(jnp.bfloat16)
    pieces = [to_users(normed, part) for part in parts]

    k, r, p, q = jnp.meshgrid(
        jnp.arange(chunks), jnp.arange(rows_per), jnp.arange(tok_size), jnp.arange(cols),
        indexing="ij",
    )
    row = (r + side * (rows_per // 2)) % rows_per
    slots = (row * cols_per + (p ^ tok) * share + k * cols + q).reshape(-1).astype(jnp.int32)
    gate_at = lookup(gate_block_places[0], slots)
    up_at = lookup(up_block_places[0], slots)
    slots = tok * share * width_blocks + jnp.arange(share * width_blocks, dtype=jnp.int32)
    down_at = lookup(down_slots, slots).reshape(-1)
    gate_at, up_at = gate_at.reshape(chunks, -1), up_at.reshape(chunks, -1)

    def spread(chunk, after):
        return spread_shares(
            gate_at[chunk], up_at[chunk], gate_block_entries, up_block_entries,
            rows_per, tok_size, cols, after, chunk,
        )

    dense, mark = spread(0, [])
    own = pack(pieces, [mark])
    other = swap_core(own)

    place = jnp.stack([chip, chip ^ tok, side])

    def send(hidden):
        far = swap_chip(hidden, 2)
        near = swap_chip(hidden, 1)
        inner = lax.ppermute(hidden, "col", [(i, i ^ 6) for i in range(2, 6)])
        ends = lax.ppermute(far, "col", [(i, i ^ 2) for i in range(2, 6)])
        return [hidden, near, far], [inner, ends]

    *sums, mark = panel_product(own, other, dense, [], 0)
    dense, mark = spread(1, [mark])
    mixed = None
    for chunk in range(2):
        kept_a, sent_a, kept_b, sent_b = sums
        came_a, came_b = swap_tok(sent_a, 1), swap_tok(sent_b, 2)
        last_a, last_b, mark = halfway(kept_a, came_a, kept_b, came_b, [mark], chunk)
        last_a, last_b = swap_tok(last_a, 2), swap_tok(last_b, 1)
        if chunk:
            held, mark = stack(early, (0, 1, 2), mark)
        else:
            *sums, mark = panel_product(own, other, dense, [mark], 1)
        hidden, mark = combine(kept_a, came_a, last_a, kept_b, came_b, last_b, [mark], chunk)
        if chunk:
            mixed, mark = down_steps(
                place, held, swap_core(held), (0, 1, 2), down_dense, None, 0, False, mark
            )
            waiting = late
        else:
            kept_a, sent_a, kept_b, sent_b = sums
            sent_a, sent_b = hold([sent_a, sent_b], [mark])
            sums = kept_a, sent_a, kept_b, sent_b
            down_dense, mark = spread_panels(
                down_at, down_values, chunks, cols, width_blocks, [mark]
            )
        early, late = send(hidden)
    held, mark = stack(early, (0, 1, 2), mark)
    mixed, mark = down_steps(
        place, held, swap_core(held), (0, 1, 2), down_dense, mixed, 1, False, mark
    )
    before, mark = stack(waiting, (3,), mark)
    mixed, mark = down_steps(
        place, before, swap_core(before), (3,), down_dense, mixed, 0, False, mark
    )
    held, mark = stack(late, (3,), mark)
    *mixed, _ = down_steps(place, held, swap_core(held), (3,), down_dense, mixed, 1, True, mark)

    total = mixed[0].astype(jnp.float32)
    for step in parts[1:]:
        total += swap_tok(mixed[step], step).astype(jnp.float32)
    return total.astype(jnp.bfloat16)


def shards(*arrays):
    tok_size = lax.axis_size("tok")
    col_size = lax.axis_size("col")
    blocks = HIDDEN_UNITS // arrays[2].shape[-1]
    even = blocks % (2 * col_size * tok_size) == 0 and col_size == 2 * tok_size == 8
    return (by_columns if even else by_tokens)(*arrays)


def solution(mesh):
    return jax.shard_map(
        shards,
        mesh=mesh,
        in_specs=(
            P("tok", "col"),
            P(),
            P("tok", "col", None, None),
            P("tok", "col"),
            P("tok", "col", None, None),
            P("tok", "col"),
            P(None, "col", None, None),
            P(None, "col"),
        ),
        out_specs=P("tok", "col"),
        check_vma=False,
    )
```

```python
import functools

import jax
import jax.numpy as jnp
from jax import lax
from jax.experimental import pallas as pl
from jax.experimental.pallas import tpu as pltpu
from jax.sharding import PartitionSpec as P

MODEL_WIDTH = 8192
HIDDEN_UNITS = 24576

EPSILON = 1e-05
MIB = 1 << 20
MARK = jax.ShapeDtypeStruct((8, 128), jnp.float32)
MARK_SPEC = pl.BlockSpec(MARK.shape, lambda *_: (0, 0))
ANY_SPEC = pl.BlockSpec(memory_space=pl.ANY)
LITTLE = pl.CostEstimate(flops=1, bytes_accessed=1, transcendentals=0)


def leave(mark):
    mark[...] = jnp.zeros_like(mark)


def lookup(places, slots):
    hit = places[..., None, :] == slots[:, None]
    entry = jnp.arange(places.shape[-1], dtype=jnp.int32)
    return jnp.max(jnp.where(hit, entry, -1), axis=-1)


def put(out_ref, row, col, source_ref, entry):
    edge = source_ref.shape[-1]
    block = source_ref[0, jnp.maximum(entry, 0)]
    block = jnp.where(entry >= 0, block, jnp.zeros_like(block))
    out_ref[0, pl.ds(pl.multiple_of(row * edge, edge), edge), col * edge:(col + 1) * edge] = block


def spread_gate_up_kernel(gate_at, up_at, gate_ref, up_ref, out_ref, *, rows, cols):
    chunk = pl.program_id(0)

    @pl.loop(0, rows)
    def _(row):
        for col in range(cols):
            at = (chunk * rows + row) * cols + col
            put(out_ref, row, col, gate_ref, gate_at[at])
            put(out_ref, row, cols + col, up_ref, up_at[at])


def spread_gate_up(gate_at, up_at, gate, up, chunks, rows, cols):
    edge = gate.shape[-1]
    whole = pl.BlockSpec(gate.shape, lambda k, *_: (0, 0, 0, 0), pipeline_mode=pl.Buffered(1))
    out = jax.ShapeDtypeStruct((chunks, rows * edge, 2 * cols * edge), gate.dtype)
    return pl.pallas_call(
        functools.partial(spread_gate_up_kernel, rows=rows, cols=cols),
        out_shape=out,
        grid_spec=pltpu.PrefetchScalarGridSpec(
            num_scalar_prefetch=2,
            grid=(chunks,),
            in_specs=[whole, whole],
            out_specs=pl.BlockSpec((1,) + out.shape[1:], lambda k, *_: (k, 0, 0)),
        ),
        compiler_params=pltpu.CompilerParams(vmem_limit_bytes=48 * MIB),
        cost_estimate=pl.CostEstimate(
            flops=0, bytes_accessed=2 * (2 * gate.size + out.size), transcendentals=0
        ),
        name="spread_gate_up",
    )(gate_at, up_at, gate, up)


def spread_down_kernel(at_ref, values_ref, out_ref, *, rows, cols):
    panel, chunk = pl.program_id(0), pl.program_id(1)
    base = (panel * pl.num_programs(1) + chunk) * rows * cols

    @pl.loop(0, rows)
    def _(row):
        for col in range(cols):
            put(out_ref.at[0], row, col, values_ref, at_ref[base + row * cols + col])


def spread_down(at, values, chunks, rows, cols):
    panels, _, edge, _ = values.shape
    out = jax.ShapeDtypeStruct((chunks, panels, rows * edge, cols * edge), values.dtype)
    return pl.pallas_call(
        functools.partial(spread_down_kernel, rows=rows, cols=cols),
        out_shape=out,
        grid_spec=pltpu.PrefetchScalarGridSpec(
            num_scalar_prefetch=1,
            grid=(panels, chunks),
            in_specs=[pl.BlockSpec((1,) + values.shape[1:], lambda g, k, *_: (g, 0, 0, 0))],
            out_specs=pl.BlockSpec((1, 1) + out.shape[2:], lambda g, k, *_: (k, g, 0, 0)),
        ),
        compiler_params=pltpu.CompilerParams(vmem_limit_bytes=48 * MIB),
        cost_estimate=pl.CostEstimate(
            flops=0, bytes_accessed=2 * (values.size + out.size), transcendentals=0
        ),
        name="spread_down",
    )(at, values)


def gate_up_kernel(*refs, parts):
    own, other = refs[:parts], refs[parts:2 * parts]
    weight = refs[2 * parts]
    outs, held = refs[2 * parts + 1:3 * parts + 1], refs[-1]
    count, half = own[0].shape

    @pl.when(pl.program_id(0) == 0)
    def _():
        for part in range(parts):
            rows = slice(part * count, (part + 1) * count)
            held[rows, :half] = own[part][...]
            held[rows, half:] = other[part][...]

    product = jnp.dot(held[...], weight[0], preferred_element_type=jnp.float32)
    for part in range(parts):
        outs[part][...] = product[part * count:(part + 1) * count].astype(outs[part].dtype)


def gate_up(own, other, dense, chunk):
    parts = len(own)
    count, half = own[0].shape
    _, depth, width = dense.shape
    tile = 256
    out = jax.ShapeDtypeStruct((count, width), own[0].dtype)
    return pl.pallas_call(
        functools.partial(gate_up_kernel, parts=parts),
        out_shape=[out] * parts,
        grid=(width // tile,),
        in_specs=[pl.BlockSpec((count, half), lambda n: (0, 0))] * (2 * parts)
        + [pl.BlockSpec((1, depth, tile), lambda n: (chunk, 0, n))],
        out_specs=[pl.BlockSpec((count, tile), lambda n: (0, n))] * parts,
        scratch_shapes=[pltpu.VMEM((parts * count, 2 * half), own[0].dtype)],
        compiler_params=pltpu.CompilerParams(vmem_limit_bytes=32 * MIB),
        cost_estimate=pl.CostEstimate(
            flops=2 * parts * count * depth * width,
            bytes_accessed=2 * (depth * width + parts * count * (depth + width)),
            transcendentals=0,
        ),
        name=f"gate_up_{chunk}",
    )(*own, *other, dense)


def down_kernel(hidden_ref, weight_ref, before_ref, out_ref, total):
    panel = pl.program_id(0)

    @pl.when(panel == 0)
    def _():
        total[...] = before_ref[...]

    total[...] += jnp.dot(hidden_ref[0], weight_ref[0, 0], preferred_element_type=jnp.float32)

    @pl.when(panel == pl.num_programs(0) - 1)
    def _():
        out_ref[...] = total[...].astype(out_ref.dtype)


def down(hidden, dense, before, chunk, dtype):
    panels, count, depth = hidden.shape
    width = dense.shape[-1]
    return pl.pallas_call(
        down_kernel,
        out_shape=jax.ShapeDtypeStruct((count, width), dtype),
        grid=(panels,),
        in_specs=[
            pl.BlockSpec((1, count, depth), lambda g: (g, 0, 0)),
            pl.BlockSpec((1, 1, depth, width), lambda g: (chunk, g, 0, 0)),
            pl.BlockSpec((count, width), lambda g: (0, 0)),
        ],
        out_specs=pl.BlockSpec((count, width), lambda g: (0, 0)),
        scratch_shapes=[pltpu.VMEM((count, width), jnp.float32)],
        compiler_params=pltpu.CompilerParams(vmem_limit_bytes=32 * MIB),
        cost_estimate=pl.CostEstimate(
            flops=2 * panels * count * depth * width,
            bytes_accessed=2 * panels * depth * (width + count) + 6 * count * width,
            transcendentals=0,
        ),
        name=f"down_{chunk}",
    )(hidden, dense, before)


def by_tokens(
    tokens,
    norm_gain,
    gate_block_entries,
    gate_block_places,
    up_block_entries,
    up_block_places,
    down_values,
    down_slots,
):
    edge = gate_block_entries.shape[-1]
    tok_size = lax.axis_size("tok")
    col_size = lax.axis_size("col")
    rows_per = MODEL_WIDTH // edge // tok_size
    cols_per = HIDDEN_UNITS // edge // col_size
    width_blocks = MODEL_WIDTH // edge // col_size
    chunks = 4 if cols_per % 4 == 0 else 1
    chunk_cols = cols_per // chunks
    count, features = tokens.shape
    half = MODEL_WIDTH // tok_size // 2
    tok, col = lax.axis_index("tok"), lax.axis_index("col")
    side = col % 2

    def swap_tok(array, step):
        return lax.ppermute(array, "tok", [(i, i ^ step) for i in range(tok_size)])

    def swap_core(array):
        return lax.ppermute(array, "col", [(i, i ^ 1) for i in range(col_size)])

    k, r, q = jnp.meshgrid(
        jnp.arange(chunks), jnp.arange(rows_per), jnp.arange(chunk_cols), indexing="ij"
    )
    row = (r + side * (rows_per // 2)) % rows_per
    slots = (row * cols_per + k * chunk_cols + q).reshape(-1).astype(jnp.int32)
    gate_at = lookup(gate_block_places[0], slots)
    up_at = lookup(up_block_places[0], slots)
    down_at = lookup(down_slots, jnp.arange(cols_per * width_blocks, dtype=jnp.int32)).reshape(-1)

    gathered = lax.all_gather(tokens, "col")
    dense = spread_gate_up(
        gate_at, up_at, gate_block_entries, up_block_entries, chunks, rows_per, chunk_cols
    )
    down_dense = spread_down(down_at, down_values, chunks, chunk_cols, width_blocks)

    widened = gathered.astype(jnp.float32)
    mean_square = jnp.mean(widened * widened, axis=(0, 2))[:, None]
    scale = lax.rsqrt(mean_square + EPSILON)
    subs = half // features

    def normed(panel):
        at = panel * 2 + side
        piece = lax.dynamic_slice_in_dim(gathered, at * subs, subs, 0)
        piece = piece.transpose(1, 0, 2).reshape(count, half).astype(jnp.float32)
        gain = lax.dynamic_slice_in_dim(norm_gain, at * half, half, 0)
        return (piece * scale * gain).astype(jnp.bfloat16)

    own = [normed(tok ^ part) for part in range(tok_size)]
    own = [own[0]] + [swap_tok(own[part], part) for part in range(1, tok_size)]
    other = [swap_core(part) for part in own]

    hiddens, halves = [], []
    for chunk in range(chunks):
        sums = gate_up(own, other, dense, chunk)
        terms = [sums[0]] + [swap_tok(sums[part], part) for part in range(1, tok_size)]
        total = functools.reduce(jnp.add, [term.astype(jnp.float32) for term in terms])
        gate_sum, up_sum = jnp.split(total, 2, axis=1)
        hiddens.append((jax.nn.silu(gate_sum) * up_sum).astype(jnp.bfloat16))

    mixed = jnp.zeros((count, width_blocks * edge), jnp.float32)
    for chunk in range(chunks):
        hidden = lax.all_gather(hiddens[chunk], "col")
        last = chunk == chunks - 1
        mixed = down(hidden, down_dense, mixed, chunk, jnp.bfloat16 if last else jnp.float32)
    return mixed

def spread_shares_kernel(gate_at, up_at, *refs, rows, shares, cols):
    (gate_ref, up_ref), (out_ref, mark) = refs[:2], refs[-2:]
    step = pl.program_id(0)
    leave(mark)

    @pl.loop(0, rows)
    def _(row):
        for share in range(shares):
            for col in range(cols):
                at = ((step * rows + row) * shares + share) * cols + col
                put(out_ref, row, 2 * share * cols + col, gate_ref, gate_at[at])
                put(out_ref, row, (2 * share + 1) * cols + col, up_ref, up_at[at])


def spread_shares(gate_at, up_at, gate, up, rows, shares, cols, after, chunk):
    edge = gate.shape[-1]
    steps = 4
    whole = pl.BlockSpec(gate.shape, lambda k, *_: (0, 0, 0, 0), pipeline_mode=pl.Buffered(1))
    out = jax.ShapeDtypeStruct((1, rows * edge, 2 * shares * cols * edge), gate.dtype)
    block = (1, out.shape[1] // steps, out.shape[2])
    return pl.pallas_call(
        functools.partial(spread_shares_kernel, rows=rows // steps, shares=shares, cols=cols),
        out_shape=[out, MARK],
        grid_spec=pltpu.PrefetchScalarGridSpec(
            num_scalar_prefetch=2,
            grid=(steps,),
            in_specs=[whole, whole] + [ANY_SPEC] * len(after),
            out_specs=[pl.BlockSpec(block, lambda k, *_: (0, k, 0)), MARK_SPEC],
        ),
        compiler_params=pltpu.CompilerParams(vmem_limit_bytes=53 * MIB),
        cost_estimate=LITTLE,
        name=f"spread_gate_up_{chunk}",
    )(gate_at, up_at, gate, up, *after)


def spread_panels_kernel(at_ref, values_ref, *refs, chunks, rows, cols):
    out_ref, mark = refs[-2:]
    panel = pl.program_id(0)
    leave(mark)
    for chunk in range(chunks):
        for row in range(rows):
            for col in range(cols):
                at = ((panel * chunks + chunk) * rows + row) * cols + col
                put(out_ref.at[pl.ds(chunk, 1)], row, col, values_ref, at_ref[at])


def spread_panels(at, values, chunks, rows, cols, after):
    count, _, edge, _ = values.shape
    out = jax.ShapeDtypeStruct((chunks, count * rows * edge, cols * edge), values.dtype)
    return pl.pallas_call(
        functools.partial(spread_panels_kernel, chunks=chunks, rows=rows, cols=cols),
        out_shape=[out, MARK],
        grid_spec=pltpu.PrefetchScalarGridSpec(
            num_scalar_prefetch=1,
            grid=(count,),
            in_specs=[
                pl.BlockSpec((1,) + values.shape[1:], lambda m, *_: (m, 0, 0, 0))
            ]
            + [ANY_SPEC] * len(after),
            out_specs=[
                pl.BlockSpec((chunks, rows * edge, cols * edge), lambda m, *_: (0, m, 0)),
                MARK_SPEC,
            ],
        ),
        compiler_params=pltpu.CompilerParams(vmem_limit_bytes=50 * MIB),
        cost_estimate=LITTLE,
        name="spread_down",
    )(at, values, *after)

def sum_squares_kernel(tokens, out):
    widened = tokens[...].astype(jnp.float32)
    out[...] = jnp.sum(widened * widened, axis=1)[None]


def sum_squares(tokens):
    return pl.pallas_call(
        sum_squares_kernel,
        out_shape=jax.ShapeDtypeStruct((1, tokens.shape[0]), jnp.float32),
        in_specs=[pl.BlockSpec(memory_space=pltpu.VMEM)],
        out_specs=pl.BlockSpec(memory_space=pltpu.VMEM),
        compiler_params=pltpu.CompilerParams(vmem_limit_bytes=4 * MIB),
        name="sum_squares",
    )(tokens)


def pack_kernel(*refs, parts):
    count = refs[0].shape[0]
    for part in range(parts):
        refs[-1][part * count:(part + 1) * count] = refs[part][...]


def pack(pieces, after):
    parts = len(pieces)
    count, width = pieces[0].shape
    return pl.pallas_call(
        functools.partial(pack_kernel, parts=parts),
        out_shape=jax.ShapeDtypeStruct((parts * count, width), pieces[0].dtype),
        in_specs=[pl.BlockSpec(memory_space=pltpu.VMEM)] * parts + [ANY_SPEC] * len(after),
        out_specs=pl.BlockSpec(memory_space=pltpu.VMEM),
        compiler_params=pltpu.CompilerParams(vmem_limit_bytes=16 * MIB),
        cost_estimate=LITTLE,
        name="pack",
    )(*pieces, *after)


def hold_kernel(*refs):
    leave(refs[-1])


def hold(arrays, after):
    count = len(arrays)
    *arrays, _ = pl.pallas_call(
        hold_kernel,
        out_shape=[jax.ShapeDtypeStruct(array.shape, array.dtype) for array in arrays] + [MARK],
        in_specs=[ANY_SPEC] * (count + len(after)),
        out_specs=[ANY_SPEC] * count + [pl.BlockSpec(memory_space=pltpu.VMEM)],
        input_output_aliases={i: i for i in range(count)},
        cost_estimate=LITTLE,
        name="hold",
    )(*arrays, *after)
    return arrays


def stack_kernel(*refs, steps):
    pieces, out, mark = refs[:-3], refs[-2], refs[-1]
    leave(mark)
    count = out.shape[1] // 4
    for i, step in enumerate(steps):
        for part in range(4):
            there = slice((part ^ step) * count, ((part ^ step) + 1) * count)
            rows = pieces[i][there]
            if i + 1 == len(steps) < len(pieces):
                rows += pieces[i + 1][there]
            out[i, part * count:(part + 1) * count] = rows


def stack(pieces, steps, after):
    return pl.pallas_call(
        functools.partial(stack_kernel, steps=steps),
        out_shape=[jax.ShapeDtypeStruct((len(steps),) + pieces[0].shape, pieces[0].dtype), MARK],
        in_specs=[pl.BlockSpec(memory_space=pltpu.VMEM)] * len(pieces) + [ANY_SPEC],
        out_specs=[pl.BlockSpec(memory_space=pltpu.VMEM)] * 2,
        compiler_params=pltpu.CompilerParams(vmem_limit_bytes=16 * MIB),
        cost_estimate=LITTLE,
        name="stack",
    )(*pieces, after)


def halfway_kernel(kept_a, came_a, kept_b, came_b, *refs):
    out_a, out_b, mark = refs[-3:]
    leave(mark)
    for kept, came, out in ((kept_a, came_a, out_a), (kept_b, came_b, out_b)):
        out[...] = (kept[0].astype(jnp.float32) + came[0].astype(jnp.float32)).astype(out.dtype)


def halfway(kept_a, came_a, kept_b, came_b, after, chunk):
    _, count, width = kept_a.shape
    second = pl.BlockSpec((1, count, width), lambda i: (1, 0, 0))
    whole = pl.BlockSpec((count, width), lambda i: (0, 0))
    out = jax.ShapeDtypeStruct((count, width), kept_a.dtype)
    return pl.pallas_call(
        halfway_kernel,
        out_shape=[out, out, MARK],
        grid=(1,),
        in_specs=[second] * 4 + [ANY_SPEC] * len(after),
        out_specs=[whole, whole, MARK_SPEC],
        compiler_params=pltpu.CompilerParams(vmem_limit_bytes=8 * MIB),
        cost_estimate=LITTLE,
        name=f"halfway_{chunk}",
    )(kept_a, came_a, kept_b, came_b, *after)


def combine_kernel(*refs):
    terms, out, mark = refs[:6], refs[-2], refs[-1]
    leave(mark)
    count = out.shape[0] // 2
    width = out.shape[1]
    for i in range(2):
        kept, came, last = terms[3 * i:3 * i + 3]
        total = kept[0].astype(jnp.float32) + came[0].astype(jnp.float32)
        total += last[...].astype(jnp.float32)
        gate_sum, up_sum = total[:, :width], total[:, width:]
        hidden = gate_sum / (1.0 + jnp.exp(-gate_sum)) * up_sum
        out[i * count:(i + 1) * count] = hidden.astype(out.dtype)


def combine(kept_a, came_a, last_a, kept_b, came_b, last_b, after, chunk):
    count, width = last_a.shape
    first = pl.BlockSpec((1, count, width), lambda i: (0, 0, 0))
    whole = pl.BlockSpec((count, width), lambda i: (0, 0))
    return pl.pallas_call(
        combine_kernel,
        out_shape=[jax.ShapeDtypeStruct((2 * count, width // 2), last_a.dtype), MARK],
        grid=(1,),
        in_specs=[first, first, whole] * 2 + [ANY_SPEC] * len(after),
        out_specs=[pl.BlockSpec((2 * count, width // 2), lambda i: (0, 0)), MARK_SPEC],
        compiler_params=pltpu.CompilerParams(vmem_limit_bytes=10 * MIB),
        cost_estimate=LITTLE,
        name=f"combine_{chunk}",
    )(kept_a, came_a, last_a, kept_b, came_b, last_b, *after)


def panel_product_kernel(own, other, weight, *refs):
    kept_a, sent_a, kept_b, sent_b, mark = refs[-5:]
    leave(mark)
    half = own.shape[1]
    product = jnp.dot(own[...], weight[0, :half], preferred_element_type=jnp.float32)
    product += jnp.dot(other[...], weight[0, half:], preferred_element_type=jnp.float32)
    product = product.astype(kept_a.dtype)
    count = product.shape[0] // 2
    part = pl.program_id(0)
    for flip in range(2):

        @pl.when(part % 2 == flip)
        def _():
            (sent_a if flip else kept_a)[0] = product[:count]

        @pl.when(part // 2 == flip)
        def _():
            (sent_b if flip else kept_b)[0] = product[count:]


def panel_product(own, other, dense, after, chunk):
    count, half = own.shape
    _, depth, width = dense.shape
    tile = width // 4
    out = jax.ShapeDtypeStruct((2, count // 2, tile), own.dtype)
    return pl.pallas_call(
        panel_product_kernel,
        out_shape=[out] * 4 + [MARK],
        grid=(4,),
        in_specs=[pl.BlockSpec((count, half), lambda n: (0, 0))] * 2
        + [pl.BlockSpec((1, depth, tile), lambda n: (0, 0, n))]
        + [ANY_SPEC] * len(after),
        out_specs=[
            pl.BlockSpec((1,) + out.shape[1:], lambda n: (n // 2, 0, 0)),
            pl.BlockSpec((1,) + out.shape[1:], lambda n: (n // 2, 0, 0)),
            pl.BlockSpec((1,) + out.shape[1:], lambda n: (jnp.minimum(n, 1), 0, 0)),
            pl.BlockSpec((1,) + out.shape[1:], lambda n: (jnp.maximum(n - 2, 0), 0, 0)),
            MARK_SPEC,
        ],
        compiler_params=pltpu.CompilerParams(vmem_limit_bytes=53 * MIB),
        cost_estimate=LITTLE,
        name=f"gate_up_{chunk}",
    )(own, other, dense, *after)


def down_steps_kernel(place, own, other, *refs, added, outputs):
    pieces = 2 * own.shape[0]
    weights, before = refs[:pieces], refs[pieces:pieces + added]
    outs, mark = refs[-1 - outputs:-1], refs[-1]
    leave(mark)
    count = own.shape[1] // len(outs)
    for step, out in enumerate(outs):
        at = 0 if len(outs) == 1 else (place[1] ^ step) * count
        rows = pl.ds(pl.multiple_of(at, count), count)
        total = 0.0
        for term in before:
            total += term[rows]
        for i in range(pieces // 2):
            for j, side in enumerate((own, other)):
                total += jnp.dot(
                    side[i, rows], weights[2 * i + j][0, 0], preferred_element_type=jnp.float32
                )
        out[...] = total.astype(out.dtype)


def down_steps(place, own, other, steps, dense, before, chunk, last, after):
    _, count, depth = own.shape
    width = dense.shape[-1]
    dense = dense.reshape(dense.shape[0], -1, depth, width)
    tile = width // 2
    tiles = pl.BlockSpec((count, tile), lambda n, *_: (0, n))
    whole = pl.BlockSpec(own.shape, lambda n, *_: (0, 0, 0))
    weights = []
    for step in steps:
        for flip in range(2):

            def at(n, place, step=step, flip=flip):
                return chunk, 2 * (place[0] ^ step) + (place[2] ^ flip), 0, n

            weights.append(pl.BlockSpec((1, 1, depth, tile), at))
    added = [] if before is None else [before]
    out, out_tiles = [jax.ShapeDtypeStruct((count, width), jnp.float32)], [tiles]
    if last:
        out = [jax.ShapeDtypeStruct((count // 4, width), own.dtype)] * 4
        out_tiles = [pl.BlockSpec((count // 4, tile), lambda n, *_: (0, n))] * 4
    return pl.pallas_call(
        functools.partial(down_steps_kernel, added=len(added), outputs=len(out)),
        out_shape=out + [MARK],
        grid_spec=pltpu.PrefetchScalarGridSpec(
            num_scalar_prefetch=1,
            grid=(width // tile,),
            in_specs=[whole, whole] + weights + [tiles] * len(added) + [ANY_SPEC],
            out_specs=out_tiles + [MARK_SPEC],
        ),
        compiler_params=pltpu.CompilerParams(vmem_limit_bytes=42 * MIB),
        cost_estimate=LITTLE,
        name=f"down_{chunk}_{steps[0]}",
    )(place, own, other, *[dense] * len(weights), *added, after)


def by_columns(
    tokens,
    norm_gain,
    gate_block_entries,
    gate_block_places,
    up_block_entries,
    up_block_places,
    down_values,
    down_slots,
):
    edge = gate_block_entries.shape[-1]
    tok_size = lax.axis_size("tok")
    col_size = lax.axis_size("col")
    rows_per = MODEL_WIDTH // edge // tok_size
    cols_per = HIDDEN_UNITS // edge // col_size
    width_blocks = MODEL_WIDTH // edge // col_size
    share = cols_per // tok_size
    chunks = 2
    cols = share // chunks
    count, half = tokens.shape
    tok, col = lax.axis_index("tok"), lax.axis_index("col")
    chip, side = col // 2, col % 2
    parts = range(tok_size)

    def swap_tok(array, step):
        return lax.ppermute(array, "tok", [(i, i ^ step) for i in parts])

    def swap_chip(array, step):
        return lax.ppermute(array, "col", [(i, i ^ (2 * step)) for i in range(col_size)])

    def swap_core(array):
        return lax.ppermute(array, "col", [(i, i ^ 1) for i in range(col_size)])

    def to_users(array, part):
        pairs = []
        for i in parts:
            for j in range(col_size):
                user = (j // 2) * col_size + 2 * (i ^ part) + j % 2
                pairs.append((i * col_size + j, user))
        return lax.ppermute(array, ("tok", "col"), pairs)

    squares = sum_squares(tokens)
    squares += swap_core(squares)
    squares += functools.reduce(jnp.add, [swap_chip(squares, step) for step in parts[1:]])
    scale = lax.rsqrt(squares.reshape(-1, 1) / MODEL_WIDTH + EPSILON)
    gain = lax.dynamic_slice_in_dim(norm_gain, col * half, half, 0)
    normed = (tokens.astype(jnp.float32) * scale * gain).astype(jnp.bfloat16)
    pieces = [to_users(normed, part) for part in parts]

    k, r, p, q = jnp.meshgrid(
        jnp.arange(chunks), jnp.arange(rows_per), jnp.arange(tok_size), jnp.arange(cols),
        indexing="ij",
    )
    row = (r + side * (rows_per // 2)) % rows_per
    slots = (row * cols_per + (p ^ tok) * share + k * cols + q).reshape(-1).astype(jnp.int32)
    gate_at = lookup(gate_block_places[0], slots)
    up_at = lookup(up_block_places[0], slots)
    slots = tok * share * width_blocks + jnp.arange(share * width_blocks, dtype=jnp.int32)
    down_at = lookup(down_slots, slots).reshape(-1)
    gate_at, up_at = gate_at.reshape(chunks, -1), up_at.reshape(chunks, -1)

    def spread(chunk, after):
        return spread_shares(
            gate_at[chunk], up_at[chunk], gate_block_entries, up_block_entries,
            rows_per, tok_size, cols, after, chunk,
        )

    dense, mark = spread(0, [])
    own = pack(pieces, [mark])
    other = swap_core(own)

    place = jnp.stack([chip, chip ^ tok, side])

    def send(hidden):
        far = swap_chip(hidden, 2)
        near = swap_chip(hidden, 1)
        inner = lax.ppermute(hidden, "col", [(i, i ^ 6) for i in range(2, 6)])
        ends = lax.ppermute(far, "col", [(i, i ^ 2) for i in range(2, 6)])
        return [hidden, near, far], [inner, ends]

    *sums, mark = panel_product(own, other, dense, [], 0)
    dense, mark = spread(1, [mark])
    mixed = None
    for chunk in range(2):
        kept_a, sent_a, kept_b, sent_b = sums
        came_a, came_b = swap_tok(sent_a, 1), swap_tok(sent_b, 2)
        last_a, last_b, mark = halfway(kept_a, came_a, kept_b, came_b, [mark], chunk)
        last_a, last_b = swap_tok(last_a, 2), swap_tok(last_b, 1)
        if chunk:
            held, mark = stack(early, (0, 1, 2), mark)
        else:
            *sums, mark = panel_product(own, other, dense, [mark], 1)
        hidden, mark = combine(kept_a, came_a, last_a, kept_b, came_b, last_b, [mark], chunk)
        if chunk:
            mixed, mark = down_steps(
                place, held, swap_core(held), (0, 1, 2), down_dense, None, 0, False, mark
            )
            held, mark = stack(late, (3,), mark)
            mixed, mark = down_steps(
                place, held, swap_core(held), (3,), down_dense, mixed, 0, False, mark
            )
        else:
            kept_a, sent_a, kept_b, sent_b = sums
            sent_a, sent_b = hold([sent_a, sent_b], [mark])
            sums = kept_a, sent_a, kept_b, sent_b
            down_dense, mark = spread_panels(
                down_at, down_values, chunks, cols, width_blocks, [mark]
            )
        early, late = send(hidden)
    held, mark = stack(early, (0, 1, 2), mark)
    mixed, mark = down_steps(
        place, held, swap_core(held), (0, 1, 2), down_dense, mixed, 1, False, mark
    )
    held, mark = stack(late, (3,), mark)
    *mixed, _ = down_steps(place, held, swap_core(held), (3,), down_dense, mixed, 1, True, mark)

    total = mixed[0].astype(jnp.float32)
    for step in parts[1:]:
        total += swap_tok(mixed[step], step).astype(jnp.float32)
    return total.astype(jnp.bfloat16)


def shards(*arrays):
    tok_size = lax.axis_size("tok")
    col_size = lax.axis_size("col")
    blocks = HIDDEN_UNITS // arrays[2].shape[-1]
    even = blocks % (2 * col_size * tok_size) == 0 and col_size == 2 * tok_size == 8
    return (by_columns if even else by_tokens)(*arrays)


def solution(mesh):
    return jax.shard_map(
        shards,
        mesh=mesh,
        in_specs=(
            P("tok", "col"),
            P(),
            P("tok", "col", None, None),
            P("tok", "col"),
            P("tok", "col", None, None),
            P("tok", "col"),
            P(None, "col", None, None),
            P(None, "col"),
        ),
        out_specs=P("tok", "col"),
        check_vma=False,
    )
```
